32 devices in a mesh: row: 8 (over y, x, core), col: 4 (over z).
Axes of the slice: x: 2, y: 2, z: 4, core: 2. Of those that a mesh axis runs over, the one named last changes fastest.
Arguments:
- features: bfloat16 [8192, 128], P(('row', 'col')), may hold values from -6 to 6
- degree: int32 [8192], P(('row', 'col')), may hold values from 1 to 256
- weight: bfloat16 [128, 128], replicated, may hold values from -0.5 to 0.5
- bias: float32 [128], replicated, may hold values from -3 to 3
- cotangent: bfloat16 [8192, 128], P(('row', 'col')), may hold values from -8 to 8
- tile_rows: int32 [8, 4, 128], P('row', 'col'), may hold values from 0 to 7
- tile_cols: int32 [8, 4, 128], P('row', 'col'), may hold values from 0 to 15
- tile_count: int32 [8, 4, 1], P('row', 'col'), may hold values from 32 to 128, as said below
- tile_codes: int32 [8, 4, 128, 256], P('row', 'col'), may hold values from 0 to 4095
Outputs:
- hidden: bfloat16 [8192, 128], P(('row', 'col'))
- grad_features: bfloat16 [8192, 128], P(('row', 'col'))
- grad_weight: float32 [128, 128], replicated
- grad_bias: float32 [128], replicated
The draws below stay inside these ranges and needn't reach their ends.
Inputs may be any that keep to these rules, and one draw needn't show every extreme that they name: Only the first tile_count slots of a block are live; on some block the count is exactly 128. `tile_rows`: A tile position may repeat within a block; repeated tiles add.
All inputs are finite; a program needn't handle non-finite values.
Results may differ from the reference program's by a relative error of at most 0.019.
Values may be sent and summed in bfloat16 or wider, within the bound.
No kernel may reach another device: no remote copies, remote signals or barrier semaphores. Data moves between devices by JAX's collectives and lax.ppermute only.
A program may use at most 64 MiB of HBM per device.

```python
import math
import jax
import jax.numpy as jnp
from jax import lax

FEAT = 128
TILE = 128
NODE_TILES = 2
SLOTS = 128
BLOCK = 16
ROW_TILES = 8
COL_TILES = 16
NODES = 8192
N_ROW = 8
N_COL = 4


def draw_cotangent(key, part):
    piece_rows = TILE * NODE_TILES
    piece_total = NODES // piece_rows
    piece_ids = jnp.arange(NODES, dtype=jnp.int32) // piece_rows
    ramp = 0.5 + piece_ids.astype(jnp.float32) / (piece_total - 1)
    noise = jnp.clip(jax.random.normal(jax.random.fold_in(key, 13), (NODES, FEAT), jnp.float32), -4.0, 4.0)
    values = noise * ramp[:, None]
    return values.astype(jnp.bfloat16)


def draw_tile_count(key, part):
    rows_axis = COL_TILES // NODE_TILES
    cols_axis = ROW_TILES // NODE_TILES
    device_total = rows_axis * cols_axis
    counts = jax.random.randint(jax.random.fold_in(key, 21), (device_total,), SLOTS // 4, SLOTS + 1, jnp.int32)
    fullest = jax.random.randint(jax.random.fold_in(key, 22), (), 0, device_total, jnp.int32)
    counts = counts.at[fullest].set(SLOTS)
    return counts.reshape(rows_axis, cols_axis, 1)


def touch_ends(drawn, rng, low, largest):
    extent = drawn.shape
    place = [jax.random.randint(jax.random.fold_in(rng, axis), (), 0, extent[axis]) for axis in range(len(extent))]
    drawn = drawn.at[tuple(place)].set(low)
    longest = extent.index(max(extent))
    place[longest] = (place[longest] + 1) % extent[longest]
    return drawn.at[tuple(place)].set(largest)


def shard_levels(stream_key, dims, cuts, low, top_value):
    def one(dim, shards_of):
        draws = jax.random.uniform(jax.random.fold_in(jax.random.fold_in(stream_key, 6), dim), (shards_of,), jnp.float32, low / len(cuts), top_value / len(cuts))
        return jnp.repeat(jnp.exp(draws), dims[dim] // shards_of).reshape((-1,) + (1,) * (len(dims) - dim - 1))

    factor_of = one(*cuts[0])
    for cut in cuts[1:]:
        factor_of = factor_of * one(*cut)
    return factor_of


def bell_draw(own_key, shape, scale, most, cuts=(), held_as=jnp.bfloat16):
    entries = jax.random.normal(own_key, shape, jnp.float32) * scale
    if len(cuts) > 0:
        entries = shard_levels(own_key, shape, cuts, -0.22, 0.18) * entries
    return jnp.clip(entries, min=-most, max=most).astype(held_as)


def setup_inputs(seed: int = 0) -> dict:
    keys = jax.random.split(jax.random.key(seed), 10)
    return {
        "features": bell_draw(keys[0], (NODES, FEAT), 1.0, 6.0, ((0, 32),)),
        "degree": touch_ends(jax.random.randint(keys[1], (NODES,), 1, 257), jax.random.fold_in(keys[1], 1), 1, 256).astype(jnp.int32),
        "weight": bell_draw(keys[2], (FEAT, FEAT), FEAT ** -0.5, 0.5),
        "bias": bell_draw(keys[3], (FEAT,), 0.5, 3.0, (), jnp.float32),
        "cotangent": draw_cotangent(jax.random.fold_in(keys[9], 71), 0),
        "tile_rows": touch_ends(jax.random.randint(keys[5], (N_ROW, N_COL, SLOTS), 0, ROW_TILES), jax.random.fold_in(keys[5], 1), 0, ROW_TILES - 1).astype(jnp.int32),
        "tile_cols": touch_ends(jax.random.randint(keys[6], (N_ROW, N_COL, SLOTS), 0, COL_TILES), jax.random.fold_in(keys[6], 1), 0, COL_TILES - 1).astype(jnp.int32),
        "tile_count": draw_tile_count(jax.random.fold_in(keys[9], 71), 0),
        "tile_codes": touch_ends(jax.random.randint(keys[8], (N_ROW, N_COL, SLOTS, 2 * TILE), 0, 4096), jax.random.fold_in(keys[8], 1), 0, 4095).astype(jnp.int32),
    }


def tile_mask(code_block, living):
    row_code = code_block[:, :TILE][:, :, None]
    col_code = code_block[:, TILE:][:, None, :]
    hashed = (row_code * col_code + row_code + 3 * col_code) % 4093
    return (hashed < 64) & living[:, None, None]

def device_sum(codes_dev, rows_dev, cols_dev, count_dev, source, out_tiles, backward):

    def block_step(summed, block_id):
        slot_start = block_id * BLOCK
        code_block = lax.dynamic_slice_in_dim(codes_dev, slot_start, BLOCK, 0)
        row_block = lax.dynamic_slice_in_dim(rows_dev, slot_start, BLOCK, 0)
        col_block = lax.dynamic_slice_in_dim(cols_dev, slot_start, BLOCK, 0)
        slot_ids = slot_start + jnp.arange(BLOCK, dtype=jnp.int32)
        living = slot_ids < count_dev
        keep = tile_mask(code_block, living).astype(jnp.float32)
        if backward:
            picked = source[row_block].astype(jnp.float32)
            product = jnp.einsum('tij,tif->tjf', keep, picked)
            return (summed.at[col_block].add(product), None)
        picked = source[col_block].astype(jnp.float32)
        product = jnp.einsum('tij,tjf->tif', keep, picked)
        return (summed.at[row_block].add(product), None)
    start_sum = jnp.zeros((out_tiles, TILE, FEAT), jnp.float32)
    summed, unused = lax.scan(block_step, start_sum, jnp.arange(SLOTS // BLOCK, dtype=jnp.int32))
    return summed

def reference(features, degree, weight, bias, cotangent, tile_rows, tile_cols, tile_count, tile_codes):
    pieces = TILE * NODE_TILES
    inv_root = lax.rsqrt(degree.astype(jnp.float32)).reshape(N_ROW, N_COL, pieces, 1)
    scaled = (inv_root * features.reshape(N_ROW, N_COL, pieces, FEAT).astype(jnp.float32)).astype(jnp.bfloat16)

    def forward_row(row_id):

        def add_col(col_id, summed):
            source = lax.dynamic_index_in_dim(scaled, col_id, 1, keepdims=False).reshape(COL_TILES, TILE, FEAT)
            partial_sum = device_sum(tile_codes[row_id, col_id], tile_rows[row_id, col_id], tile_cols[row_id, col_id], tile_count[row_id, col_id, 0], source, ROW_TILES, False)
            rounded = lax.optimization_barrier(partial_sum.astype(jnp.bfloat16))
            return summed + rounded.astype(jnp.float32)
        summed = lax.fori_loop(0, N_COL, add_col, jnp.zeros((ROW_TILES, TILE, FEAT), jnp.float32))
        row_root = lax.dynamic_index_in_dim(inv_root, row_id, 0, keepdims=False)
        return (row_root * summed.reshape(N_COL, pieces, FEAT)).astype(jnp.bfloat16)
    aggregate = lax.map(forward_row, jnp.arange(N_ROW, dtype=jnp.int32)).reshape(NODES, FEAT)
    preact = jnp.dot(aggregate, weight, preferred_element_type=jnp.float32) + bias
    hidden = jax.nn.elu(preact).astype(jnp.bfloat16)
    elu_slope = jnp.where(preact > 0, 1.0, jnp.exp(jnp.minimum(preact, 0.0)))
    grad_pre = cotangent.astype(jnp.float32) * elu_slope
    grad_pre_b = grad_pre.astype(jnp.bfloat16)
    grad_scale = 1.0 / math.sqrt(NODES)
    grad_weight = jnp.dot(aggregate.T, grad_pre_b, preferred_element_type=jnp.float32) * grad_scale
    grad_bias = lax.optimization_barrier(jnp.sum(grad_pre, axis=0)) * grad_scale
    grad_agg = jnp.dot(grad_pre_b, weight.T, preferred_element_type=jnp.float32)
    grad_scaled = (inv_root.reshape(NODES, 1) * grad_agg).astype(jnp.bfloat16).reshape(N_ROW, N_COL, pieces, FEAT)

    def backward_col(col_id):

        def add_row(row_id, summed):
            source = lax.dynamic_index_in_dim(grad_scaled, row_id, 0, keepdims=False).reshape(ROW_TILES, TILE, FEAT)
            partial_sum = device_sum(tile_codes[row_id, col_id], tile_rows[row_id, col_id], tile_cols[row_id, col_id], tile_count[row_id, col_id, 0], source, COL_TILES, True)
            rounded = lax.optimization_barrier(partial_sum.astype(jnp.bfloat16))
            return summed + rounded.astype(jnp.float32)
        summed = lax.fori_loop(0, N_ROW, add_row, jnp.zeros((COL_TILES, TILE, FEAT), jnp.float32))
        col_root = lax.dynamic_index_in_dim(inv_root, col_id, 1, keepdims=False)
        return (col_root * summed.reshape(N_ROW, pieces, FEAT)).astype(jnp.bfloat16)
    by_column = lax.map(backward_col, jnp.arange(N_COL, dtype=jnp.int32))
    grad_features = jnp.transpose(by_column, (1, 0, 2, 3)).reshape(NODES, FEAT)
    return (hidden, grad_features, grad_weight, grad_bias)
```

```python
import functools
import math

import jax
import jax.numpy as jnp
from jax import lax
from jax.experimental import pallas as pl
from jax.experimental.pallas import tpu as pltpu
from jax.sharding import PartitionSpec as P

BLOCK = 16
GROUP = 16
MOD = 4093
HIT = 64
DENSE_BYTES = 8 * 2**20
LIMIT = 16 * 2**20


def tile_mask(code_block, living):
    tile_side = code_block.shape[1] // 2
    row_code = code_block[:, :tile_side][:, :, None]
    col_code = code_block[:, tile_side:][:, None, :]
    hashed = (row_code * col_code + row_code + 3 * col_code) % MOD
    return ((hashed < HIT) & living[:, None, None]).astype(jnp.bfloat16)


def accumulate(codes_dev, rows_dev, cols_dev, count_dev, source, out_tiles, backward):
    tile_side = source.shape[1]
    width_feat = source.shape[2]

    def block_step(block_id, summed):
        slot_start = block_id * BLOCK
        code_block = lax.dynamic_slice_in_dim(codes_dev, slot_start, BLOCK, 0)
        row_block = lax.dynamic_slice_in_dim(rows_dev, slot_start, BLOCK, 0)
        col_block = lax.dynamic_slice_in_dim(cols_dev, slot_start, BLOCK, 0)
        slot_ids = slot_start + jnp.arange(BLOCK, dtype=jnp.int32)
        target = col_block if backward else row_block
        anchor = row_block if backward else col_block
        living = slot_ids < count_dev
        keep = tile_mask(code_block, living)
        picked = jnp.take(source, anchor, axis=0)
        if backward:
            product = jnp.einsum("tij,tif->tjf", keep, picked, preferred_element_type=jnp.float32)
        else:
            product = jnp.einsum("tij,tjf->tif", keep, picked, preferred_element_type=jnp.float32)
        return summed.at[target].add(product)

    start_sum = jnp.zeros((out_tiles, tile_side, width_feat), jnp.float32)
    loop_count = codes_dev.shape[0] // BLOCK
    summed = lax.fori_loop(0, loop_count, block_step, start_sum)
    return summed.reshape(out_tiles * tile_side, width_feat)


def dense_part(aggregate, weight, bias, cotangent, inv_root):
    preact = jnp.dot(aggregate, weight, preferred_element_type=jnp.float32) + bias
    hidden = jax.nn.elu(preact).astype(jnp.bfloat16)
    elu_slope = jnp.where(preact > 0, 1.0, jnp.exp(jnp.minimum(preact, 0.0)))
    grad_pre = cotangent.astype(jnp.float32) * elu_slope
    grad_pre_b = grad_pre.astype(jnp.bfloat16)
    grad_weight = lax.dot_general(
        aggregate, grad_pre_b, (((0,), (0,)), ((), ())), preferred_element_type=jnp.float32
    )
    grad_bias = jnp.sum(grad_pre, axis=0)
    grad_agg = jnp.dot(grad_pre_b, weight.T, preferred_element_type=jnp.float32)
    grad_scaled = (inv_root * grad_agg).astype(jnp.bfloat16)
    return (hidden, grad_weight, grad_bias, grad_scaled)


def sparse_local(
    features, degree, weight, bias, cotangent, tile_rows, tile_cols, tile_count, tile_codes
):
    codes_dev = tile_codes[0, 0]
    rows_dev = tile_rows[0, 0]
    cols_dev = tile_cols[0, 0]
    count_dev = tile_count[0, 0, 0]
    pieces = features.shape[0]
    width_feat = features.shape[1]
    tile_side = codes_dev.shape[1] // 2
    row_devs = lax.axis_size("row")
    col_devs = lax.axis_size("col")
    grad_scale = 1.0 / math.sqrt(pieces * row_devs * col_devs)
    row_tiles = pieces * col_devs // tile_side
    col_tiles = pieces * row_devs // tile_side
    inv_root = lax.rsqrt(degree.astype(jnp.float32))[:, None]
    scaled = (inv_root * features.astype(jnp.float32)).astype(jnp.bfloat16)
    column_feats = lax.all_gather(scaled, "row", axis=0, tiled=True).reshape(
        col_tiles, tile_side, width_feat
    )
    row_terms = accumulate(codes_dev, rows_dev, cols_dev, count_dev, column_feats, row_tiles, False)
    row_sum = lax.psum_scatter(
        row_terms.astype(jnp.bfloat16), "col", scatter_dimension=0, tiled=True
    ).astype(jnp.float32)
    aggregate = (inv_root * row_sum).astype(jnp.bfloat16)
    hidden, grad_weight, grad_bias, grads = dense_part(
        aggregate, weight, bias, cotangent, inv_root
    )
    grad_weight, grad_bias = (
        lax.psum((grad_weight * grad_scale).astype(jnp.bfloat16), ("row", "col")),
        lax.psum((grad_bias * grad_scale).astype(jnp.bfloat16), ("row", "col")),
    )
    row_sources = lax.all_gather(grads, "col", axis=0, tiled=True).reshape(
        row_tiles, tile_side, width_feat
    )
    col_terms = accumulate(codes_dev, rows_dev, cols_dev, count_dev, row_sources, col_tiles, True)
    grad_sum = lax.psum_scatter(
        col_terms.astype(jnp.bfloat16), "row", scatter_dimension=0, tiled=True
    ).astype(jnp.float32)
    grad_features = (inv_root * grad_sum).astype(jnp.bfloat16)
    return (
        hidden,
        grad_features,
        grad_weight.astype(jnp.float32),
        grad_bias.astype(jnp.float32),
    )


def swap(value, axis, bits):
    size = lax.axis_size(axis)
    return lax.ppermute(value, axis, [(i, i ^ bits) for i in range(size)])


def column_of(row):
    n = row.shape[1]
    blocks = [
        jnp.broadcast_to(row[:, k : k + 128], (128, 128)).T for k in range(0, n, 128)
    ]
    return jnp.concatenate(blocks, axis=0)


def build_kernel(rows_ref, cols_ref, count_ref, codes_ref, block_ref, row_scr, col_scr):
    slots = codes_ref.shape[0]
    side = codes_ref.shape[1] // 2
    block_ref[...] = jnp.zeros_like(block_ref)
    row_code = codes_ref[:, :side].astype(jnp.float32) + 3.0
    row_code = jnp.where(row_code > MOD // 2, row_code - MOD, row_code)
    slot = lax.broadcasted_iota(jnp.int32, (slots, side), 0)
    row_code = jnp.where(slot < count_ref[0], row_code, 0.0)
    col_code = codes_ref[:, side:].astype(jnp.float32) + 1.0
    col_code = jnp.where(col_code > MOD // 2, col_code - MOD, col_code)
    coarse = 2.0**-12
    col_scr[...] = col_code * coarse + col_code * (1.0 / MOD - coarse)
    by_side = row_code.T
    groups = slots // GROUP
    for g in range(groups):
        row_scr[g] = by_side if g == 0 else pltpu.roll(by_side, slots - g * GROUP, axis=1)

    def step(g, carry):
        row_vals = row_scr[g]
        col_vals = col_scr[pl.ds(pl.multiple_of(g * GROUP, GROUP), GROUP), :]
        for t in range(GROUP):
            s = g * GROUP + t
            turns = jnp.broadcast_to(row_vals[:, t : t + 1], (side, side)) * jnp.broadcast_to(
                col_vals[t : t + 1, :], (side, side)
            )
            part = turns - jnp.round(turns)
            middle = 3.0 + (HIT - 1) / 2.0
            keep = jnp.abs(part - middle / MOD) < (HIT / 2.0) / MOD
            down = pl.ds(pl.multiple_of(rows_ref[s] * side, side), side)
            across = pl.ds(pl.multiple_of(cols_ref[s] * side, side), side)
            block_ref[down, across] += keep.astype(jnp.float32).astype(jnp.bfloat16)
        return carry

    lax.fori_loop(0, groups, step, 0)


def build_block(tile_rows, tile_cols, tile_count, codes, row_nodes, col_nodes):
    slots, width = codes.shape
    side = width // 2
    smem = pl.BlockSpec(memory_space=pltpu.SMEM)
    vmem = pl.BlockSpec(memory_space=pltpu.VMEM)
    return pl.pallas_call(
        build_kernel,
        out_shape=jax.ShapeDtypeStruct((row_nodes, col_nodes), jnp.bfloat16),
        in_specs=[smem, smem, smem, vmem],
        out_specs=vmem,
        scratch_shapes=[
            pltpu.VMEM((slots // GROUP, side, slots), jnp.float32),
            pltpu.VMEM((slots, side), jnp.float32),
        ],
        compiler_params=pltpu.CompilerParams(vmem_limit_bytes=LIMIT),
        cost_estimate=pl.CostEstimate(
            flops=20 * slots * side * side, bytes_accessed=2**24, transcendentals=0
        ),
        name="build_block",
    )(tile_rows, tile_cols, tile_count, codes)


def forward_kernel(n_row, n_col, block_ref, *refs):
    sources = refs[:n_row]
    outs = refs[n_row : n_row + n_col]
    source = refs[n_row + n_col]
    pieces = sources[0].shape[0]
    me_row = lax.axis_index("row")
    me_col = lax.axis_index("col")
    for k in range(n_row):
        at = pl.multiple_of((me_row ^ k) * pieces, pieces)
        source[pl.ds(at, pieces), :] = sources[k][...]
    whole = source[...]
    for k in range(n_col):
        at = pl.multiple_of((me_col ^ k) * pieces, pieces)
        outs[k][...] = jnp.dot(
            block_ref[pl.ds(at, pieces), :], whole, preferred_element_type=jnp.float32
        ).astype(jnp.bfloat16)


def forward_parts(block, sources, n_col):
    pieces, feat = sources[0].shape
    n_row = len(sources)
    vmem = pl.BlockSpec(memory_space=pltpu.VMEM)
    return pl.pallas_call(
        functools.partial(forward_kernel, n_row, n_col),
        out_shape=[jax.ShapeDtypeStruct((pieces, feat), jnp.bfloat16)] * n_col,
        in_specs=[vmem] * (1 + n_row),
        out_specs=[vmem] * n_col,
        scratch_shapes=[pltpu.VMEM((pieces * n_row, feat), jnp.bfloat16)],
        compiler_params=pltpu.CompilerParams(vmem_limit_bytes=LIMIT),
        name="forward_parts",
    )(block, *sources)


def dense_kernel(
    n_col, degree_ref, weight_ref, bias_ref, cot_ref, *refs
):
    parts = refs[:n_col]
    hidden_ref, grad_ref, terms_ref = refs[n_col:]
    total = parts[0][...].astype(jnp.float32)
    for k in range(1, n_col):
        total += parts[k][...].astype(jnp.float32)
    inv_row = lax.rsqrt(degree_ref[...].astype(jnp.float32))
    aggregate = (column_of(inv_row) * total).astype(jnp.bfloat16)
    weight = weight_ref[...]
    preact = jnp.dot(aggregate, weight, preferred_element_type=jnp.float32) + bias_ref[...]
    decay = jnp.exp(jnp.minimum(preact, 0.0))
    positive = preact > 0
    hidden_ref[...] = jnp.where(positive, preact, decay - 1.0).astype(jnp.bfloat16)
    grad_pre = cot_ref[...].astype(jnp.float32) * jnp.where(positive, 1.0, decay)
    grad_pre_b = grad_pre.astype(jnp.bfloat16)
    back = lax.dot_general(
        weight, grad_pre_b, (((1,), (1,)), ((), ())), preferred_element_type=jnp.float32
    )
    grad_ref[...] = (inv_row * back).astype(jnp.bfloat16)
    feat = weight.shape[0]
    terms_ref[:feat, :] = lax.dot_general(
        aggregate, grad_pre_b, (((0,), (0,)), ((), ())), preferred_element_type=jnp.float32
    ).astype(jnp.bfloat16)
    bias_terms = jnp.sum(grad_pre, axis=0, keepdims=True)
    terms_ref[feat:, :] = jnp.broadcast_to(bias_terms, (16, feat)).astype(jnp.bfloat16)


def dense_step(degree, weight, bias, cotangent, parts):
    pieces, feat = cotangent.shape
    vmem = pl.BlockSpec(memory_space=pltpu.VMEM)
    return pl.pallas_call(
        functools.partial(dense_kernel, len(parts)),
        out_shape=[
            jax.ShapeDtypeStruct((pieces, feat), jnp.bfloat16),
            jax.ShapeDtypeStruct((feat, pieces), jnp.bfloat16),
            jax.ShapeDtypeStruct((feat + 16, feat), jnp.bfloat16),
        ],
        in_specs=[vmem] * (4 + len(parts)),
        out_specs=[vmem] * 3,
        compiler_params=pltpu.CompilerParams(vmem_limit_bytes=LIMIT),
        name="dense_step",
    )(degree.reshape(1, pieces), weight, bias.reshape(1, feat), cotangent, *parts)


def backward_kernel(n_row, n_col, first, block_ref, *refs):
    sources = refs[:n_col]
    out_ref = refs[n_col]
    pieces = sources[0].shape[1]
    feat = sources[0].shape[0]
    me_row = lax.axis_index("row")
    me_col = lax.axis_index("col")
    for m in range(n_row // 2):
        across = pl.ds(pl.multiple_of((me_row ^ (2 * m + first)) * pieces, pieces), pieces)
        total = jnp.zeros((feat, pieces), jnp.float32)
        for k in range(n_col):
            down = pl.ds(pl.multiple_of((me_col ^ k) * pieces, pieces), pieces)
            total += jnp.dot(
                sources[k][...], block_ref[down, across], preferred_element_type=jnp.float32
            )
        out_ref[m * feat : (m + 1) * feat, :] = total.astype(jnp.bfloat16)


def backward_parts(block, sources, n_row, first):
    feat, pieces = sources[0].shape
    n_col = len(sources)
    vmem = pl.BlockSpec(memory_space=pltpu.VMEM)
    return pl.pallas_call(
        functools.partial(backward_kernel, n_row, n_col, first),
        out_shape=jax.ShapeDtypeStruct((n_row // 2 * feat, pieces), jnp.bfloat16),
        in_specs=[vmem] * (1 + n_col),
        out_specs=vmem,
        compiler_params=pltpu.CompilerParams(vmem_limit_bytes=LIMIT),
        name="backward_other" if first else "backward_own",
    )(block, *sources)


def pair_kernel(n, mine_ref, theirs_ref, *refs):
    terms, outs = refs[:-n], refs[-n:]
    feat = outs[0].shape[0]
    for m in range(n):
        span = slice(m * feat, (m + 1) * feat)
        outs[m][...] = (
            mine_ref[span, :].astype(jnp.float32) + theirs_ref[span, :].astype(jnp.float32)
        ).astype(jnp.bfloat16)


def pair_sum(mine, theirs, n):
    rows, width = mine.shape
    vmem = pl.BlockSpec(memory_space=pltpu.VMEM)
    return pl.pallas_call(
        functools.partial(pair_kernel, n),
        out_shape=[jax.ShapeDtypeStruct((rows // n, width), jnp.bfloat16)] * n,
        in_specs=[vmem] * 2,
        out_specs=[vmem] * n,
        compiler_params=pltpu.CompilerParams(vmem_limit_bytes=LIMIT),
        name="pair_sum",
    )(mine, theirs)


def finish_kernel(n, degree_ref, *refs):
    parts, out_ref = refs[:n], refs[n]
    total = parts[0][...].astype(jnp.float32)
    for k in range(1, n):
        total += parts[k][...].astype(jnp.float32)
    inv_row = lax.rsqrt(degree_ref[...].astype(jnp.float32))
    out_ref[...] = (inv_row * total).T.astype(jnp.bfloat16)


def finish(degree, parts):
    feat, pieces = parts[0].shape
    vmem = pl.BlockSpec(memory_space=pltpu.VMEM)
    return pl.pallas_call(
        functools.partial(finish_kernel, len(parts)),
        out_shape=jax.ShapeDtypeStruct((pieces, feat), jnp.bfloat16),
        in_specs=[vmem] * (1 + len(parts)),
        out_specs=vmem,
        compiler_params=pltpu.CompilerParams(vmem_limit_bytes=LIMIT),
        name="finish",
    )(degree.reshape(1, pieces), *parts)


def terms_kernel(n, scale, *refs):
    parts, out_ref = refs[:n], refs[n]
    total = parts[0][...].astype(jnp.float32)
    for k in range(1, n):
        total += parts[k][...].astype(jnp.float32)
    out_ref[...] = (total * scale).astype(out_ref.dtype)


def terms_sum(parts, scale, dtype):
    vmem = pl.BlockSpec(memory_space=pltpu.VMEM)
    return pl.pallas_call(
        functools.partial(terms_kernel, len(parts), scale),
        out_shape=jax.ShapeDtypeStruct(parts[0].shape, dtype),
        in_specs=[vmem] * len(parts),
        out_specs=vmem,
        compiler_params=pltpu.CompilerParams(vmem_limit_bytes=LIMIT),
        name="terms_sum",
    )(*parts)


def dense_local(
    features, degree, weight, bias, cotangent, tile_rows, tile_cols, tile_count, tile_codes
):
    pieces, feat = features.shape
    n_row = lax.axis_size("row")
    n_col = lax.axis_size("col")
    grad_scale = 1.0 / math.sqrt(pieces * n_row * n_col)
    inv_root = lax.rsqrt(degree.astype(jnp.float32))[:, None]
    scaled = (inv_root * features.astype(jnp.float32)).astype(jnp.bfloat16)
    block = build_block(
        tile_rows[0, 0],
        tile_cols[0, 0],
        tile_count[0, 0],
        tile_codes[0, 0],
        pieces * n_col,
        pieces * n_row,
    )
    sources = [None] * n_row
    sources[0] = scaled
    for m in range(2, n_row, 2):
        sources[m] = swap(scaled, "row", m)
    for m in range(0, n_row, 2):
        sources[m + 1] = swap(sources[m], "row", 1)
    parts = forward_parts(block, sources, n_col)
    landed = [parts[0]] + [swap(parts[k], "col", k) for k in range(1, n_col)]
    hidden, grad_own, terms = dense_step(degree, weight, bias, cotangent, landed)
    grads = [grad_own] + [swap(grad_own, "col", k) for k in range(1, n_col)]
    for_other = backward_parts(block, grads, n_row, 1)
    from_other = swap(for_other, "row", 1)
    for_own = backward_parts(block, grads, n_row, 0)
    chunks = pair_sum(for_own, from_other, n_row // 2)
    landed = [chunks[0]] + [swap(chunks[m], "row", 2 * m) for m in range(1, n_row // 2)]
    grad_features = finish(degree, landed)
    by_chip = terms_sum(
        [terms] + [swap(terms, "row", k) for k in range(1, n_row)], 1.0, jnp.bfloat16
    )
    all_terms = terms_sum(
        [by_chip] + [swap(by_chip, "col", k) for k in range(1, n_col)], grad_scale, jnp.float32
    )
    return (hidden, grad_features, all_terms[:feat], all_terms[feat])


def power_of_two(n):
    return n & (n - 1) == 0


def solution(mesh):
    placed = (
        P(("row", "col"), None),
        P(("row", "col")),
        P(),
        P(),
        P(("row", "col"), None),
        P("row", "col", None),
        P("row", "col", None),
        P("row", "col", None),
        P("row", "col", None, None),
    )
    n_row, n_col = mesh.shape["row"], mesh.shape["col"]

    def local(features, *rest):
        block_bytes = 2 * features.shape[0] ** 2 * n_row * n_col
        paired = power_of_two(n_row) and power_of_two(n_col) and n_row > 1
        if paired and block_bytes <= DENSE_BYTES:
            return dense_local(features, *rest)
        return sparse_local(features, *rest)

    return jax.shard_map(
        local,
        mesh=mesh,
        in_specs=placed,
        out_specs=(P(("row", "col"), None), P(("row", "col"), None), P(), P()),
        check_vma=False,
    )
```

```python
import functools
import math

import jax
import jax.numpy as jnp
from jax import lax
from jax.experimental import pallas as pl
from jax.experimental.pallas import tpu as pltpu
from jax.sharding import PartitionSpec as P

BLOCK = 16
GROUP = 16
MOD = 4093
HIT = 64
DENSE_BYTES = 8 * 2**20
LIMIT = 16 * 2**20


def tile_mask(code_block, living):
    tile_side = code_block.shape[1] // 2
    row_code = code_block[:, :tile_side][:, :, None]
    col_code = code_block[:, tile_side:][:, None, :]
    hashed = (row_code * col_code + row_code + 3 * col_code) % MOD
    return ((hashed < HIT) & living[:, None, None]).astype(jnp.bfloat16)


def accumulate(codes_dev, rows_dev, cols_dev, count_dev, source, out_tiles, backward):
    tile_side = source.shape[1]
    width_feat = source.shape[2]

    def block_step(block_id, summed):
        slot_start = block_id * BLOCK
        code_block = lax.dynamic_slice_in_dim(codes_dev, slot_start, BLOCK, 0)
        row_block = lax.dynamic_slice_in_dim(rows_dev, slot_start, BLOCK, 0)
        col_block = lax.dynamic_slice_in_dim(cols_dev, slot_start, BLOCK, 0)
        slot_ids = slot_start + jnp.arange(BLOCK, dtype=jnp.int32)
        target = col_block if backward else row_block
        anchor = row_block if backward else col_block
        living = slot_ids < count_dev
        keep = tile_mask(code_block, living)
        picked = jnp.take(source, anchor, axis=0)
        if backward:
            product = jnp.einsum("tij,tif->tjf", keep, picked, preferred_element_type=jnp.float32)
        else:
            product = jnp.einsum("tij,tjf->tif", keep, picked, preferred_element_type=jnp.float32)
        return summed.at[target].add(product)

    start_sum = jnp.zeros((out_tiles, tile_side, width_feat), jnp.float32)
    loop_count = codes_dev.shape[0] // BLOCK
    summed = lax.fori_loop(0, loop_count, block_step, start_sum)
    return summed.reshape(out_tiles * tile_side, width_feat)


def dense_part(aggregate, weight, bias, cotangent, inv_root):
    preact = jnp.dot(aggregate, weight, preferred_element_type=jnp.float32) + bias
    hidden = jax.nn.elu(preact).astype(jnp.bfloat16)
    elu_slope = jnp.where(preact > 0, 1.0, jnp.exp(jnp.minimum(preact, 0.0)))
    grad_pre = cotangent.astype(jnp.float32) * elu_slope
    grad_pre_b = grad_pre.astype(jnp.bfloat16)
    grad_weight = lax.dot_general(
        aggregate, grad_pre_b, (((0,), (0,)), ((), ())), preferred_element_type=jnp.float32
    )
    grad_bias = jnp.sum(grad_pre, axis=0)
    grad_agg = jnp.dot(grad_pre_b, weight.T, preferred_element_type=jnp.float32)
    grad_scaled = (inv_root * grad_agg).astype(jnp.bfloat16)
    return (hidden, grad_weight, grad_bias, grad_scaled)


def sparse_local(
    features, degree, weight, bias, cotangent, tile_rows, tile_cols, tile_count, tile_codes
):
    codes_dev = tile_codes[0, 0]
    rows_dev = tile_rows[0, 0]
    cols_dev = tile_cols[0, 0]
    count_dev = tile_count[0, 0, 0]
    pieces = features.shape[0]
    width_feat = features.shape[1]
    tile_side = codes_dev.shape[1] // 2
    row_devs = lax.axis_size("row")
    col_devs = lax.axis_size("col")
    grad_scale = 1.0 / math.sqrt(pieces * row_devs * col_devs)
    row_tiles = pieces * col_devs // tile_side
    col_tiles = pieces * row_devs // tile_side
    inv_root = lax.rsqrt(degree.astype(jnp.float32))[:, None]
    scaled = (inv_root * features.astype(jnp.float32)).astype(jnp.bfloat16)
    column_feats = lax.all_gather(scaled, "row", axis=0, tiled=True).reshape(
        col_tiles, tile_side, width_feat
    )
    row_terms = accumulate(codes_dev, rows_dev, cols_dev, count_dev, column_feats, row_tiles, False)
    row_sum = lax.psum_scatter(
        row_terms.astype(jnp.bfloat16), "col", scatter_dimension=0, tiled=True
    ).astype(jnp.float32)
    aggregate = (inv_root * row_sum).astype(jnp.bfloat16)
    hidden, grad_weight, grad_bias, grads = dense_part(
        aggregate, weight, bias, cotangent, inv_root
    )
    grad_weight, grad_bias = (
        lax.psum((grad_weight * grad_scale).astype(jnp.bfloat16), ("row", "col")),
        lax.psum((grad_bias * grad_scale).astype(jnp.bfloat16), ("row", "col")),
    )
    row_sources = lax.all_gather(grads, "col", axis=0, tiled=True).reshape(
        row_tiles, tile_side, width_feat
    )
    col_terms = accumulate(codes_dev, rows_dev, cols_dev, count_dev, row_sources, col_tiles, True)
    grad_sum = lax.psum_scatter(
        col_terms.astype(jnp.bfloat16), "row", scatter_dimension=0, tiled=True
    ).astype(jnp.float32)
    grad_features = (inv_root * grad_sum).astype(jnp.bfloat16)
    return (
        hidden,
        grad_features,
        grad_weight.astype(jnp.float32),
        grad_bias.astype(jnp.float32),
    )


def swap(value, axis, bits):
    size = lax.axis_size(axis)
    return lax.ppermute(value, axis, [(i, i ^ bits) for i in range(size)])


def column_of(row):
    n = row.shape[1]
    blocks = [
        jnp.broadcast_to(row[:, k : k + 128], (128, 128)).T for k in range(0, n, 128)
    ]
    return jnp.concatenate(blocks, axis=0)


def fetch(sources, targets, sems):
    copies = [
        pltpu.make_async_copy(src, dst, sems.at[k])
        for k, (src, dst) in enumerate(zip(sources, targets))
    ]
    for copy in copies:
        copy.start()
    return copies


def build_kernel(
    rows_vmem, cols_vmem, count_vmem, codes_ref, block_ref, row_scr, col_scr, rows_ref, cols_ref,
    count_ref, sems
):
    slots = codes_ref.shape[0]
    side = codes_ref.shape[1] // 2
    copies = fetch((rows_vmem, cols_vmem, count_vmem), (rows_ref, cols_ref, count_ref), sems)
    block_ref[...] = jnp.zeros_like(block_ref)
    for copy in copies:
        copy.wait()
    row_code = codes_ref[:, :side].astype(jnp.float32) + 3.0
    row_code = jnp.where(row_code > MOD // 2, row_code - MOD, row_code)
    slot = lax.broadcasted_iota(jnp.int32, (slots, side), 0)
    row_code = jnp.where(slot < count_ref[0, 0], row_code, 0.0)
    col_code = codes_ref[:, side:].astype(jnp.float32) + 1.0
    col_code = jnp.where(col_code > MOD // 2, col_code - MOD, col_code)
    coarse = 2.0**-12
    col_scr[...] = col_code * coarse + col_code * (1.0 / MOD - coarse)
    by_side = row_code.T
    groups = slots // GROUP
    for g in range(groups):
        row_scr[g] = by_side if g == 0 else pltpu.roll(by_side, slots - g * GROUP, axis=1)

    def step(g, carry):
        row_vals = row_scr[g]
        col_vals = col_scr[pl.ds(pl.multiple_of(g * GROUP, GROUP), GROUP), :]
        for t in range(GROUP):
            s = g * GROUP + t
            turns = jnp.broadcast_to(row_vals[:, t : t + 1], (side, side)) * jnp.broadcast_to(
                col_vals[t : t + 1, :], (side, side)
            )
            part = turns - jnp.round(turns)
            middle = 3.0 + (HIT - 1) / 2.0
            keep = jnp.abs(part - middle / MOD) < (HIT / 2.0) / MOD
            down = pl.ds(pl.multiple_of(rows_ref[0, s] * side, side), side)
            across = pl.ds(pl.multiple_of(cols_ref[0, s] * side, side), side)
            block_ref[down, across] += keep.astype(jnp.float32).astype(jnp.bfloat16)
        return carry

    lax.fori_loop(0, groups, step, 0)


def build_block(tile_rows, tile_cols, tile_count, codes, row_nodes, col_nodes):
    slots, width = codes.shape
    side = width // 2
    vmem = pl.BlockSpec(memory_space=pltpu.VMEM)
    return pl.pallas_call(
        build_kernel,
        out_shape=jax.ShapeDtypeStruct((row_nodes, col_nodes), jnp.bfloat16),
        in_specs=[vmem] * 4,
        out_specs=vmem,
        scratch_shapes=[
            pltpu.VMEM((slots // GROUP, side, slots), jnp.float32),
            pltpu.VMEM((slots, side), jnp.float32),
            pltpu.SMEM((1, slots), jnp.int32),
            pltpu.SMEM((1, slots), jnp.int32),
            pltpu.SMEM((1, 1), jnp.int32),
            pltpu.SemaphoreType.DMA((3,)),
        ],
        compiler_params=pltpu.CompilerParams(vmem_limit_bytes=LIMIT),
        cost_estimate=pl.CostEstimate(
            flops=20 * slots * side * side, bytes_accessed=2**24, transcendentals=0
        ),
        name="build_block",
    )(tile_rows, tile_cols, tile_count, codes)


def forward_kernel(n_row, far, block_ref, *refs):
    sources = refs[:n_row]
    outs = refs[n_row : n_row + len(far)]
    source = refs[-1]
    pieces = sources[0].shape[0]
    me_row = lax.axis_index("row")
    me_col = lax.axis_index("col")
    for k in range(n_row):
        at = pl.multiple_of((me_row ^ k) * pieces, pieces)
        source[pl.ds(at, pieces), :] = sources[k][...]
    whole = source[...]
    for out, k in zip(outs, far):
        at = pl.multiple_of((me_col ^ k) * pieces, pieces)
        out[...] = jnp.dot(
            block_ref[pl.ds(at, pieces), :], whole, preferred_element_type=jnp.float32
        ).astype(jnp.bfloat16)


def forward_parts(block, sources, far, name):
    pieces, feat = sources[0].shape
    n_row = len(sources)
    vmem = pl.BlockSpec(memory_space=pltpu.VMEM)
    return pl.pallas_call(
        functools.partial(forward_kernel, n_row, far),
        out_shape=[jax.ShapeDtypeStruct((pieces, feat), jnp.bfloat16)] * len(far),
        in_specs=[vmem] * (1 + n_row),
        out_specs=[vmem] * len(far),
        scratch_shapes=[pltpu.VMEM((pieces * n_row, feat), jnp.bfloat16)],
        compiler_params=pltpu.CompilerParams(vmem_limit_bytes=LIMIT),
        name=name,
    )(block, *sources)


def slope_of(aggregate, weight, bias, cotangent):
    preact = jnp.dot(aggregate, weight, preferred_element_type=jnp.float32) + bias
    decay = jnp.exp(jnp.minimum(preact, 0.0))
    positive = preact > 0
    grad_pre = cotangent.astype(jnp.float32) * jnp.where(positive, 1.0, decay)
    return jnp.where(positive, preact, decay - 1.0), grad_pre


def gradient_kernel(n_col, degree_ref, weight_ref, bias_ref, cot_ref, *refs):
    parts = refs[:n_col]
    grad_ref, both_ref, aggregate_ref = refs[n_col:]
    total = parts[0][...].astype(jnp.float32)
    for k in range(1, n_col):
        total += parts[k][...].astype(jnp.float32)
    inv_row = lax.rsqrt(degree_ref[...].astype(jnp.float32))
    aggregate = (column_of(inv_row) * total).astype(jnp.bfloat16)
    aggregate_ref[...] = aggregate
    weight = weight_ref[...]
    feat = weight.shape[0]
    half = feat // 2
    _, grad_pre = slope_of(aggregate, weight, bias_ref[...], cot_ref[...])
    grad_pre_b = grad_pre.astype(jnp.bfloat16)
    back = lax.dot_general(
        weight, grad_pre_b, (((1,), (1,)), ((), ())), preferred_element_type=jnp.float32
    )
    grad = (inv_row * back).astype(jnp.bfloat16)
    grad_ref[...] = grad
    both_ref[:feat, :] = grad
    weight_terms = lax.dot_general(
        aggregate, grad_pre_b, (((0,), (0,)), ((), ())), preferred_element_type=jnp.float32
    ).astype(jnp.bfloat16)
    both_ref[feat : feat + half, :feat] = weight_terms[:half]
    both_ref[feat : feat + half, feat:] = weight_terms[half:]
    bias_terms = jnp.sum(grad_pre, axis=0, keepdims=True)
    bias_terms = jnp.broadcast_to(bias_terms, (16, feat)).astype(jnp.bfloat16)
    both_ref[feat + half :, :feat] = bias_terms
    both_ref[feat + half :, feat:] = bias_terms


def gradient_step(degree, weight, bias, cotangent, parts):
    pieces, feat = cotangent.shape
    vmem = pl.BlockSpec(memory_space=pltpu.VMEM)
    return pl.pallas_call(
        functools.partial(gradient_kernel, len(parts)),
        out_shape=[
            jax.ShapeDtypeStruct((feat, pieces), jnp.bfloat16),
            jax.ShapeDtypeStruct((feat + feat // 2 + 16, pieces), jnp.bfloat16),
            jax.ShapeDtypeStruct((pieces, feat), jnp.bfloat16),
        ],
        in_specs=[vmem] * (4 + len(parts)),
        out_specs=[vmem] * 3,
        compiler_params=pltpu.CompilerParams(vmem_limit_bytes=LIMIT),
        name="gradient_step",
    )(degree.reshape(1, pieces), weight, bias.reshape(1, feat), cotangent, *parts)


def hidden_kernel(weight_ref, bias_ref, cot_ref, aggregate_ref, hidden_ref):
    hidden, _ = slope_of(aggregate_ref[...], weight_ref[...], bias_ref[...], cot_ref[...])
    hidden_ref[...] = hidden.astype(jnp.bfloat16)


def hidden_step(weight, bias, cotangent, aggregate):
    pieces, feat = cotangent.shape
    vmem = pl.BlockSpec(memory_space=pltpu.VMEM)
    return pl.pallas_call(
        hidden_kernel,
        out_shape=jax.ShapeDtypeStruct((pieces, feat), jnp.bfloat16),
        in_specs=[vmem] * 4,
        out_specs=vmem,
        compiler_params=pltpu.CompilerParams(vmem_limit_bytes=LIMIT),
        name="hidden_step",
    )(weight, bias.reshape(1, feat), cotangent, aggregate)


def backward_kernel(n_row, n_col, first, block_ref, *refs):
    sources, terms = refs[:n_col], refs[n_col:-1]
    out_ref = refs[-1]
    feat, pieces = sources[0].shape
    me_row = lax.axis_index("row")
    me_col = lax.axis_index("col")
    for m in range(n_row // 2):
        across = pl.ds(pl.multiple_of((me_row ^ (2 * m + first)) * pieces, pieces), pieces)
        total = jnp.zeros((feat, pieces), jnp.float32)
        for k in range(n_col):
            down = pl.ds(pl.multiple_of((me_col ^ k) * pieces, pieces), pieces)
            total += jnp.dot(
                sources[k][:feat, :], block_ref[down, across], preferred_element_type=jnp.float32
            )
        out_ref[m * feat : (m + 1) * feat, :] = total.astype(jnp.bfloat16)
    if terms:
        out_ref[n_row // 2 * feat :, :] = sum_of(terms).astype(jnp.bfloat16)


def sum_of(refs):
    total = refs[0][...].astype(jnp.float32)
    for ref in refs[1:]:
        total += ref[...].astype(jnp.float32)
    return total


def backward_parts(block, sources, terms, n_row, first):
    feat, pieces = sources[0].shape
    n_col = len(sources)
    extra = terms[0].shape[0] if terms else 0
    vmem = pl.BlockSpec(memory_space=pltpu.VMEM)
    return pl.pallas_call(
        functools.partial(backward_kernel, n_row, n_col, first),
        out_shape=jax.ShapeDtypeStruct((n_row // 2 * feat + extra, pieces), jnp.bfloat16),
        in_specs=[vmem] * (1 + n_col + len(terms)),
        out_specs=vmem,
        compiler_params=pltpu.CompilerParams(vmem_limit_bytes=LIMIT),
        name="backward_other" if first else "backward_own",
    )(block, *sources, *terms)


def pair_kernel(n, mine_ref, sent_ref, theirs_ref, *outs):
    feat = outs[0].shape[0]
    for m in range(n):
        span = slice(m * feat, (m + 1) * feat)
        outs[m][...] = (
            mine_ref[span, :].astype(jnp.float32) + theirs_ref[span, :].astype(jnp.float32)
        ).astype(jnp.bfloat16)
    outs[n][...] = (
        sent_ref[n * feat :, :].astype(jnp.float32) + theirs_ref[n * feat :, :].astype(jnp.float32)
    ).astype(jnp.bfloat16)


def pair_sum(mine, sent, theirs, n):
    rows, width = mine.shape
    vmem = pl.BlockSpec(memory_space=pltpu.VMEM)
    *chunks, terms = pl.pallas_call(
        functools.partial(pair_kernel, n),
        out_shape=[jax.ShapeDtypeStruct((rows // n, width), jnp.bfloat16)] * n
        + [jax.ShapeDtypeStruct((sent.shape[0] - rows, width), jnp.bfloat16)],
        in_specs=[vmem] * 3,
        out_specs=[vmem] * (n + 1),
        compiler_params=pltpu.CompilerParams(vmem_limit_bytes=LIMIT),
        name="pair_sum",
    )(mine, sent, theirs)
    return chunks, terms


def finish_kernel(n, scale, degree_ref, *refs):
    parts, terms = refs[:n], refs[n:-3]
    out_ref, weight_ref, bias_ref = refs[-3:]
    inv_row = lax.rsqrt(degree_ref[...].astype(jnp.float32))
    out_ref[...] = (inv_row * sum_of(parts)).T.astype(jnp.bfloat16)
    total = sum_of(terms) * scale
    feat = weight_ref.shape[0]
    half = feat // 2
    weight_ref[:half, :] = total[:half, :feat]
    weight_ref[half:, :] = total[:half, feat:]
    bias_ref[...] = total[half : half + 1, :feat]


def finish(degree, parts, terms, scale):
    feat, pieces = parts[0].shape
    vmem = pl.BlockSpec(memory_space=pltpu.VMEM)
    grad_features, grad_weight, grad_bias = pl.pallas_call(
        functools.partial(finish_kernel, len(parts), scale),
        out_shape=[
            jax.ShapeDtypeStruct((pieces, feat), jnp.bfloat16),
            jax.ShapeDtypeStruct((feat, feat), jnp.float32),
            jax.ShapeDtypeStruct((1, feat), jnp.float32),
        ],
        in_specs=[vmem] * (1 + len(parts) + len(terms)),
        out_specs=[vmem] * 3,
        compiler_params=pltpu.CompilerParams(vmem_limit_bytes=LIMIT),
        name="finish",
    )(degree.reshape(1, pieces), *parts, *terms)
    return grad_features, grad_weight, grad_bias.reshape(feat)


def scale_kernel(n, degree_hbm, features_hbm, *refs):
    degree_ref, features_ref, sems = refs[-3:]
    out_ref = refs[n]
    first, second, *others = fetch(
        (degree_hbm, features_hbm) + refs[:n],
        (degree_ref, features_ref) + refs[n + 1 : 2 * n + 1],
        sems,
    )
    first.wait()
    inv_root = column_of(lax.rsqrt(degree_ref[...].astype(jnp.float32)))
    second.wait()
    out_ref[...] = (inv_root * features_ref[...].astype(jnp.float32)).astype(jnp.bfloat16)
    for copy in others:
        copy.wait()


def scale_rows(degree, features, *others):
    pieces, feat = features.shape
    n = len(others)
    operands = (degree.reshape(1, pieces), features, *others)
    return pl.pallas_call(
        functools.partial(scale_kernel, n),
        out_shape=[
            pltpu.VMEM(features.shape, jnp.bfloat16),
            *(pltpu.VMEM(x.shape, x.dtype) for x in others),
        ],
        in_specs=[pl.BlockSpec(memory_space=pl.ANY)] * (2 + n),
        out_specs=[pl.BlockSpec(memory_space=pltpu.VMEM)] * (1 + n),
        scratch_shapes=[
            pltpu.VMEM((1, pieces), jnp.int32),
            pltpu.VMEM((pieces, feat), jnp.bfloat16),
            pltpu.SemaphoreType.DMA((2 + n,)),
        ],
        compiler_params=pltpu.CompilerParams(vmem_limit_bytes=60*2**20),
        name="scale_rows",
    )(*operands)


def terms_kernel(feat, mine_ref, theirs_ref, out_ref):
    out_ref[...] = (
        mine_ref[feat:, :].astype(jnp.float32) + theirs_ref[feat:, :].astype(jnp.float32)
    ).astype(jnp.bfloat16)


def terms_sum(mine, theirs, feat):
    vmem = pl.BlockSpec(memory_space=pltpu.VMEM)
    return pl.pallas_call(
        functools.partial(terms_kernel, feat),
        out_shape=jax.ShapeDtypeStruct((mine.shape[0] - feat, mine.shape[1]), jnp.bfloat16),
        in_specs=[vmem] * 2,
        out_specs=vmem,
        compiler_params=pltpu.CompilerParams(vmem_limit_bytes=LIMIT),
        name="terms_sum",
    )(mine, theirs)


def dense_local(
    features, degree, weight, bias, cotangent, tile_rows, tile_cols, tile_count, tile_codes
):
    pieces, feat = features.shape
    n_row = lax.axis_size("row")
    n_col = lax.axis_size("col")
    grad_scale = 1.0 / math.sqrt(pieces * n_row * n_col)
    scaled, *lists = scale_rows(
        degree, features, tile_rows[0], tile_cols[0], tile_count[0], tile_codes[0, 0]
    )
    block = build_block(*lists, pieces * n_col, pieces * n_row)
    chips = list(range(n_row - 2, 0, -2))
    lines = list(range(n_col - 1, 0, -1))
    sources = [None] * n_row
    sources[0] = scaled
    for m in chips:
        sources[m] = swap(scaled, "row", m)
    sources[1] = swap(scaled, "row", 1)
    block, *landed = lax.optimization_barrier((block, *(sources[m] for m in chips)))
    for m, value in zip(chips, landed):
        sources[m] = value
        sources[m + 1] = swap(value, "row", 1)
    half = max(1, n_col // 2)
    far = forward_parts(block, sources, lines[:half], "forward_far")
    near = forward_parts(block, sources, lines[half:] + [0], "forward_near")
    parts = dict(zip(lines + [0], far + near))
    landed = [parts[0]] + [swap(parts[k], "col", k) for k in lines]
    grad_own, both, aggregate = gradient_step(degree, weight, bias, cotangent, landed)
    grads = [grad_own, swap(both, "col", 1)] + [swap(grad_own, "col", k) for k in range(2, n_col)]
    grads[1], aggregate = lax.optimization_barrier((grads[1], aggregate))
    hidden = hidden_step(weight, bias, cotangent, aggregate)
    terms = terms_sum(both, grads[1], feat)
    from_chips = [swap(terms, "row", m) for m in chips]
    grads[2:], from_chips = lax.optimization_barrier((grads[2:], from_chips))
    for_other = backward_parts(block, grads, [terms] + from_chips, n_row, 1)
    from_other = swap(for_other, "row", 1)
    for_own = backward_parts(block, grads, [], n_row, 0)
    chunks, terms = pair_sum(for_own, for_other, from_other, n_row // 2)
    landed = [chunks[0]] + [swap(chunks[m // 2], "row", m) for m in chips]
    for k in range(1, n_col.bit_length() - 1):
        terms = [terms, swap(terms, "col", 2**k)]
    grad_features, grad_weight, grad_bias = finish(degree, landed, terms, grad_scale)
    return (hidden, grad_features, grad_weight, grad_bias)


def power_of_two(n):
    return n & (n - 1) == 0


def solution(mesh):
    placed = (
        P(("row", "col"), None),
        P(("row", "col")),
        P(),
        P(),
        P(("row", "col"), None),
        P("row", "col", None),
        P("row", "col", None),
        P("row", "col", None),
        P("row", "col", None, None),
    )
    n_row, n_col = mesh.shape["row"], mesh.shape["col"]

    def local(features, *rest):
        block_bytes = 2 * features.shape[0] ** 2 * n_row * n_col
        paired = power_of_two(n_row) and power_of_two(n_col) and n_row > 1
        if paired and block_bytes <= DENSE_BYTES:
            return dense_local(features, *rest)
        return sparse_local(features, *rest)

    return jax.shard_map(
        local,
        mesh=mesh,
        in_specs=placed,
        out_specs=(P(("row", "col"), None), P(("row", "col"), None), P(), P()),
        check_vma=False,
    )
```

```python
import functools
import math

import jax
import jax.numpy as jnp
from jax import lax
from jax.experimental import pallas as pl
from jax.experimental.pallas import tpu as pltpu
from jax.sharding import PartitionSpec as P

BLOCK = 16
GROUP = 16
MOD = 4093
HIT = 64
DENSE_BYTES = 8 * 2**20
LIMIT = 16 * 2**20


def tile_mask(code_block, living):
    tile_side = code_block.shape[1] // 2
    row_code = code_block[:, :tile_side][:, :, None]
    col_code = code_block[:, tile_side:][:, None, :]
    hashed = (row_code * col_code + row_code + 3 * col_code) % MOD
    return ((hashed < HIT) & living[:, None, None]).astype(jnp.bfloat16)


def accumulate(codes_dev, rows_dev, cols_dev, count_dev, source, out_tiles, backward):
    tile_side = source.shape[1]
    width_feat = source.shape[2]

    def block_step(block_id, summed):
        slot_start = block_id * BLOCK
        code_block = lax.dynamic_slice_in_dim(codes_dev, slot_start, BLOCK, 0)
        row_block = lax.dynamic_slice_in_dim(rows_dev, slot_start, BLOCK, 0)
        col_block = lax.dynamic_slice_in_dim(cols_dev, slot_start, BLOCK, 0)
        slot_ids = slot_start + jnp.arange(BLOCK, dtype=jnp.int32)
        target = col_block if backward else row_block
        anchor = row_block if backward else col_block
        living = slot_ids < count_dev
        keep = tile_mask(code_block, living)
        picked = jnp.take(source, anchor, axis=0)
        if backward:
            product = jnp.einsum("tij,tif->tjf", keep, picked, preferred_element_type=jnp.float32)
        else:
            product = jnp.einsum("tij,tjf->tif", keep, picked, preferred_element_type=jnp.float32)
        return summed.at[target].add(product)

    start_sum = jnp.zeros((out_tiles, tile_side, width_feat), jnp.float32)
    loop_count = codes_dev.shape[0] // BLOCK
    summed = lax.fori_loop(0, loop_count, block_step, start_sum)
    return summed.reshape(out_tiles * tile_side, width_feat)


def dense_part(aggregate, weight, bias, cotangent, inv_root):
    preact = jnp.dot(aggregate, weight, preferred_element_type=jnp.float32) + bias
    hidden = jax.nn.elu(preact).astype(jnp.bfloat16)
    elu_slope = jnp.where(preact > 0, 1.0, jnp.exp(jnp.minimum(preact, 0.0)))
    grad_pre = cotangent.astype(jnp.float32) * elu_slope
    grad_pre_b = grad_pre.astype(jnp.bfloat16)
    grad_weight = lax.dot_general(
        aggregate, grad_pre_b, (((0,), (0,)), ((), ())), preferred_element_type=jnp.float32
    )
    grad_bias = jnp.sum(grad_pre, axis=0)
    grad_agg = jnp.dot(grad_pre_b, weight.T, preferred_element_type=jnp.float32)
    grad_scaled = (inv_root * grad_agg).astype(jnp.bfloat16)
    return (hidden, grad_weight, grad_bias, grad_scaled)


def sparse_local(
    features, degree, weight, bias, cotangent, tile_rows, tile_cols, tile_count, tile_codes
):
    codes_dev = tile_codes[0, 0]
    rows_dev = tile_rows[0, 0]
    cols_dev = tile_cols[0, 0]
    count_dev = tile_count[0, 0, 0]
    pieces = features.shape[0]
    width_feat = features.shape[1]
    tile_side = codes_dev.shape[1] // 2
    row_devs = lax.axis_size("row")
    col_devs = lax.axis_size("col")
    grad_scale = 1.0 / math.sqrt(pieces * row_devs * col_devs)
    row_tiles = pieces * col_devs // tile_side
    col_tiles = pieces * row_devs // tile_side
    inv_root = lax.rsqrt(degree.astype(jnp.float32))[:, None]
    scaled = (inv_root * features.astype(jnp.float32)).astype(jnp.bfloat16)
    column_feats = lax.all_gather(scaled, "row", axis=0, tiled=True).reshape(
        col_tiles, tile_side, width_feat
    )
    row_terms = accumulate(codes_dev, rows_dev, cols_dev, count_dev, column_feats, row_tiles, False)
    row_sum = lax.psum_scatter(
        row_terms.astype(jnp.bfloat16), "col", scatter_dimension=0, tiled=True
    ).astype(jnp.float32)
    aggregate = (inv_root * row_sum).astype(jnp.bfloat16)
    hidden, grad_weight, grad_bias, grads = dense_part(
        aggregate, weight, bias, cotangent, inv_root
    )
    grad_weight, grad_bias = (
        lax.psum((grad_weight * grad_scale).astype(jnp.bfloat16), ("row", "col")),
        lax.psum((grad_bias * grad_scale).astype(jnp.bfloat16), ("row", "col")),
    )
    row_sources = lax.all_gather(grads, "col", axis=0, tiled=True).reshape(
        row_tiles, tile_side, width_feat
    )
    col_terms = accumulate(codes_dev, rows_dev, cols_dev, count_dev, row_sources, col_tiles, True)
    grad_sum = lax.psum_scatter(
        col_terms.astype(jnp.bfloat16), "row", scatter_dimension=0, tiled=True
    ).astype(jnp.float32)
    grad_features = (inv_root * grad_sum).astype(jnp.bfloat16)
    return (
        hidden,
        grad_features,
        grad_weight.astype(jnp.float32),
        grad_bias.astype(jnp.float32),
    )


def swap(value, axis, bits):
    size = lax.axis_size(axis)
    return lax.ppermute(value, axis, [(i, i ^ bits) for i in range(size)])


def column_of(row):
    n = row.shape[1]
    blocks = [
        jnp.broadcast_to(row[:, k : k + 128], (128, 128)).T for k in range(0, n, 128)
    ]
    return jnp.concatenate(blocks, axis=0)


def fetch(sources, targets, sems):
    copies = [
        pltpu.make_async_copy(src, dst, sems.at[k])
        for k, (src, dst) in enumerate(zip(sources, targets))
    ]
    for copy in copies:
        copy.start()
    return copies


def build_kernel(lists_vmem, codes_ref, block_ref, row_scr, col_scr, lists_ref, sems):
    slots = codes_ref.shape[0]
    side = codes_ref.shape[1] // 2
    (copy,) = fetch((lists_vmem,), (lists_ref,), sems)
    block_ref[...] = jnp.zeros_like(block_ref)
    copy.wait()
    row_code = codes_ref[:, :side].astype(jnp.float32) + 3.0
    row_code = jnp.where(row_code > MOD // 2, row_code - MOD, row_code)
    slot = lax.broadcasted_iota(jnp.int32, (slots, side), 0)
    row_code = jnp.where(slot < lists_ref[2, 0], row_code, 0.0)
    col_code = codes_ref[:, side:].astype(jnp.float32) + 1.0
    col_code = jnp.where(col_code > MOD // 2, col_code - MOD, col_code)
    coarse = 2.0**-12
    col_scr[...] = col_code * coarse + col_code * (1.0 / MOD - coarse)
    by_side = row_code.T
    groups = slots // GROUP
    for g in range(groups):
        row_scr[g] = by_side if g == 0 else pltpu.roll(by_side, slots - g * GROUP, axis=1)

    def step(g, carry):
        row_vals = row_scr[g]
        col_vals = col_scr[pl.ds(pl.multiple_of(g * GROUP, GROUP), GROUP), :]
        for t in range(GROUP):
            s = g * GROUP + t
            turns = jnp.broadcast_to(row_vals[:, t : t + 1], (side, side)) * jnp.broadcast_to(
                col_vals[t : t + 1, :], (side, side)
            )
            part = turns - jnp.round(turns)
            middle = 3.0 + (HIT - 1) / 2.0
            keep = jnp.abs(part - middle / MOD) < (HIT / 2.0) / MOD
            down = pl.ds(pl.multiple_of(lists_ref[0, s] * side, side), side)
            across = pl.ds(pl.multiple_of(lists_ref[1, s] * side, side), side)
            block_ref[down, across] += keep.astype(jnp.float32).astype(jnp.bfloat16)
        return carry

    lax.fori_loop(0, groups, step, 0)


def build_block(lists, codes, row_nodes, col_nodes):
    slots, width = codes.shape
    side = width // 2
    vmem = pl.BlockSpec(memory_space=pltpu.VMEM)
    return pl.pallas_call(
        build_kernel,
        out_shape=jax.ShapeDtypeStruct((row_nodes, col_nodes), jnp.bfloat16),
        in_specs=[vmem] * 2,
        out_specs=vmem,
        scratch_shapes=[
            pltpu.VMEM((slots // GROUP, side, slots), jnp.float32),
            pltpu.VMEM((slots, side), jnp.float32),
            pltpu.SMEM(lists.shape, jnp.int32),
            pltpu.SemaphoreType.DMA((1,)),
        ],
        compiler_params=pltpu.CompilerParams(vmem_limit_bytes=LIMIT),
        cost_estimate=pl.CostEstimate(
            flops=20 * slots * side * side, bytes_accessed=2**24, transcendentals=0
        ),
        name="build_block",
    )(lists, codes)


def forward_kernel(n_row, far, block_ref, *refs):
    sources = refs[:n_row]
    outs = refs[n_row : n_row + len(far)]
    source = refs[-1]
    pieces = sources[0].shape[0]
    me_row = lax.axis_index("row")
    me_col = lax.axis_index("col")
    for k in range(n_row):
        at = pl.multiple_of((me_row ^ k) * pieces, pieces)
        source[pl.ds(at, pieces), :] = sources[k][...]
    whole = source[...]
    for out, k in zip(outs, far):
        at = pl.multiple_of((me_col ^ k) * pieces, pieces)
        out[...] = jnp.dot(
            block_ref[pl.ds(at, pieces), :], whole, preferred_element_type=jnp.float32
        ).astype(jnp.bfloat16)


def forward_parts(block, sources, far, name):
    pieces, feat = sources[0].shape
    n_row = len(sources)
    vmem = pl.BlockSpec(memory_space=pltpu.VMEM)
    return pl.pallas_call(
        functools.partial(forward_kernel, n_row, far),
        out_shape=[jax.ShapeDtypeStruct((pieces, feat), jnp.bfloat16)] * len(far),
        in_specs=[vmem] * (1 + n_row),
        out_specs=[vmem] * len(far),
        scratch_shapes=[pltpu.VMEM((pieces * n_row, feat), jnp.bfloat16)],
        compiler_params=pltpu.CompilerParams(vmem_limit_bytes=LIMIT),
        name=name,
    )(block, *sources)


def slope_of(aggregate, weight, bias, cotangent):
    preact = jnp.dot(aggregate, weight, preferred_element_type=jnp.float32) + bias
    decay = jnp.exp(jnp.minimum(preact, 0.0))
    positive = preact > 0
    grad_pre = cotangent.astype(jnp.float32) * jnp.where(positive, 1.0, decay)
    return jnp.where(positive, preact, decay - 1.0), grad_pre


def gradient_kernel(n_col, degree_ref, weight_ref, bias_ref, cot_ref, *refs):
    parts = refs[:n_col]
    grad_ref, both_ref, aggregate_ref = refs[n_col:]
    total = parts[0][...].astype(jnp.float32)
    for k in range(1, n_col):
        total += parts[k][...].astype(jnp.float32)
    inv_row = lax.rsqrt(degree_ref[...].astype(jnp.float32))
    aggregate = (column_of(inv_row) * total).astype(jnp.bfloat16)
    aggregate_ref[...] = aggregate
    weight = weight_ref[...]
    feat = weight.shape[0]
    half = feat // 2
    _, grad_pre = slope_of(aggregate, weight, bias_ref[...], cot_ref[...])
    grad_pre_b = grad_pre.astype(jnp.bfloat16)
    back = lax.dot_general(
        weight, grad_pre_b, (((1,), (1,)), ((), ())), preferred_element_type=jnp.float32
    )
    grad = (inv_row * back).astype(jnp.bfloat16)
    grad_ref[...] = grad
    both_ref[:feat, :] = grad
    weight_terms = lax.dot_general(
        aggregate, grad_pre_b, (((0,), (0,)), ((), ())), preferred_element_type=jnp.float32
    ).astype(jnp.bfloat16)
    both_ref[feat : feat + half, :feat] = weight_terms[:half]
    both_ref[feat : feat + half, feat:] = weight_terms[half:]
    bias_terms = jnp.sum(grad_pre, axis=0, keepdims=True)
    bias_terms = jnp.broadcast_to(bias_terms, (16, feat)).astype(jnp.bfloat16)
    both_ref[feat + half :, :feat] = bias_terms
    both_ref[feat + half :, feat:] = bias_terms


def gradient_step(degree, weight, bias, cotangent, parts):
    pieces, feat = cotangent.shape
    vmem = pl.BlockSpec(memory_space=pltpu.VMEM)
    return pl.pallas_call(
        functools.partial(gradient_kernel, len(parts)),
        out_shape=[
            jax.ShapeDtypeStruct((feat, pieces), jnp.bfloat16),
            jax.ShapeDtypeStruct((feat + feat // 2 + 16, pieces), jnp.bfloat16),
            jax.ShapeDtypeStruct((pieces, feat), jnp.bfloat16),
        ],
        in_specs=[vmem] * (4 + len(parts)),
        out_specs=[vmem] * 3,
        compiler_params=pltpu.CompilerParams(vmem_limit_bytes=LIMIT),
        name="gradient_step",
    )(degree.reshape(1, pieces), weight, bias.reshape(1, feat), cotangent, *parts)


def hidden_kernel(weight_ref, bias_ref, cot_ref, aggregate_ref, hidden_ref):
    hidden, _ = slope_of(aggregate_ref[...], weight_ref[...], bias_ref[...], cot_ref[...])
    hidden_ref[...] = hidden.astype(jnp.bfloat16)


def hidden_step(weight, bias, cotangent, aggregate):
    pieces, feat = cotangent.shape
    vmem = pl.BlockSpec(memory_space=pltpu.VMEM)
    return pl.pallas_call(
        hidden_kernel,
        out_shape=jax.ShapeDtypeStruct((pieces, feat), jnp.bfloat16),
        in_specs=[vmem] * 4,
        out_specs=vmem,
        compiler_params=pltpu.CompilerParams(vmem_limit_bytes=LIMIT),
        name="hidden_step",
    )(weight, bias.reshape(1, feat), cotangent, aggregate)


def backward_kernel(n_row, n_col, first, block_ref, *refs):
    sources, terms = refs[:n_col], refs[n_col:-1]
    out_ref = refs[-1]
    feat, pieces = sources[0].shape
    me_row = lax.axis_index("row")
    me_col = lax.axis_index("col")
    for m in range(n_row // 2):
        across = pl.ds(pl.multiple_of((me_row ^ (2 * m + first)) * pieces, pieces), pieces)
        total = jnp.zeros((feat, pieces), jnp.float32)
        for k in range(n_col):
            down = pl.ds(pl.multiple_of((me_col ^ k) * pieces, pieces), pieces)
            total += jnp.dot(
                sources[k][:feat, :], block_ref[down, across], preferred_element_type=jnp.float32
            )
        out_ref[m * feat : (m + 1) * feat, :] = total.astype(jnp.bfloat16)
    if terms:
        out_ref[n_row // 2 * feat :, :] = sum_of(terms).astype(jnp.bfloat16)


def sum_of(refs):
    total = refs[0][...].astype(jnp.float32)
    for ref in refs[1:]:
        total += ref[...].astype(jnp.float32)
    return total


def backward_parts(block, sources, terms, n_row, first):
    feat, pieces = sources[0].shape
    n_col = len(sources)
    extra = terms[0].shape[0] if terms else 0
    vmem = pl.BlockSpec(memory_space=pltpu.VMEM)
    return pl.pallas_call(
        functools.partial(backward_kernel, n_row, n_col, first),
        out_shape=jax.ShapeDtypeStruct((n_row // 2 * feat + extra, pieces), jnp.bfloat16),
        in_specs=[vmem] * (1 + n_col + len(terms)),
        out_specs=vmem,
        compiler_params=pltpu.CompilerParams(vmem_limit_bytes=LIMIT),
        name="backward_other" if first else "backward_own",
    )(block, *sources, *terms)


def pair_kernel(n, mine_ref, sent_ref, theirs_ref, *outs):
    feat = mine_ref.shape[0] // n
    terms = (
        sent_ref[n * feat :, :].astype(jnp.float32) + theirs_ref[n * feat :, :].astype(jnp.float32)
    ).astype(jnp.bfloat16)
    for m in range(n):
        span = slice(m * feat, (m + 1) * feat)
        outs[m][:feat, :] = (
            mine_ref[span, :].astype(jnp.float32) + theirs_ref[span, :].astype(jnp.float32)
        ).astype(jnp.bfloat16)
        outs[m][feat:, :] = terms


def pair_sum(mine, sent, theirs, n):
    rows, width = mine.shape
    vmem = pl.BlockSpec(memory_space=pltpu.VMEM)
    chunk = rows // n + sent.shape[0] - rows
    return pl.pallas_call(
        functools.partial(pair_kernel, n),
        out_shape=[jax.ShapeDtypeStruct((chunk, width), jnp.bfloat16)] * n,
        in_specs=[vmem] * 3,
        out_specs=[vmem] * n,
        compiler_params=pltpu.CompilerParams(vmem_limit_bytes=LIMIT),
        name="pair_sum",
    )(mine, sent, theirs)


def finish_kernel(scale, degree_ref, *refs):
    parts = refs[:-3]
    out_ref, weight_ref, bias_ref = refs[-3:]
    inv_row = lax.rsqrt(degree_ref[...].astype(jnp.float32))
    total = sum_of(parts)
    feat = weight_ref.shape[0]
    half = feat // 2
    out_ref[...] = (inv_row * total[:feat]).T.astype(jnp.bfloat16)
    weight_ref[:half, :] = total[feat : feat + half, :feat] * scale
    weight_ref[half:, :] = total[feat : feat + half, feat:] * scale
    bias_ref[...] = total[feat + half : feat + half + 1, :feat] * scale


def finish(degree, parts, feat, scale):
    pieces = parts[0].shape[1]
    vmem = pl.BlockSpec(memory_space=pltpu.VMEM)
    grad_features, grad_weight, grad_bias = pl.pallas_call(
        functools.partial(finish_kernel, scale),
        out_shape=[
            jax.ShapeDtypeStruct((pieces, feat), jnp.bfloat16),
            jax.ShapeDtypeStruct((feat, feat), jnp.float32),
            jax.ShapeDtypeStruct((1, feat), jnp.float32),
        ],
        in_specs=[vmem] * (1 + len(parts)),
        out_specs=[vmem] * 3,
        compiler_params=pltpu.CompilerParams(vmem_limit_bytes=LIMIT),
        name="finish",
    )(degree.reshape(1, pieces), *parts)
    return grad_features, grad_weight, grad_bias.reshape(feat)


def scale_kernel(
    degree_hbm, features_hbm, rows_hbm, cols_hbm, count_hbm, codes_hbm, out_ref, lists_ref,
    codes_ref, degree_ref, features_ref, count_ref, sems
):
    slots = codes_ref.shape[0]
    first, second, *others = fetch(
        (degree_hbm, features_hbm, rows_hbm.at[0], cols_hbm.at[0], count_hbm, codes_hbm),
        (
            degree_ref,
            features_ref,
            lists_ref.at[0:1, 0:slots],
            lists_ref.at[1:2, 0:slots],
            count_ref,
            codes_ref,
        ),
        sems,
    )
    first.wait()
    inv_root = column_of(lax.rsqrt(degree_ref[...].astype(jnp.float32)))
    second.wait()
    out_ref[...] = (inv_root * features_ref[...].astype(jnp.float32)).astype(jnp.bfloat16)
    for copy in others:
        copy.wait()
    lists_ref[2:3, :] = jnp.broadcast_to(count_ref[0], (1, slots))


def scale_rows(degree, features, tile_rows, tile_cols, tile_count, codes):
    pieces, feat = features.shape
    return pl.pallas_call(
        scale_kernel,
        out_shape=[
            pltpu.VMEM(features.shape, jnp.bfloat16),
            pltpu.VMEM((8, codes.shape[0]), jnp.int32),
            pltpu.VMEM(codes.shape, codes.dtype),
        ],
        in_specs=[pl.BlockSpec(memory_space=pl.ANY)] * 6,
        out_specs=[pl.BlockSpec(memory_space=pltpu.VMEM)] * 3,
        scratch_shapes=[
            pltpu.VMEM((1, pieces), jnp.int32),
            pltpu.VMEM((pieces, feat), jnp.bfloat16),
            pltpu.VMEM((1, 1, 1), jnp.int32),
            pltpu.SemaphoreType.DMA((6,)),
        ],
        compiler_params=pltpu.CompilerParams(vmem_limit_bytes=60 * 2**20),
        name="scale_rows",
    )(degree.reshape(1, pieces), features, tile_rows, tile_cols, tile_count, codes)


def terms_kernel(feat, mine_ref, theirs_ref, out_ref):
    out_ref[...] = (
        mine_ref[feat:, :].astype(jnp.float32) + theirs_ref[feat:, :].astype(jnp.float32)
    ).astype(jnp.bfloat16)


def terms_sum(mine, theirs, feat):
    vmem = pl.BlockSpec(memory_space=pltpu.VMEM)
    return pl.pallas_call(
        functools.partial(terms_kernel, feat),
        out_shape=jax.ShapeDtypeStruct((mine.shape[0] - feat, mine.shape[1]), jnp.bfloat16),
        in_specs=[vmem] * 2,
        out_specs=vmem,
        compiler_params=pltpu.CompilerParams(vmem_limit_bytes=LIMIT),
        name="terms_sum",
    )(mine, theirs)


def dense_local(
    features, degree, weight, bias, cotangent, tile_rows, tile_cols, tile_count, tile_codes
):
    pieces, feat = features.shape
    n_row = lax.axis_size("row")
    n_col = lax.axis_size("col")
    grad_scale = 1.0 / math.sqrt(pieces * n_row * n_col)
    scaled, lists, codes = scale_rows(
        degree, features, tile_rows, tile_cols, tile_count, tile_codes[0, 0]
    )
    block = build_block(lists, codes, pieces * n_col, pieces * n_row)
    chips = list(range(n_row - 2, 0, -2))
    lines = list(range(n_col - 1, 0, -1))
    sources = [None] * n_row
    sources[0] = scaled
    for m in chips:
        sources[m] = swap(scaled, "row", m)
    sources[1] = swap(scaled, "row", 1)
    block, *landed = lax.optimization_barrier((block, *(sources[m] for m in chips)))
    for m, value in zip(chips, landed):
        sources[m] = value
        sources[m + 1] = swap(value, "row", 1)
    half = max(1, n_col // 2)
    far = forward_parts(block, sources, lines[:half], "forward_far")
    near = forward_parts(block, sources, lines[half:] + [0], "forward_near")
    parts = dict(zip(lines + [0], far + near))
    landed = [parts[0]] + [swap(parts[k], "col", k) for k in lines]
    grad_own, both, aggregate = gradient_step(degree, weight, bias, cotangent, landed)
    grads = [grad_own, swap(both, "col", 1)] + [swap(grad_own, "col", k) for k in range(2, n_col)]
    grads[1], aggregate = lax.optimization_barrier((grads[1], aggregate))
    hidden = hidden_step(weight, bias, cotangent, aggregate)
    terms = [terms_sum(both, grads[1], feat)]
    terms += [swap(terms[0], "col", k) for k in range(2, n_col, 2)]
    grads[2:], terms = lax.optimization_barrier((grads[2:], terms))
    for_other = backward_parts(block, grads, terms, n_row, 1)
    from_other = swap(for_other, "row", 1)
    for_own = backward_parts(block, grads, [], n_row, 0)
    chunks = pair_sum(for_own, for_other, from_other, n_row // 2)
    landed = [chunks[0]] + [swap(chunks[m // 2], "row", m) for m in chips]
    grad_features, grad_weight, grad_bias = finish(degree, landed, feat, grad_scale)
    return (hidden, grad_features, grad_weight, grad_bias)


def power_of_two(n):
    return n & (n - 1) == 0


def solution(mesh):
    placed = (
        P(("row", "col"), None),
        P(("row", "col")),
        P(),
        P(),
        P(("row", "col"), None),
        P("row", "col", None),
        P("row", "col", None),
        P("row", "col", None),
        P("row", "col", None, None),
    )
    n_row, n_col = mesh.shape["row"], mesh.shape["col"]

    def local(features, *rest):
        block_bytes = 2 * features.shape[0] ** 2 * n_row * n_col
        paired = power_of_two(n_row) and power_of_two(n_col) and n_row > 1
        if paired and block_bytes <= DENSE_BYTES:
            return dense_local(features, *rest)
        return sparse_local(features, *rest)

    return jax.shard_map(
        local,
        mesh=mesh,
        in_specs=placed,
        out_specs=(P(("row", "col"), None), P(("row", "col"), None), P(), P()),
        check_vma=False,
    )
```

```python
import functools
import math

import jax
import jax.numpy as jnp
from jax import lax
from jax.experimental import pallas as pl
from jax.experimental.pallas import tpu as pltpu
from jax.sharding import PartitionSpec as P

BLOCK = 16
GROUP = 32
MOD = 4093
HIT = 64
DENSE_BYTES = 8 * 2**20
LIMIT = 16 * 2**20


def tile_mask(code_block, living):
    tile_side = code_block.shape[1] // 2
    row_code = code_block[:, :tile_side][:, :, None]
    col_code = code_block[:, tile_side:][:, None, :]
    hashed = (row_code * col_code + row_code + 3 * col_code) % MOD
    return ((hashed < HIT) & living[:, None, None]).astype(jnp.bfloat16)


def accumulate(codes_dev, rows_dev, cols_dev, count_dev, source, out_tiles, backward):
    tile_side = source.shape[1]
    width_feat = source.shape[2]

    def block_step(block_id, summed):
        slot_start = block_id * BLOCK
        code_block = lax.dynamic_slice_in_dim(codes_dev, slot_start, BLOCK, 0)
        row_block = lax.dynamic_slice_in_dim(rows_dev, slot_start, BLOCK, 0)
        col_block = lax.dynamic_slice_in_dim(cols_dev, slot_start, BLOCK, 0)
        slot_ids = slot_start + jnp.arange(BLOCK, dtype=jnp.int32)
        target = col_block if backward else row_block
        anchor = row_block if backward else col_block
        living = slot_ids < count_dev
        keep = tile_mask(code_block, living)
        picked = jnp.take(source, anchor, axis=0)
        if backward:
            product = jnp.einsum("tij,tif->tjf", keep, picked, preferred_element_type=jnp.float32)
        else:
            product = jnp.einsum("tij,tjf->tif", keep, picked, preferred_element_type=jnp.float32)
        return summed.at[target].add(product)

    start_sum = jnp.zeros((out_tiles, tile_side, width_feat), jnp.float32)
    loop_count = codes_dev.shape[0] // BLOCK
    summed = lax.fori_loop(0, loop_count, block_step, start_sum)
    return summed.reshape(out_tiles * tile_side, width_feat)


def dense_part(aggregate, weight, bias, cotangent, inv_root):
    preact = jnp.dot(aggregate, weight, preferred_element_type=jnp.float32) + bias
    hidden = jax.nn.elu(preact).astype(jnp.bfloat16)
    elu_slope = jnp.where(preact > 0, 1.0, jnp.exp(jnp.minimum(preact, 0.0)))
    grad_pre = cotangent.astype(jnp.float32) * elu_slope
    grad_pre_b = grad_pre.astype(jnp.bfloat16)
    grad_weight = lax.dot_general(
        aggregate, grad_pre_b, (((0,), (0,)), ((), ())), preferred_element_type=jnp.float32
    )
    grad_bias = jnp.sum(grad_pre, axis=0)
    grad_agg = jnp.dot(grad_pre_b, weight.T, preferred_element_type=jnp.float32)
    grad_scaled = (inv_root * grad_agg).astype(jnp.bfloat16)
    return (hidden, grad_weight, grad_bias, grad_scaled)


def sparse_local(
    features, degree, weight, bias, cotangent, tile_rows, tile_cols, tile_count, tile_codes
):
    codes_dev = tile_codes[0, 0]
    rows_dev = tile_rows[0, 0]
    cols_dev = tile_cols[0, 0]
    count_dev = tile_count[0, 0, 0]
    pieces = features.shape[0]
    width_feat = features.shape[1]
    tile_side = codes_dev.shape[1] // 2
    row_devs = lax.axis_size("row")
    col_devs = lax.axis_size("col")
    grad_scale = 1.0 / math.sqrt(pieces * row_devs * col_devs)
    row_tiles = pieces * col_devs // tile_side
    col_tiles = pieces * row_devs // tile_side
    inv_root = lax.rsqrt(degree.astype(jnp.float32))[:, None]
    scaled = (inv_root * features.astype(jnp.float32)).astype(jnp.bfloat16)
    column_feats = lax.all_gather(scaled, "row", axis=0, tiled=True).reshape(
        col_tiles, tile_side, width_feat
    )
    row_terms = accumulate(codes_dev, rows_dev, cols_dev, count_dev, column_feats, row_tiles, False)
    row_sum = lax.psum_scatter(
        row_terms.astype(jnp.bfloat16), "col", scatter_dimension=0, tiled=True
    ).astype(jnp.float32)
    aggregate = (inv_root * row_sum).astype(jnp.bfloat16)
    hidden, grad_weight, grad_bias, grads = dense_part(
        aggregate, weight, bias, cotangent, inv_root
    )
    grad_weight, grad_bias = (
        lax.psum((grad_weight * grad_scale).astype(jnp.bfloat16), ("row", "col")),
        lax.psum((grad_bias * grad_scale).astype(jnp.bfloat16), ("row", "col")),
    )
    row_sources = lax.all_gather(grads, "col", axis=0, tiled=True).reshape(
        row_tiles, tile_side, width_feat
    )
    col_terms = accumulate(codes_dev, rows_dev, cols_dev, count_dev, row_sources, col_tiles, True)
    grad_sum = lax.psum_scatter(
        col_terms.astype(jnp.bfloat16), "row", scatter_dimension=0, tiled=True
    ).astype(jnp.float32)
    grad_features = (inv_root * grad_sum).astype(jnp.bfloat16)
    return (
        hidden,
        grad_features,
        grad_weight.astype(jnp.float32),
        grad_bias.astype(jnp.float32),
    )


def swap(value, axis, bits):
    size = lax.axis_size(axis)
    return lax.ppermute(value, axis, [(i, i ^ bits) for i in range(size)])


def column_of(row):
    n = row.shape[1]
    blocks = [
        jnp.broadcast_to(row[:, k : k + 128], (128, 128)).T for k in range(0, n, 128)
    ]
    return jnp.concatenate(blocks, axis=0)


def fetch(sources, targets, sems):
    copies = [
        pltpu.make_async_copy(src, dst, sems.at[k])
        for k, (src, dst) in enumerate(zip(sources, targets))
    ]
    for copy in copies:
        copy.start()
    return copies


def build_kernel(first, last, lists_vmem, count_ref, codes_ref, *refs):
    block_ref, row_scr, col_scr, lists_ref, sems = refs[-5:]
    slots = codes_ref.shape[0]
    side = codes_ref.shape[1] // 2
    (copy,) = fetch((lists_vmem,), (lists_ref,), sems)
    if first == 0:
        block_ref[...] = jnp.zeros_like(block_ref)
    row_code = codes_ref[:, :side].astype(jnp.float32) + 3.0
    row_code = jnp.where(row_code > MOD // 2, row_code - MOD, row_code)
    slot = lax.broadcasted_iota(jnp.int32, (slots, side), 0)
    row_code = jnp.where(slot < count_ref[0, 0, 0], row_code, 0.0)
    col_code = codes_ref[:, side:].astype(jnp.float32) + 1.0
    col_code = jnp.where(col_code > MOD // 2, col_code - MOD, col_code)
    coarse = 2.0**-12
    col_scr[...] = col_code * coarse + col_code * (1.0 / MOD - coarse)
    by_side = row_code.T
    groups = range(first // GROUP, last // GROUP)
    for g in groups:
        row_scr[g] = by_side if g == 0 else pltpu.roll(by_side, slots - g * GROUP, axis=1)
    copy.wait()
    middle = (3.0 + (HIT - 1) / 2.0) / MOD
    reach = jnp.bfloat16(2.0**-7)
    one, zero = jnp.bfloat16(1.0), jnp.bfloat16(0.0)

    def step(g, carry):
        row_vals = row_scr[g]
        col_vals = col_scr[pl.ds(pl.multiple_of(g * GROUP, GROUP), GROUP), :]
        for t in range(GROUP):
            s = g * GROUP + t
            turns = jnp.broadcast_to(row_vals[:, t : t + 1], (side, side)) * jnp.broadcast_to(
                col_vals[t : t + 1, :], (side, side)
            )
            part = turns - jnp.round(turns)
            keep = jnp.abs((part - middle).astype(jnp.bfloat16)) < reach
            down = pl.ds(pl.multiple_of(lists_ref[0, s] * side, side), side)
            across = pl.ds(pl.multiple_of(lists_ref[1, s] * side, side), side)
            block_ref[down, across] += jnp.where(keep, one, zero)
        return carry

    lax.fori_loop(groups.start, groups.stop, step, 0)


def build_block(lists, tile_count, codes, row_nodes, col_nodes, first, last, block=None):
    slots, width = codes.shape
    side = width // 2
    vmem = pl.BlockSpec(memory_space=pltpu.VMEM)
    begun = [] if block is None else [block]
    return pl.pallas_call(
        functools.partial(build_kernel, first, last),
        out_shape=pltpu.VMEM((row_nodes, col_nodes), jnp.bfloat16),
        in_specs=[vmem, pl.BlockSpec(memory_space=pltpu.SMEM), vmem] + [vmem] * len(begun),
        out_specs=vmem,
        input_output_aliases={3: 0} if begun else {},
        scratch_shapes=[
            pltpu.VMEM((slots // GROUP, side, slots), jnp.float32),
            pltpu.VMEM((slots, side), jnp.float32),
            pltpu.SMEM(lists.shape, jnp.int32),
            pltpu.SemaphoreType.DMA((1,)),
        ],
        compiler_params=pltpu.CompilerParams(vmem_limit_bytes=LIMIT),
        cost_estimate=pl.CostEstimate(
            flops=20 * (last - first) * side * side, bytes_accessed=2**23, transcendentals=0
        ),
        name="build_rest" if begun else "build_block",
    )(lists, tile_count, codes, *begun)


def stack_kernel(*refs):
    *parts, out_ref = refs
    rows = parts[0].shape[0]
    for m, part in enumerate(parts):
        out_ref[m * rows : (m + 1) * rows, :] = part[...]


def stack(parts):
    rows, width = parts[0].shape
    vmem = pl.BlockSpec(memory_space=pltpu.VMEM)
    return pl.pallas_call(
        stack_kernel,
        out_shape=jax.ShapeDtypeStruct((len(parts) * rows, width), parts[0].dtype),
        in_specs=[vmem] * len(parts),
        out_specs=vmem,
        compiler_params=pltpu.CompilerParams(vmem_limit_bytes=LIMIT),
        name="stack",
    )(*parts)


def forward_kernel(n_own, n_row, far, block_ref, *refs):
    own, other = refs[:n_own], refs[n_own : -1 - len(far)]
    outs = refs[-1 - len(far) : -1]
    source = refs[-1]
    pieces = own[0].shape[0]
    me_row = lax.axis_index("row")
    me_col = lax.axis_index("col")
    for m, part in enumerate(own):
        at = pl.multiple_of((me_row ^ (2 * m)) * pieces, pieces)
        source[pl.ds(at, pieces), :] = part[...]
    bits = 1
    for part in other:
        for k in range(part.shape[0] // pieces):
            at = pl.multiple_of((me_row ^ bits) * pieces, pieces)
            source[pl.ds(at, pieces), :] = part[k * pieces : (k + 1) * pieces, :]
            bits += 2
    whole = source[...]
    for out, k in zip(outs, far):
        at = pl.multiple_of((me_col ^ k) * pieces, pieces)
        out[...] = jnp.dot(
            block_ref[pl.ds(at, pieces), :], whole, preferred_element_type=jnp.float32
        ).astype(jnp.bfloat16)


def forward_parts(block, own, other, n_row, far, name):
    pieces, feat = own[0].shape
    vmem = pl.BlockSpec(memory_space=pltpu.VMEM)
    return pl.pallas_call(
        functools.partial(forward_kernel, len(own), n_row, far),
        out_shape=[jax.ShapeDtypeStruct((pieces, feat), jnp.bfloat16)] * len(far),
        in_specs=[vmem] * (1 + len(own) + len(other)),
        out_specs=[vmem] * len(far),
        scratch_shapes=[pltpu.VMEM((pieces * n_row, feat), jnp.bfloat16)],
        compiler_params=pltpu.CompilerParams(vmem_limit_bytes=LIMIT),
        name=name,
    )(block, *own, *other)


def slope_of(aggregate, weight, bias, cotangent):
    preact = jnp.dot(aggregate, weight, preferred_element_type=jnp.float32) + bias
    decay = jnp.exp(jnp.minimum(preact, 0.0))
    positive = preact > 0
    grad_pre = cotangent.astype(jnp.float32) * jnp.where(positive, 1.0, decay)
    return jnp.where(positive, preact, decay - 1.0), grad_pre


def gradient_kernel(n_col, degree_ref, weight_ref, bias_ref, cot_ref, *refs):
    parts = refs[:n_col]
    grad_ref, both_ref, aggregate_ref = refs[n_col:]
    total = parts[0][...].astype(jnp.float32)
    for k in range(1, n_col):
        total += parts[k][...].astype(jnp.float32)
    inv_row = lax.rsqrt(degree_ref[...].astype(jnp.float32))
    aggregate = (column_of(inv_row) * total).astype(jnp.bfloat16)
    aggregate_ref[...] = aggregate
    weight = weight_ref[...]
    feat = weight.shape[0]
    half = feat // 2
    _, grad_pre = slope_of(aggregate, weight, bias_ref[...], cot_ref[...])
    grad_pre_b = grad_pre.astype(jnp.bfloat16)
    back = lax.dot_general(
        weight, grad_pre_b, (((1,), (1,)), ((), ())), preferred_element_type=jnp.float32
    )
    grad = (inv_row * back).astype(jnp.bfloat16)
    grad_ref[...] = grad
    both_ref[:feat, :] = grad
    weight_terms = lax.dot_general(
        aggregate, grad_pre_b, (((0,), (0,)), ((), ())), preferred_element_type=jnp.float32
    ).astype(jnp.bfloat16)
    both_ref[feat : feat + half, :feat] = weight_terms[:half]
    both_ref[feat : feat + half, feat:] = weight_terms[half:]
    bias_terms = jnp.sum(grad_pre, axis=0, keepdims=True)
    bias_terms = jnp.broadcast_to(bias_terms, (16, feat)).astype(jnp.bfloat16)
    both_ref[feat + half :, :feat] = bias_terms
    both_ref[feat + half :, feat:] = bias_terms


def gradient_step(degree, weight, bias, cotangent, parts):
    pieces, feat = cotangent.shape
    vmem = pl.BlockSpec(memory_space=pltpu.VMEM)
    return pl.pallas_call(
        functools.partial(gradient_kernel, len(parts)),
        out_shape=[
            jax.ShapeDtypeStruct((feat, pieces), jnp.bfloat16),
            jax.ShapeDtypeStruct((feat + feat // 2 + 16, pieces), jnp.bfloat16),
            jax.ShapeDtypeStruct((pieces, feat), jnp.bfloat16),
        ],
        in_specs=[vmem] * (4 + len(parts)),
        out_specs=[vmem] * 3,
        compiler_params=pltpu.CompilerParams(vmem_limit_bytes=LIMIT),
        name="gradient_step",
    )(degree.reshape(1, pieces), weight, bias.reshape(1, feat), cotangent, *parts)


def hidden_kernel(weight_ref, bias_ref, cot_ref, aggregate_ref, hidden_ref):
    hidden, _ = slope_of(aggregate_ref[...], weight_ref[...], bias_ref[...], cot_ref[...])
    hidden_ref[...] = hidden.astype(jnp.bfloat16)


def hidden_step(weight, bias, cotangent, aggregate):
    pieces, feat = cotangent.shape
    vmem = pl.BlockSpec(memory_space=pltpu.VMEM)
    return pl.pallas_call(
        hidden_kernel,
        out_shape=jax.ShapeDtypeStruct((pieces, feat), jnp.bfloat16),
        in_specs=[vmem] * 4,
        out_specs=vmem,
        compiler_params=pltpu.CompilerParams(vmem_limit_bytes=LIMIT),
        name="hidden_step",
    )(weight, bias.reshape(1, feat), cotangent, aggregate)


def sum_of(refs):
    total = refs[0][...].astype(jnp.float32)
    for ref in refs[1:]:
        total += ref[...].astype(jnp.float32)
    return total


def backward_kernel(feat, kinds, chunks, begun, block_ref, *refs):
    sources, out_ref = refs[: len(kinds)], refs[-1]
    terms = refs[len(kinds) + begun : -1]
    pieces = out_ref.shape[1]
    me_row = lax.axis_index("row")
    me_col = lax.axis_index("col")
    for m, chunk in enumerate(chunks):
        across = pl.ds(pl.multiple_of((me_row ^ chunk) * pieces, pieces), pieces)
        if begun:
            total = refs[len(kinds)][chunk * feat : (chunk + 1) * feat, :]
        else:
            total = jnp.zeros((feat, pieces), jnp.float32)
        for k, source in zip(kinds, sources):
            down = pl.ds(pl.multiple_of((me_col ^ k) * pieces, pieces), pieces)
            total += jnp.dot(
                source[:feat, :], block_ref[down, across], preferred_element_type=jnp.float32
            )
        out_ref[m * feat : (m + 1) * feat, :] = total.astype(out_ref.dtype)
    if terms:
        out_ref[len(chunks) * feat :, :] = sum_of(terms).astype(out_ref.dtype)


def backward_parts(block, sources, kinds, chunks, begun, terms, name):
    feat, pieces = sources[0].shape
    begun = [] if begun is None else [begun]
    extra = terms[0].shape[0] if terms else 0
    vmem = pl.BlockSpec(memory_space=pltpu.VMEM)
    dtype = jnp.bfloat16 if begun else jnp.float32
    return pl.pallas_call(
        functools.partial(backward_kernel, feat, kinds, chunks, len(begun)),
        out_shape=jax.ShapeDtypeStruct((len(chunks) * feat + extra, pieces), dtype),
        in_specs=[vmem] * (1 + len(kinds) + len(begun) + len(terms)),
        out_specs=vmem,
        compiler_params=pltpu.CompilerParams(vmem_limit_bytes=LIMIT),
        name=name,
    )(block, *(sources[k] for k in kinds), *begun, *terms)


def pair_kernel(n, mine_ref, sent_ref, theirs_ref, *outs):
    feat = mine_ref.shape[0] // n
    terms = (
        sent_ref[n * feat :, :].astype(jnp.float32) + theirs_ref[n * feat :, :].astype(jnp.float32)
    ).astype(jnp.bfloat16)
    for m in range(n):
        span = slice(m * feat, (m + 1) * feat)
        outs[m][:feat, :] = (
            mine_ref[span, :].astype(jnp.float32) + theirs_ref[span, :].astype(jnp.float32)
        ).astype(jnp.bfloat16)
        outs[m][feat:, :] = terms


def pair_sum(mine, sent, theirs, n):
    rows, width = mine.shape
    vmem = pl.BlockSpec(memory_space=pltpu.VMEM)
    chunk = rows // n + sent.shape[0] - rows
    return pl.pallas_call(
        functools.partial(pair_kernel, n),
        out_shape=[jax.ShapeDtypeStruct((chunk, width), jnp.bfloat16)] * n,
        in_specs=[vmem] * 3,
        out_specs=[vmem] * n,
        compiler_params=pltpu.CompilerParams(vmem_limit_bytes=LIMIT),
        name="pair_sum",
    )(mine, sent, theirs)


def finish_kernel(scale, degree_ref, *refs):
    parts = refs[:-3]
    out_ref, weight_ref, bias_ref = refs[-3:]
    inv_row = lax.rsqrt(degree_ref[...].astype(jnp.float32))
    total = sum_of(parts)
    feat = weight_ref.shape[0]
    half = feat // 2
    out_ref[...] = (inv_row * total[:feat]).T.astype(jnp.bfloat16)
    weight_ref[:half, :] = total[feat : feat + half, :feat] * scale
    weight_ref[half:, :] = total[feat : feat + half, feat:] * scale
    bias_ref[...] = total[feat + half : feat + half + 1, :feat] * scale


def finish(degree, parts, feat, scale):
    pieces = parts[0].shape[1]
    vmem = pl.BlockSpec(memory_space=pltpu.VMEM)
    grad_features, grad_weight, grad_bias = pl.pallas_call(
        functools.partial(finish_kernel, scale),
        out_shape=[
            jax.ShapeDtypeStruct((pieces, feat), jnp.bfloat16),
            jax.ShapeDtypeStruct((feat, feat), jnp.float32),
            jax.ShapeDtypeStruct((1, feat), jnp.float32),
        ],
        in_specs=[vmem] * (1 + len(parts)),
        out_specs=[vmem] * 3,
        compiler_params=pltpu.CompilerParams(vmem_limit_bytes=LIMIT),
        name="finish",
    )(degree.reshape(1, pieces), *parts)
    return grad_features, grad_weight, grad_bias.reshape(feat)


def scale_kernel(
    degree_hbm, features_hbm, rows_hbm, cols_hbm, codes_hbm, out_ref, lists_ref, codes_ref,
    degree_ref, features_ref, sems
):
    slots = codes_ref.shape[0]
    first, second, *others = fetch(
        (degree_hbm, features_hbm, rows_hbm.at[0], cols_hbm.at[0], codes_hbm),
        (
            degree_ref,
            features_ref,
            lists_ref.at[0:1, 0:slots],
            lists_ref.at[1:2, 0:slots],
            codes_ref,
        ),
        sems,
    )
    first.wait()
    inv_root = column_of(lax.rsqrt(degree_ref[...].astype(jnp.float32)))
    second.wait()
    out_ref[...] = (inv_root * features_ref[...].astype(jnp.float32)).astype(jnp.bfloat16)
    for copy in others:
        copy.wait()


def scale_rows(degree, features, tile_rows, tile_cols, codes):
    pieces, feat = features.shape
    return pl.pallas_call(
        scale_kernel,
        out_shape=[
            pltpu.VMEM(features.shape, jnp.bfloat16),
            pltpu.VMEM((8, codes.shape[0]), jnp.int32),
            pltpu.VMEM(codes.shape, codes.dtype),
        ],
        in_specs=[pl.BlockSpec(memory_space=pl.ANY)] * 5,
        out_specs=[pl.BlockSpec(memory_space=pltpu.VMEM)] * 3,
        scratch_shapes=[
            pltpu.VMEM((1, pieces), jnp.int32),
            pltpu.VMEM((pieces, feat), jnp.bfloat16),
            pltpu.SemaphoreType.DMA((5,)),
        ],
        compiler_params=pltpu.CompilerParams(vmem_limit_bytes=60 * 2**20),
        name="scale_rows",
    )(degree.reshape(1, pieces), features, tile_rows, tile_cols, codes)


def terms_kernel(skip, *refs):
    *parts, out_ref = refs
    total = parts[0][skip:, :].astype(jnp.float32)
    for part in parts[1:]:
        total += part[skip:, :].astype(jnp.float32)
    out_ref[...] = total.astype(jnp.bfloat16)


def terms_sum(parts, skip, name):
    rows, width = parts[0].shape
    vmem = pl.BlockSpec(memory_space=pltpu.VMEM)
    return pl.pallas_call(
        functools.partial(terms_kernel, skip),
        out_shape=jax.ShapeDtypeStruct((rows - skip, width), jnp.bfloat16),
        in_specs=[vmem] * len(parts),
        out_specs=vmem,
        compiler_params=pltpu.CompilerParams(vmem_limit_bytes=LIMIT),
        name=name,
    )(*parts)


def dense_local(
    features, degree, weight, bias, cotangent, tile_rows, tile_cols, tile_count, tile_codes
):
    pieces, feat = features.shape
    n_row = lax.axis_size("row")
    n_col = lax.axis_size("col")
    grad_scale = 1.0 / math.sqrt(pieces * n_row * n_col)
    scaled, lists, codes = scale_rows(
        degree, features, tile_rows, tile_cols, tile_codes[0, 0]
    )
    chips = list(range(2, n_row, 2))
    lines = list(range(n_col - 1, 0, -1))
    own = [scaled] + [swap(scaled, "row", m) for m in chips]
    other = [swap(scaled, "row", 1)]
    slots = codes.shape[0]
    middle = slots * 3 // 4 // GROUP * GROUP
    size = (pieces * n_col, pieces * n_row)
    block = build_block(lists, tile_count, codes, *size, 0, middle)
    block, own = lax.optimization_barrier((block, own))
    if chips:
        other.append(swap(stack(own[1:]), "row", 1))
    block = build_block(lists, tile_count, codes, *size, middle, slots, block)
    half = max(1, n_col // 2)
    far = forward_parts(block, own, other, n_row, lines[:half], "forward_far")
    near = forward_parts(block, own, other, n_row, lines[half:] + [0], "forward_near")
    parts = dict(zip(lines + [0], far + near))
    landed = [parts[0]] + [swap(parts[k], "col", k) for k in lines]
    grad_own, both, aggregate = gradient_step(degree, weight, bias, cotangent, landed)
    grads = [grad_own, swap(both, "col", 1)] + [swap(grad_own, "col", k) for k in range(2, n_col)]
    grads[1], aggregate = lax.optimization_barrier((grads[1], aggregate))
    hidden = hidden_step(weight, bias, cotangent, aggregate)
    terms = [terms_sum([both, grads[1]], feat, "terms_col")]
    terms += [swap(terms[0], "col", k) for k in range(2, n_col, 2)]
    begun = backward_parts(block, grads, [0, 1], range(n_row), None, [], "backward_near")
    grads[2:], begun, terms = lax.optimization_barrier((grads[2:], begun, terms))
    far = range(2, n_col)
    for_other = backward_parts(
        block, grads, far, range(1, n_row, 2), begun, terms, "backward_other"
    )
    from_other = swap(for_other, "row", 1)
    for_own = backward_parts(block, grads, far, range(0, n_row, 2), begun, [], "backward_own")
    chunks = pair_sum(for_own, for_other, from_other, n_row // 2)
    landed = [chunks[0]] + [swap(chunks[m // 2], "row", m) for m in chips[::-1]]
    grad_features, grad_weight, grad_bias = finish(degree, landed, feat, grad_scale)
    return (hidden, grad_features, grad_weight, grad_bias)


def power_of_two(n):
    return n & (n - 1) == 0


def solution(mesh):
    placed = (
        P(("row", "col"), None),
        P(("row", "col")),
        P(),
        P(),
        P(("row", "col"), None),
        P("row", "col", None),
        P("row", "col", None),
        P("row", "col", None),
        P("row", "col", None, None),
    )
    n_row, n_col = mesh.shape["row"], mesh.shape["col"]

    def local(features, *rest):
        block_bytes = 2 * features.shape[0] ** 2 * n_row * n_col
        paired = power_of_two(n_row) and power_of_two(n_col) and n_row > 1 and n_col > 2
        if paired and block_bytes <= DENSE_BYTES:
            return dense_local(features, *rest)
        return sparse_local(features, *rest)

    return jax.shard_map(
        local,
        mesh=mesh,
        in_specs=placed,
        out_specs=(P(("row", "col"), None), P(("row", "col"), None), P(), P()),
        check_vma=False,
    )
```

```python
import functools
import math

import jax
import jax.numpy as jnp
from jax import lax
from jax.experimental import pallas as pl
from jax.experimental.pallas import tpu as pltpu
from jax.sharding import PartitionSpec as P

BLOCK = 16
GROUP = 32
MOD = 4093
HIT = 64
DENSE_BYTES = 8 * 2**20
LIMIT = 16 * 2**20


def tile_mask(code_block, living):
    tile_side = code_block.shape[1] // 2
    row_code = code_block[:, :tile_side][:, :, None]
    col_code = code_block[:, tile_side:][:, None, :]
    hashed = (row_code * col_code + row_code + 3 * col_code) % MOD
    return ((hashed < HIT) & living[:, None, None]).astype(jnp.bfloat16)


def accumulate(codes_dev, rows_dev, cols_dev, count_dev, source, out_tiles, backward):
    tile_side = source.shape[1]
    width_feat = source.shape[2]

    def block_step(block_id, summed):
        slot_start = block_id * BLOCK
        code_block = lax.dynamic_slice_in_dim(codes_dev, slot_start, BLOCK, 0)
        row_block = lax.dynamic_slice_in_dim(rows_dev, slot_start, BLOCK, 0)
        col_block = lax.dynamic_slice_in_dim(cols_dev, slot_start, BLOCK, 0)
        slot_ids = slot_start + jnp.arange(BLOCK, dtype=jnp.int32)
        target = col_block if backward else row_block
        anchor = row_block if backward else col_block
        living = slot_ids < count_dev
        keep = tile_mask(code_block, living)
        picked = jnp.take(source, anchor, axis=0)
        if backward:
            product = jnp.einsum("tij,tif->tjf", keep, picked, preferred_element_type=jnp.float32)
        else:
            product = jnp.einsum("tij,tjf->tif", keep, picked, preferred_element_type=jnp.float32)
        return summed.at[target].add(product)

    start_sum = jnp.zeros((out_tiles, tile_side, width_feat), jnp.float32)
    loop_count = codes_dev.shape[0] // BLOCK
    summed = lax.fori_loop(0, loop_count, block_step, start_sum)
    return summed.reshape(out_tiles * tile_side, width_feat)


def dense_part(aggregate, weight, bias, cotangent, inv_root):
    preact = jnp.dot(aggregate, weight, preferred_element_type=jnp.float32) + bias
    hidden = jax.nn.elu(preact).astype(jnp.bfloat16)
    elu_slope = jnp.where(preact > 0, 1.0, jnp.exp(jnp.minimum(preact, 0.0)))
    grad_pre = cotangent.astype(jnp.float32) * elu_slope
    grad_pre_b = grad_pre.astype(jnp.bfloat16)
    grad_weight = lax.dot_general(
        aggregate, grad_pre_b, (((0,), (0,)), ((), ())), preferred_element_type=jnp.float32
    )
    grad_bias = jnp.sum(grad_pre, axis=0)
    grad_agg = jnp.dot(grad_pre_b, weight.T, preferred_element_type=jnp.float32)
    grad_scaled = (inv_root * grad_agg).astype(jnp.bfloat16)
    return (hidden, grad_weight, grad_bias, grad_scaled)


def sparse_local(
    features, degree, weight, bias, cotangent, tile_rows, tile_cols, tile_count, tile_codes
):
    codes_dev = tile_codes[0, 0]
    rows_dev = tile_rows[0, 0]
    cols_dev = tile_cols[0, 0]
    count_dev = tile_count[0, 0, 0]
    pieces = features.shape[0]
    width_feat = features.shape[1]
    tile_side = codes_dev.shape[1] // 2
    row_devs = lax.axis_size("row")
    col_devs = lax.axis_size("col")
    grad_scale = 1.0 / math.sqrt(pieces * row_devs * col_devs)
    row_tiles = pieces * col_devs // tile_side
    col_tiles = pieces * row_devs // tile_side
    inv_root = lax.rsqrt(degree.astype(jnp.float32))[:, None]
    scaled = (inv_root * features.astype(jnp.float32)).astype(jnp.bfloat16)
    column_feats = lax.all_gather(scaled, "row", axis=0, tiled=True).reshape(
        col_tiles, tile_side, width_feat
    )
    row_terms = accumulate(codes_dev, rows_dev, cols_dev, count_dev, column_feats, row_tiles, False)
    row_sum = lax.psum_scatter(
        row_terms.astype(jnp.bfloat16), "col", scatter_dimension=0, tiled=True
    ).astype(jnp.float32)
    aggregate = (inv_root * row_sum).astype(jnp.bfloat16)
    hidden, grad_weight, grad_bias, grads = dense_part(
        aggregate, weight, bias, cotangent, inv_root
    )
    grad_weight, grad_bias = (
        lax.psum((grad_weight * grad_scale).astype(jnp.bfloat16), ("row", "col")),
        lax.psum((grad_bias * grad_scale).astype(jnp.bfloat16), ("row", "col")),
    )
    row_sources = lax.all_gather(grads, "col", axis=0, tiled=True).reshape(
        row_tiles, tile_side, width_feat
    )
    col_terms = accumulate(codes_dev, rows_dev, cols_dev, count_dev, row_sources, col_tiles, True)
    grad_sum = lax.psum_scatter(
        col_terms.astype(jnp.bfloat16), "row", scatter_dimension=0, tiled=True
    ).astype(jnp.float32)
    grad_features = (inv_root * grad_sum).astype(jnp.bfloat16)
    return (
        hidden,
        grad_features,
        grad_weight.astype(jnp.float32),
        grad_bias.astype(jnp.float32),
    )


def swap(value, axis, bits):
    size = lax.axis_size(axis)
    return lax.ppermute(value, axis, [(i, i ^ bits) for i in range(size)])


def column_of(row):
    n = row.shape[1]
    blocks = [
        jnp.broadcast_to(row[:, k : k + 128], (128, 128)).T for k in range(0, n, 128)
    ]
    return jnp.concatenate(blocks, axis=0)


def fetch(sources, targets, sems):
    copies = [
        pltpu.make_async_copy(src, dst, sems.at[k])
        for k, (src, dst) in enumerate(zip(sources, targets))
    ]
    for copy in copies:
        copy.start()
    return copies


def build_kernel(first, last, lists_vmem, count_ref, codes_ref, *refs):
    block_ref, row_scr, col_scr, lists_ref, sems = refs[-5:]
    slots = codes_ref.shape[0]
    side = codes_ref.shape[1] // 2
    (copy,) = fetch((lists_vmem,), (lists_ref,), sems)
    if first == 0:
        block_ref[...] = jnp.zeros_like(block_ref)
    row_code = codes_ref[:, :side].astype(jnp.float32) + 3.0
    row_code = jnp.where(row_code > MOD // 2, row_code - MOD, row_code)
    slot = lax.broadcasted_iota(jnp.int32, (slots, side), 0)
    row_code = jnp.where(slot < count_ref[0, 0, 0], row_code, 0.0)
    col_code = codes_ref[:, side:].astype(jnp.float32) + 1.0
    col_code = jnp.where(col_code > MOD // 2, col_code - MOD, col_code)
    coarse = 2.0**-12
    col_scr[...] = col_code * coarse + col_code * (1.0 / MOD - coarse)
    by_side = row_code.T
    groups = range(first // GROUP, last // GROUP)
    for g in groups:
        row_scr[g] = by_side if g == 0 else pltpu.roll(by_side, slots - g * GROUP, axis=1)
    copy.wait()
    middle = (3.0 + (HIT - 1) / 2.0) / MOD
    reach = jnp.bfloat16(2.0**-7)
    one, zero = jnp.bfloat16(1.0), jnp.bfloat16(0.0)

    def step(g, carry):
        row_vals = row_scr[g]
        col_vals = col_scr[pl.ds(pl.multiple_of(g * GROUP, GROUP), GROUP), :]
        for t in range(GROUP):
            s = g * GROUP + t
            turns = jnp.broadcast_to(row_vals[:, t : t + 1], (side, side)) * jnp.broadcast_to(
                col_vals[t : t + 1, :], (side, side)
            )
            part = turns - jnp.round(turns)
            keep = jnp.abs((part - middle).astype(jnp.bfloat16)) < reach
            down = pl.ds(pl.multiple_of(lists_ref[0, s] * side, side), side)
            across = pl.ds(pl.multiple_of(lists_ref[1, s] * side, side), side)
            block_ref[down, across] += jnp.where(keep, one, zero)
        return carry

    lax.fori_loop(groups.start, groups.stop, step, 0)


def build_block(lists, tile_count, codes, row_nodes, col_nodes, first, last, block=None):
    slots, width = codes.shape
    side = width // 2
    vmem = pl.BlockSpec(memory_space=pltpu.VMEM)
    begun = [] if block is None else [block]
    return pl.pallas_call(
        functools.partial(build_kernel, first, last),
        out_shape=pltpu.VMEM((row_nodes, col_nodes), jnp.bfloat16),
        in_specs=[vmem, pl.BlockSpec(memory_space=pltpu.SMEM), vmem] + [vmem] * len(begun),
        out_specs=vmem,
        input_output_aliases={3: 0} if begun else {},
        scratch_shapes=[
            pltpu.VMEM((slots // GROUP, side, slots), jnp.float32),
            pltpu.VMEM((slots, side), jnp.float32),
            pltpu.SMEM(lists.shape, jnp.int32),
            pltpu.SemaphoreType.DMA((1,)),
        ],
        compiler_params=pltpu.CompilerParams(vmem_limit_bytes=LIMIT),
        cost_estimate=pl.CostEstimate(
            flops=20 * (last - first) * side * side, bytes_accessed=2**23, transcendentals=0
        ),
        name="build_rest" if begun else "build_block",
    )(lists, tile_count, codes, *begun)


def stack_kernel(*refs):
    *parts, out_ref = refs
    rows = parts[0].shape[0]
    for m, part in enumerate(parts):
        out_ref[m * rows : (m + 1) * rows, :] = part[...]


def stack(parts):
    rows, width = parts[0].shape
    vmem = pl.BlockSpec(memory_space=pltpu.VMEM)
    return pl.pallas_call(
        stack_kernel,
        out_shape=jax.ShapeDtypeStruct((len(parts) * rows, width), parts[0].dtype),
        in_specs=[vmem] * len(parts),
        out_specs=vmem,
        compiler_params=pltpu.CompilerParams(vmem_limit_bytes=LIMIT),
        name="stack",
    )(*parts)


def forward_kernel(bits, high, block_ref, *refs):
    *parts, even_ref, odd_ref, source = refs
    pieces = parts[0].shape[0]
    me_row = lax.axis_index("row")
    me_col = lax.axis_index("col")
    place = iter(bits)
    for part in parts:
        for m in range(part.shape[0] // pieces):
            at = pl.multiple_of((me_row ^ next(place)) * pieces, pieces)
            source[pl.ds(at, pieces), :] = part[m * pieces : (m + 1) * pieces, :]
    down = pl.multiple_of((me_col ^ high) // 2 * (2 * pieces), 2 * pieces)
    both = jnp.dot(
        block_ref[pl.ds(down, 2 * pieces), :], source[...], preferred_element_type=jnp.float32
    ).astype(jnp.bfloat16)
    first = me_col % 2 == 0
    even_ref[...] = jnp.where(first, both[:pieces], both[pieces:])
    odd_ref[...] = jnp.where(first, both[pieces:], both[:pieces])


def forward_parts(block, parts, bits, high, name):
    pieces, feat = parts[0].shape
    vmem = pl.BlockSpec(memory_space=pltpu.VMEM)
    return pl.pallas_call(
        functools.partial(forward_kernel, bits, high),
        out_shape=[jax.ShapeDtypeStruct((pieces, feat), jnp.bfloat16)] * 2,
        in_specs=[vmem] * (1 + len(parts)),
        out_specs=[vmem] * 2,
        scratch_shapes=[pltpu.VMEM((pieces * len(bits), feat), jnp.bfloat16)],
        compiler_params=pltpu.CompilerParams(vmem_limit_bytes=LIMIT),
        name=name,
    )(block, *parts)


def slope_of(aggregate, weight, bias, cotangent):
    preact = jnp.dot(aggregate, weight, preferred_element_type=jnp.float32) + bias
    decay = jnp.exp(jnp.minimum(preact, 0.0))
    positive = preact > 0
    grad_pre = cotangent.astype(jnp.float32) * jnp.where(positive, 1.0, decay)
    return jnp.where(positive, preact, decay - 1.0), grad_pre


def gradient_kernel(n_col, degree_ref, weight_ref, bias_ref, cot_ref, *refs):
    parts = refs[:n_col]
    grad_ref, both_ref, aggregate_ref = refs[n_col:]
    total = parts[0][...].astype(jnp.float32)
    for k in range(1, n_col):
        total += parts[k][...].astype(jnp.float32)
    inv_row = lax.rsqrt(degree_ref[...].astype(jnp.float32))
    aggregate = (column_of(inv_row) * total).astype(jnp.bfloat16)
    aggregate_ref[...] = aggregate
    weight = weight_ref[...]
    feat = weight.shape[0]
    half = feat // 2
    _, grad_pre = slope_of(aggregate, weight, bias_ref[...], cot_ref[...])
    grad_pre_b = grad_pre.astype(jnp.bfloat16)
    back = lax.dot_general(
        weight, grad_pre_b, (((1,), (1,)), ((), ())), preferred_element_type=jnp.float32
    )
    grad = (inv_row * back).astype(jnp.bfloat16)
    grad_ref[...] = grad
    both_ref[:feat, :] = grad
    weight_terms = lax.dot_general(
        aggregate, grad_pre_b, (((0,), (0,)), ((), ())), preferred_element_type=jnp.float32
    ).astype(jnp.bfloat16)
    both_ref[feat : feat + half, :feat] = weight_terms[:half]
    both_ref[feat : feat + half, feat:] = weight_terms[half:]
    bias_terms = jnp.sum(grad_pre, axis=0, keepdims=True)
    bias_terms = jnp.broadcast_to(bias_terms, (16, feat)).astype(jnp.bfloat16)
    both_ref[feat + half :, :feat] = bias_terms
    both_ref[feat + half :, feat:] = bias_terms


def gradient_step(degree, weight, bias, cotangent, parts):
    pieces, feat = cotangent.shape
    vmem = pl.BlockSpec(memory_space=pltpu.VMEM)
    return pl.pallas_call(
        functools.partial(gradient_kernel, len(parts)),
        out_shape=[
            jax.ShapeDtypeStruct((feat, pieces), jnp.bfloat16),
            jax.ShapeDtypeStruct((feat + feat // 2 + 16, pieces), jnp.bfloat16),
            jax.ShapeDtypeStruct((pieces, feat), jnp.bfloat16),
        ],
        in_specs=[vmem] * (4 + len(parts)),
        out_specs=[vmem] * 3,
        compiler_params=pltpu.CompilerParams(vmem_limit_bytes=LIMIT),
        name="gradient_step",
    )(degree.reshape(1, pieces), weight, bias.reshape(1, feat), cotangent, *parts)


def hidden_kernel(weight_ref, bias_ref, cot_ref, aggregate_ref, hidden_ref):
    hidden, _ = slope_of(aggregate_ref[...], weight_ref[...], bias_ref[...], cot_ref[...])
    hidden_ref[...] = hidden.astype(jnp.bfloat16)


def hidden_step(weight, bias, cotangent, aggregate):
    pieces, feat = cotangent.shape
    vmem = pl.BlockSpec(memory_space=pltpu.VMEM)
    return pl.pallas_call(
        hidden_kernel,
        out_shape=jax.ShapeDtypeStruct((pieces, feat), jnp.bfloat16),
        in_specs=[vmem] * 4,
        out_specs=vmem,
        compiler_params=pltpu.CompilerParams(vmem_limit_bytes=LIMIT),
        name="hidden_step",
    )(weight, bias.reshape(1, feat), cotangent, aggregate)


def sum_of(refs):
    total = refs[0][...].astype(jnp.float32)
    for ref in refs[1:]:
        total += ref[...].astype(jnp.float32)
    return total


def backward_kernel(feat, kinds, chunks, begun, block_ref, *refs):
    sources, out_ref = refs[: len(kinds)], refs[-1]
    terms = refs[len(kinds) + begun : -1]
    pieces = out_ref.shape[1]
    me_row = lax.axis_index("row")
    me_col = lax.axis_index("col")
    for m, chunk in enumerate(chunks):
        across = pl.ds(pl.multiple_of((me_row ^ chunk) * pieces, pieces), pieces)
        if begun:
            total = refs[len(kinds)][chunk * feat : (chunk + 1) * feat, :]
        else:
            total = jnp.zeros((feat, pieces), jnp.float32)
        for k, source in zip(kinds, sources):
            down = pl.ds(pl.multiple_of((me_col ^ k) * pieces, pieces), pieces)
            total += jnp.dot(
                source[:feat, :], block_ref[down, across], preferred_element_type=jnp.float32
            )
        out_ref[m * feat : (m + 1) * feat, :] = total.astype(out_ref.dtype)
    if terms:
        out_ref[len(chunks) * feat :, :] = sum_of(terms).astype(out_ref.dtype)


def backward_parts(block, sources, kinds, chunks, begun, terms, name):
    feat, pieces = sources[0].shape
    begun = [] if begun is None else [begun]
    extra = terms[0].shape[0] if terms else 0
    vmem = pl.BlockSpec(memory_space=pltpu.VMEM)
    dtype = jnp.bfloat16 if begun else jnp.float32
    return pl.pallas_call(
        functools.partial(backward_kernel, feat, kinds, chunks, len(begun)),
        out_shape=jax.ShapeDtypeStruct((len(chunks) * feat + extra, pieces), dtype),
        in_specs=[vmem] * (1 + len(kinds) + len(begun) + len(terms)),
        out_specs=vmem,
        compiler_params=pltpu.CompilerParams(vmem_limit_bytes=LIMIT),
        name=name,
    )(block, *(sources[k] for k in kinds), *begun, *terms)


def pair_kernel(first, mine_ref, theirs_ref, sent_ref, got_ref, *outs):
    feat = mine_ref.shape[0] // 4
    terms = sum_of((sent_ref.at[2 * feat :], got_ref.at[2 * feat :])).astype(jnp.bfloat16)
    for m, out in enumerate(outs):
        mine = mine_ref[(first + m) * feat : (first + m + 1) * feat, :].astype(jnp.float32)
        theirs = theirs_ref[m * feat : (m + 1) * feat, :].astype(jnp.float32)
        out[:feat, :] = (mine + theirs).astype(jnp.bfloat16)
        out[feat:, :] = terms


def pair_sum(first, mine, theirs, sent, got):
    vmem = pl.BlockSpec(memory_space=pltpu.VMEM)
    rows = sent.shape[0] - mine.shape[0] // 4
    return pl.pallas_call(
        functools.partial(pair_kernel, first),
        out_shape=[jax.ShapeDtypeStruct((rows, mine.shape[1]), jnp.bfloat16)] * 2,
        in_specs=[vmem] * 4,
        out_specs=[vmem] * 2,
        compiler_params=pltpu.CompilerParams(vmem_limit_bytes=LIMIT),
        name="pair_near" if first else "pair_far",
    )(mine, theirs, sent, got)


def finish_kernel(scale, degree_ref, *refs):
    parts = refs[:-3]
    out_ref, weight_ref, bias_ref = refs[-3:]
    inv_row = lax.rsqrt(degree_ref[...].astype(jnp.float32))
    total = sum_of(parts)
    feat = weight_ref.shape[0]
    half = feat // 2
    out_ref[...] = (inv_row * total[:feat]).T.astype(jnp.bfloat16)
    weight_ref[:half, :] = total[feat : feat + half, :feat] * scale
    weight_ref[half:, :] = total[feat : feat + half, feat:] * scale
    bias_ref[...] = total[feat + half : feat + half + 1, :feat] * scale


def finish(degree, parts, feat, scale):
    pieces = parts[0].shape[1]
    vmem = pl.BlockSpec(memory_space=pltpu.VMEM)
    grad_features, grad_weight, grad_bias = pl.pallas_call(
        functools.partial(finish_kernel, scale),
        out_shape=[
            jax.ShapeDtypeStruct((pieces, feat), jnp.bfloat16),
            jax.ShapeDtypeStruct((feat, feat), jnp.float32),
            jax.ShapeDtypeStruct((1, feat), jnp.float32),
        ],
        in_specs=[vmem] * (1 + len(parts)),
        out_specs=[vmem] * 3,
        compiler_params=pltpu.CompilerParams(vmem_limit_bytes=LIMIT),
        name="finish",
    )(degree.reshape(1, pieces), *parts)
    return grad_features, grad_weight, grad_bias.reshape(feat)


def scale_kernel(
    degree_hbm, features_hbm, rows_hbm, cols_hbm, codes_hbm, out_ref, lists_ref, codes_ref,
    degree_ref, features_ref, sems
):
    slots = codes_ref.shape[0]
    first, second, *others = fetch(
        (degree_hbm, features_hbm, rows_hbm.at[0], cols_hbm.at[0], codes_hbm),
        (
            degree_ref,
            features_ref,
            lists_ref.at[0:1, 0:slots],
            lists_ref.at[1:2, 0:slots],
            codes_ref,
        ),
        sems,
    )
    first.wait()
    inv_root = column_of(lax.rsqrt(degree_ref[...].astype(jnp.float32)))
    second.wait()
    out_ref[...] = (inv_root * features_ref[...].astype(jnp.float32)).astype(jnp.bfloat16)
    for copy in others:
        copy.wait()


def scale_rows(degree, features, tile_rows, tile_cols, codes):
    pieces, feat = features.shape
    return pl.pallas_call(
        scale_kernel,
        out_shape=[
            pltpu.VMEM(features.shape, jnp.bfloat16),
            pltpu.VMEM((8, codes.shape[0]), jnp.int32),
            pltpu.VMEM(codes.shape, codes.dtype),
        ],
        in_specs=[pl.BlockSpec(memory_space=pl.ANY)] * 5,
        out_specs=[pl.BlockSpec(memory_space=pltpu.VMEM)] * 3,
        scratch_shapes=[
            pltpu.VMEM((1, pieces), jnp.int32),
            pltpu.VMEM((pieces, feat), jnp.bfloat16),
            pltpu.SemaphoreType.DMA((5,)),
        ],
        compiler_params=pltpu.CompilerParams(vmem_limit_bytes=60 * 2**20),
        name="scale_rows",
    )(degree.reshape(1, pieces), features, tile_rows, tile_cols, codes)


def terms_kernel(skip, *refs):
    *parts, out_ref = refs
    total = parts[0][skip:, :].astype(jnp.float32)
    for part in parts[1:]:
        total += part[skip:, :].astype(jnp.float32)
    out_ref[...] = total.astype(jnp.bfloat16)


def terms_sum(parts, skip, name):
    rows, width = parts[0].shape
    vmem = pl.BlockSpec(memory_space=pltpu.VMEM)
    return pl.pallas_call(
        functools.partial(terms_kernel, skip),
        out_shape=jax.ShapeDtypeStruct((rows - skip, width), jnp.bfloat16),
        in_specs=[vmem] * len(parts),
        out_specs=vmem,
        compiler_params=pltpu.CompilerParams(vmem_limit_bytes=LIMIT),
        name=name,
    )(*parts)


def dense_local(
    features, degree, weight, bias, cotangent, tile_rows, tile_cols, tile_count, tile_codes
):
    pieces, feat = features.shape
    n_row = lax.axis_size("row")
    n_col = lax.axis_size("col")
    grad_scale = 1.0 / math.sqrt(pieces * n_row * n_col)
    scaled, lists, codes = scale_rows(
        degree, features, tile_rows, tile_cols, tile_codes[0, 0]
    )
    chips = [6, 4, 2]
    lines = list(range(n_col - 1, 0, -1))
    landed = [swap(scaled, "row", m) for m in chips]
    sibling = swap(scaled, "row", 1)
    slots = codes.shape[0]
    middle = slots * 3 // 4 // GROUP * GROUP
    size = (pieces * n_col, pieces * n_row)
    block = build_block(lists, tile_count, codes, *size, 0, middle)
    block, landed = lax.optimization_barrier((block, landed))
    parts = [scaled, sibling, *landed, swap(stack(landed), "row", 1)]
    bits = [0, 1, *chips, *(m + 1 for m in chips)]
    block = build_block(lists, tile_count, codes, *size, middle, slots, block)
    far = forward_parts(block, parts, bits, 2, "forward_far")
    near = forward_parts(block, parts, bits, 0, "forward_near")
    parts = [*near, *far]
    landed = [parts[0]] + [swap(parts[k], "col", k) for k in lines]
    grad_own, both, aggregate = gradient_step(degree, weight, bias, cotangent, landed)
    grads = [grad_own, swap(both, "col", 1)] + [swap(grad_own, "col", k) for k in range(2, n_col)]
    grads[1], aggregate = lax.optimization_barrier((grads[1], aggregate))
    hidden = hidden_step(weight, bias, cotangent, aggregate)
    terms = [terms_sum([both, grads[1]], feat, "terms_col")]
    terms += [swap(terms[0], "col", k) for k in range(2, n_col, 2)]
    begun = backward_parts(block, grads, [0, 1], range(n_row), None, [], "backward_near")
    grads[2:], begun, terms = lax.optimization_barrier((grads[2:], begun, terms))
    far = range(2, n_col)
    sent = backward_parts(block, grads, far, [7, 5], begun, terms, "backward_other")
    got = swap(sent, "row", 1)
    rest = swap(backward_parts(block, grads, far, [3, 1], begun, [], "backward_rest"), "row", 1)
    mine = backward_parts(block, grads, far, [6, 4, 2, 0], begun, [], "backward_own")
    chunks = pair_sum(0, mine, got, sent, got)
    landed = [swap(chunk, "row", m) for chunk, m in zip(chunks, chips)]
    chunks = pair_sum(2, mine, rest, sent, got)
    landed = [chunks[1], *landed, swap(chunks[0], "row", chips[2])]
    grad_features, grad_weight, grad_bias = finish(degree, landed, feat, grad_scale)
    return (hidden, grad_features, grad_weight, grad_bias)


def solution(mesh):
    placed = (
        P(("row", "col"), None),
        P(("row", "col")),
        P(),
        P(),
        P(("row", "col"), None),
        P("row", "col", None),
        P("row", "col", None),
        P("row", "col", None),
        P("row", "col", None, None),
    )
    n_row, n_col = mesh.shape["row"], mesh.shape["col"]

    def local(features, *rest):
        block_bytes = 2 * features.shape[0] ** 2 * n_row * n_col
        paired = n_row == 8 and n_col == 4
        if paired and block_bytes <= DENSE_BYTES:
            return dense_local(features, *rest)
        return sparse_local(features, *rest)

    return jax.shard_map(
        local,
        mesh=mesh,
        in_specs=placed,
        out_specs=(P(("row", "col"), None), P(("row", "col"), None), P(), P()),
        check_vma=False,
    )
```

```python
import functools
import math

import jax
import jax.numpy as jnp
from jax import lax
from jax.experimental import pallas as pl
from jax.experimental.pallas import tpu as pltpu
from jax.sharding import PartitionSpec as P

BLOCK = 16
GROUP = 32
MOD = 4093
HIT = 64
DENSE_BYTES = 8 * 2**20
LIMIT = 16 * 2**20


def tile_mask(code_block, living):
    tile_side = code_block.shape[1] // 2
    row_code = code_block[:, :tile_side][:, :, None]
    col_code = code_block[:, tile_side:][:, None, :]
    hashed = (row_code * col_code + row_code + 3 * col_code) % MOD
    return ((hashed < HIT) & living[:, None, None]).astype(jnp.bfloat16)


def accumulate(codes_dev, rows_dev, cols_dev, count_dev, source, out_tiles, backward):
    tile_side = source.shape[1]
    width_feat = source.shape[2]

    def block_step(block_id, summed):
        slot_start = block_id * BLOCK
        code_block = lax.dynamic_slice_in_dim(codes_dev, slot_start, BLOCK, 0)
        row_block = lax.dynamic_slice_in_dim(rows_dev, slot_start, BLOCK, 0)
        col_block = lax.dynamic_slice_in_dim(cols_dev, slot_start, BLOCK, 0)
        slot_ids = slot_start + jnp.arange(BLOCK, dtype=jnp.int32)
        target = col_block if backward else row_block
        anchor = row_block if backward else col_block
        living = slot_ids < count_dev
        keep = tile_mask(code_block, living)
        picked = jnp.take(source, anchor, axis=0)
        if backward:
            product = jnp.einsum("tij,tif->tjf", keep, picked, preferred_element_type=jnp.float32)
        else:
            product = jnp.einsum("tij,tjf->tif", keep, picked, preferred_element_type=jnp.float32)
        return summed.at[target].add(product)

    start_sum = jnp.zeros((out_tiles, tile_side, width_feat), jnp.float32)
    loop_count = codes_dev.shape[0] // BLOCK
    summed = lax.fori_loop(0, loop_count, block_step, start_sum)
    return summed.reshape(out_tiles * tile_side, width_feat)


def dense_part(aggregate, weight, bias, cotangent, inv_root):
    preact = jnp.dot(aggregate, weight, preferred_element_type=jnp.float32) + bias
    hidden = jax.nn.elu(preact).astype(jnp.bfloat16)
    elu_slope = jnp.where(preact > 0, 1.0, jnp.exp(jnp.minimum(preact, 0.0)))
    grad_pre = cotangent.astype(jnp.float32) * elu_slope
    grad_pre_b = grad_pre.astype(jnp.bfloat16)
    grad_weight = lax.dot_general(
        aggregate, grad_pre_b, (((0,), (0,)), ((), ())), preferred_element_type=jnp.float32
    )
    grad_bias = jnp.sum(grad_pre, axis=0)
    grad_agg = jnp.dot(grad_pre_b, weight.T, preferred_element_type=jnp.float32)
    grad_scaled = (inv_root * grad_agg).astype(jnp.bfloat16)
    return (hidden, grad_weight, grad_bias, grad_scaled)


def sparse_local(
    features, degree, weight, bias, cotangent, tile_rows, tile_cols, tile_count, tile_codes
):
    codes_dev = tile_codes[0, 0]
    rows_dev = tile_rows[0, 0]
    cols_dev = tile_cols[0, 0]
    count_dev = tile_count[0, 0, 0]
    pieces = features.shape[0]
    width_feat = features.shape[1]
    tile_side = codes_dev.shape[1] // 2
    row_devs = lax.axis_size("row")
    col_devs = lax.axis_size("col")
    grad_scale = 1.0 / math.sqrt(pieces * row_devs * col_devs)
    row_tiles = pieces * col_devs // tile_side
    col_tiles = pieces * row_devs // tile_side
    inv_root = lax.rsqrt(degree.astype(jnp.float32))[:, None]
    scaled = (inv_root * features.astype(jnp.float32)).astype(jnp.bfloat16)
    column_feats = lax.all_gather(scaled, "row", axis=0, tiled=True).reshape(
        col_tiles, tile_side, width_feat
    )
    row_terms = accumulate(codes_dev, rows_dev, cols_dev, count_dev, column_feats, row_tiles, False)
    row_sum = lax.psum_scatter(
        row_terms.astype(jnp.bfloat16), "col", scatter_dimension=0, tiled=True
    ).astype(jnp.float32)
    aggregate = (inv_root * row_sum).astype(jnp.bfloat16)
    hidden, grad_weight, grad_bias, grads = dense_part(
        aggregate, weight, bias, cotangent, inv_root
    )
    grad_weight, grad_bias = (
        lax.psum((grad_weight * grad_scale).astype(jnp.bfloat16), ("row", "col")),
        lax.psum((grad_bias * grad_scale).astype(jnp.bfloat16), ("row", "col")),
    )
    row_sources = lax.all_gather(grads, "col", axis=0, tiled=True).reshape(
        row_tiles, tile_side, width_feat
    )
    col_terms = accumulate(codes_dev, rows_dev, cols_dev, count_dev, row_sources, col_tiles, True)
    grad_sum = lax.psum_scatter(
        col_terms.astype(jnp.bfloat16), "row", scatter_dimension=0, tiled=True
    ).astype(jnp.float32)
    grad_features = (inv_root * grad_sum).astype(jnp.bfloat16)
    return (
        hidden,
        grad_features,
        grad_weight.astype(jnp.float32),
        grad_bias.astype(jnp.float32),
    )


def swap(value, axis, bits):
    size = lax.axis_size(axis)
    return lax.ppermute(value, axis, [(i, i ^ bits) for i in range(size)])


def turned(lhs, rhs):
    return lax.dot_general(lhs, rhs, (((1,), (1,)), ((), ())), preferred_element_type=jnp.float32)


def fetch(sources, targets, sems):
    copies = [
        pltpu.make_async_copy(src, dst, sems.at[k])
        for k, (src, dst) in enumerate(zip(sources, targets))
    ]
    for copy in copies:
        copy.start()
    return copies


def build_kernel(first, last, lists_vmem, count_ref, codes_ref, *refs):
    block_ref, col_scr, row_scr, lists_ref, sems = refs[-5:]
    slots = codes_ref.shape[0]
    side = codes_ref.shape[1] // 2
    (copy,) = fetch((lists_vmem,), (lists_ref,), sems)
    if first == 0:
        block_ref[...] = jnp.zeros_like(block_ref)
    row_code = codes_ref[:, :side].astype(jnp.float32) + 3.0
    row_code = jnp.where(row_code > MOD // 2, row_code - MOD, row_code)
    col_code = codes_ref[:, side:].astype(jnp.float32) + 1.0
    col_code = jnp.where(col_code > MOD // 2, col_code - MOD, col_code)
    slot = lax.broadcasted_iota(jnp.int32, (slots, side), 0)
    col_code = jnp.where(slot < count_ref[0, 0, 0], col_code, 0.0)
    coarse = 2.0**-12
    row_scr[...] = row_code * coarse + row_code * (1.0 / MOD - coarse)
    by_side = col_code.T
    groups = range(first // GROUP, last // GROUP)
    for g in groups:
        col_scr[g] = by_side if g == 0 else pltpu.roll(by_side, slots - g * GROUP, axis=1)
    copy.wait()
    middle = (3.0 + (HIT - 1) / 2.0) / MOD
    reach = jnp.bfloat16(2.0**-7)
    one, zero = jnp.bfloat16(1.0), jnp.bfloat16(0.0)

    def step(g, carry):
        col_vals = col_scr[g]
        row_vals = row_scr[pl.ds(pl.multiple_of(g * GROUP, GROUP), GROUP), :]
        for t in range(GROUP):
            s = g * GROUP + t
            turns = jnp.broadcast_to(col_vals[:, t : t + 1], (side, side)) * jnp.broadcast_to(
                row_vals[t : t + 1, :], (side, side)
            )
            part = turns - jnp.round(turns)
            keep = jnp.abs((part - middle).astype(jnp.bfloat16)) < reach
            down = pl.ds(pl.multiple_of(lists_ref[1, s] * side, side), side)
            across = pl.ds(pl.multiple_of(lists_ref[0, s] * side, side), side)
            block_ref[down, across] += jnp.where(keep, one, zero)
        return carry

    lax.fori_loop(groups.start, groups.stop, step, 0)


def build_block(lists, tile_count, codes, row_nodes, col_nodes, first, last, block=None):
    slots, width = codes.shape
    side = width // 2
    vmem = pl.BlockSpec(memory_space=pltpu.VMEM)
    begun = [] if block is None else [block]
    return pl.pallas_call(
        functools.partial(build_kernel, first, last),
        out_shape=pltpu.VMEM((col_nodes, row_nodes), jnp.bfloat16),
        in_specs=[vmem, pl.BlockSpec(memory_space=pltpu.SMEM), vmem] + [vmem] * len(begun),
        out_specs=vmem,
        input_output_aliases={3: 0} if begun else {},
        scratch_shapes=[
            pltpu.VMEM((slots // GROUP, side, slots), jnp.float32),
            pltpu.VMEM((slots, side), jnp.float32),
            pltpu.SMEM(lists.shape, jnp.int32),
            pltpu.SemaphoreType.DMA((1,)),
        ],
        compiler_params=pltpu.CompilerParams(vmem_limit_bytes=LIMIT),
        cost_estimate=pl.CostEstimate(
            flops=20 * (last - first) * side * side, bytes_accessed=2**23, transcendentals=0
        ),
        name="build_rest" if begun else "build_block",
    )(lists, tile_count, codes, *begun)


def stack_kernel(*refs):
    *parts, out_ref = refs
    rows = parts[0].shape[0]
    for m, part in enumerate(parts):
        out_ref[m * rows : (m + 1) * rows, :] = part[...]


def stack(parts):
    rows, width = parts[0].shape
    vmem = pl.BlockSpec(memory_space=pltpu.VMEM)
    return pl.pallas_call(
        stack_kernel,
        out_shape=jax.ShapeDtypeStruct((len(parts) * rows, width), parts[0].dtype),
        in_specs=[vmem] * len(parts),
        out_specs=vmem,
        compiler_params=pltpu.CompilerParams(vmem_limit_bytes=LIMIT),
        name="stack",
    )(*parts)


def forward_kernel(bits, far, block_ref, *refs):
    outs = refs[len(refs) - len(far) :]
    parts = refs[: len(refs) - len(far)]
    feat, pieces = parts[0].shape
    me_row = lax.axis_index("row")
    me_col = lax.axis_index("col")
    for out, k in zip(outs, far):
        across = pl.ds(pl.multiple_of((me_col ^ k) * pieces, pieces), pieces)
        total = jnp.zeros((feat, pieces), jnp.float32)
        place = iter(bits)
        for part in parts:
            for m in range(part.shape[0] // feat):
                down = pl.ds(pl.multiple_of((me_row ^ next(place)) * pieces, pieces), pieces)
                total += jnp.dot(
                    part[m * feat : (m + 1) * feat, :],
                    block_ref[down, across],
                    preferred_element_type=jnp.float32,
                )
        out[...] = total.astype(jnp.bfloat16)


def forward_parts(block, parts, bits, far, name):
    feat, pieces = parts[0].shape
    vmem = pl.BlockSpec(memory_space=pltpu.VMEM)
    return pl.pallas_call(
        functools.partial(forward_kernel, bits, far),
        out_shape=[jax.ShapeDtypeStruct((feat, pieces), jnp.bfloat16)] * len(far),
        in_specs=[vmem] * (1 + len(parts)),
        out_specs=[vmem] * len(far),
        compiler_params=pltpu.CompilerParams(vmem_limit_bytes=LIMIT),
        name=name,
    )(block, *parts)


def turn_kernel(
    weight_ref, bias_ref, cot_ref, degree_ref, weight_out, bias_out, cot_out, root_out
):
    feat, pieces = cot_out.shape
    weight_out[...] = weight_ref[...].T
    bias_out[...] = jnp.broadcast_to(bias_ref[...], (feat, feat)).T
    cot_out[...] = cot_ref[...].T
    inv_row = lax.rsqrt(degree_ref[...].astype(jnp.float32))
    root_out[...] = jnp.broadcast_to(inv_row, (feat, pieces)).T


def turn(weight, bias, cotangent, degree):
    pieces, feat = cotangent.shape
    vmem = pl.BlockSpec(memory_space=pltpu.VMEM)
    return pl.pallas_call(
        turn_kernel,
        out_shape=[
            jax.ShapeDtypeStruct((feat, feat), jnp.bfloat16),
            jax.ShapeDtypeStruct((feat, feat), jnp.float32),
            jax.ShapeDtypeStruct((feat, pieces), jnp.bfloat16),
            jax.ShapeDtypeStruct((pieces, feat), jnp.float32),
        ],
        in_specs=[vmem] * 4,
        out_specs=[vmem] * 4,
        compiler_params=pltpu.CompilerParams(vmem_limit_bytes=LIMIT),
        name="turn",
    )(weight, bias.reshape(1, feat), cotangent, degree.reshape(1, pieces))


def preact_of(aggregate, weight_turned, bias_turned):
    repeats = aggregate.shape[1] // bias_turned.shape[1]
    bias = jnp.concatenate([bias_turned] * repeats, axis=1)
    return jnp.dot(weight_turned, aggregate, preferred_element_type=jnp.float32) + bias


def gradient_kernel(n_col, degree_ref, weight_ref, turned_ref, bias_ref, cot_ref, *refs):
    grad_ref, both_ref, aggregate_ref = refs[n_col:]
    inv_row = lax.rsqrt(degree_ref[...].astype(jnp.float32))
    aggregate = (inv_row * sum_of(refs[:n_col])).astype(jnp.bfloat16)
    aggregate_ref[...] = aggregate
    feat = weight_ref.shape[0]
    preact = preact_of(aggregate, turned_ref[...], bias_ref[...])
    slope = jnp.where(preact > 0, 1.0, jnp.exp(jnp.minimum(preact, 0.0)))
    grad_pre = cot_ref[...].astype(jnp.float32) * slope
    grad = lax.dot_general(
        (inv_row * grad_pre).astype(jnp.bfloat16),
        weight_ref[...],
        (((0,), (1,)), ((), ())),
        preferred_element_type=jnp.float32,
    ).astype(jnp.bfloat16)
    pieces = grad.shape[0]
    grad_ref[...] = grad
    both_ref[:pieces, :] = grad
    grad_pre_b = grad_pre.astype(jnp.bfloat16)
    both_ref[pieces : pieces + feat, :] = turned(aggregate, grad_pre_b).astype(jnp.bfloat16)
    ones = jnp.ones((16, pieces), jnp.bfloat16)
    rest = (grad_pre - grad_pre_b.astype(jnp.float32)).astype(jnp.bfloat16)
    both_ref[pieces + feat :, :] = (turned(ones, grad_pre_b) + turned(ones, rest)).astype(
        jnp.bfloat16
    )


def gradient_step(degree, weight, turned_operands, parts):
    feat, pieces = parts[0].shape
    vmem = pl.BlockSpec(memory_space=pltpu.VMEM)
    return pl.pallas_call(
        functools.partial(gradient_kernel, len(parts)),
        out_shape=[
            jax.ShapeDtypeStruct((pieces, feat), jnp.bfloat16),
            jax.ShapeDtypeStruct((pieces + feat + 16, feat), jnp.bfloat16),
            jax.ShapeDtypeStruct((feat, pieces), jnp.bfloat16),
        ],
        in_specs=[vmem] * (5 + len(parts)),
        out_specs=[vmem] * 3,
        compiler_params=pltpu.CompilerParams(vmem_limit_bytes=LIMIT),
        name="gradient_step",
    )(degree.reshape(1, pieces), weight, *turned_operands, *parts)


def hidden_kernel(turned_ref, bias_ref, aggregate_ref, hidden_ref):
    preact = preact_of(aggregate_ref[...], turned_ref[...], bias_ref[...])
    hidden = jnp.where(preact > 0, preact, jnp.exp(jnp.minimum(preact, 0.0)) - 1.0)
    hidden_ref[...] = hidden.astype(jnp.bfloat16).T


def hidden_step(weight_turned, bias_turned, aggregate):
    feat, pieces = aggregate.shape
    vmem = pl.BlockSpec(memory_space=pltpu.VMEM)
    return pl.pallas_call(
        hidden_kernel,
        out_shape=jax.ShapeDtypeStruct((pieces, feat), jnp.bfloat16),
        in_specs=[vmem] * 3,
        out_specs=vmem,
        compiler_params=pltpu.CompilerParams(vmem_limit_bytes=LIMIT),
        name="hidden_step",
    )(weight_turned, bias_turned, aggregate)


def sum_of(refs):
    total = refs[0][...].astype(jnp.float32)
    for ref in refs[1:]:
        total += ref[...].astype(jnp.float32)
    return total


def backward_kernel(pieces, kinds, chunks, begun, block_ref, *refs):
    sources, out_ref = refs[: len(kinds)], refs[-1]
    terms = refs[len(kinds) + begun : -1]
    feat = out_ref.shape[1]
    me_row = lax.axis_index("row")
    me_col = lax.axis_index("col")
    for m, chunk in enumerate(chunks):
        down = pl.ds(pl.multiple_of((me_row ^ chunk) * pieces, pieces), pieces)
        if begun:
            total = refs[len(kinds)][chunk * pieces : (chunk + 1) * pieces, :]
        else:
            total = jnp.zeros((pieces, feat), jnp.float32)
        for k, source in zip(kinds, sources):
            across = pl.ds(pl.multiple_of((me_col ^ k) * pieces, pieces), pieces)
            total += jnp.dot(
                block_ref[down, across], source[:pieces, :], preferred_element_type=jnp.float32
            )
        out_ref[m * pieces : (m + 1) * pieces, :] = total.astype(out_ref.dtype)
    if terms:
        out_ref[len(chunks) * pieces :, :] = sum_of(terms).astype(out_ref.dtype)


def backward_parts(block, sources, kinds, chunks, begun, terms, name):
    pieces, feat = sources[0].shape
    begun = [] if begun is None else [begun]
    extra = terms[0].shape[0] if terms else 0
    vmem = pl.BlockSpec(memory_space=pltpu.VMEM)
    dtype = jnp.bfloat16 if begun else jnp.float32
    return pl.pallas_call(
        functools.partial(backward_kernel, pieces, kinds, chunks, len(begun)),
        out_shape=jax.ShapeDtypeStruct((len(chunks) * pieces + extra, feat), dtype),
        in_specs=[vmem] * (1 + len(kinds) + len(begun) + len(terms)),
        out_specs=vmem,
        compiler_params=pltpu.CompilerParams(vmem_limit_bytes=LIMIT),
        name=name,
    )(block, *(sources[k] for k in kinds), *begun, *terms)


def pair_kernel(first, mine_ref, theirs_ref, sent_ref, got_ref, *outs):
    feat = mine_ref.shape[0] // 4
    terms = sum_of((sent_ref.at[2 * feat :], got_ref.at[2 * feat :])).astype(jnp.bfloat16)
    for m, out in enumerate(outs):
        mine = mine_ref[(first + m) * feat : (first + m + 1) * feat, :].astype(jnp.float32)
        theirs = theirs_ref[m * feat : (m + 1) * feat, :].astype(jnp.float32)
        out[:feat, :] = (mine + theirs).astype(jnp.bfloat16)
        out[feat:, :] = terms


def pair_sum(first, mine, theirs, sent, got):
    vmem = pl.BlockSpec(memory_space=pltpu.VMEM)
    rows = sent.shape[0] - mine.shape[0] // 4
    return pl.pallas_call(
        functools.partial(pair_kernel, first),
        out_shape=[jax.ShapeDtypeStruct((rows, mine.shape[1]), jnp.bfloat16)] * 2,
        in_specs=[vmem] * 4,
        out_specs=[vmem] * 2,
        compiler_params=pltpu.CompilerParams(vmem_limit_bytes=LIMIT),
        name="pair_near" if first else "pair_far",
    )(mine, theirs, sent, got)


def finish_kernel(scale, root_ref, *refs):
    *parts, out_ref, weight_ref, bias_ref = refs
    total = sum_of(parts)
    pieces, feat = out_ref.shape
    out_ref[...] = (root_ref[...] * total[:pieces]).astype(jnp.bfloat16)
    weight_ref[...] = total[pieces : pieces + feat] * scale
    bias_ref[...] = total[pieces + feat : pieces + feat + 1] * scale


def finish(root, parts, scale):
    pieces, feat = root.shape
    vmem = pl.BlockSpec(memory_space=pltpu.VMEM)
    grad_features, grad_weight, grad_bias = pl.pallas_call(
        functools.partial(finish_kernel, scale),
        out_shape=[
            jax.ShapeDtypeStruct((pieces, feat), jnp.bfloat16),
            jax.ShapeDtypeStruct((feat, feat), jnp.float32),
            jax.ShapeDtypeStruct((1, feat), jnp.float32),
        ],
        in_specs=[vmem] * (1 + len(parts)),
        out_specs=[vmem] * 3,
        compiler_params=pltpu.CompilerParams(vmem_limit_bytes=LIMIT),
        name="finish",
    )(root, *parts)
    return grad_features, grad_weight, grad_bias.reshape(feat)


def scale_kernel(
    degree_hbm, features_hbm, rows_hbm, cols_hbm, codes_hbm, out_ref, lists_ref, codes_ref,
    degree_ref, features_ref, sems
):
    slots = codes_ref.shape[0]
    first, second, *others = fetch(
        (degree_hbm, features_hbm, rows_hbm.at[0], cols_hbm.at[0], codes_hbm),
        (
            degree_ref,
            features_ref,
            lists_ref.at[0:1, 0:slots],
            lists_ref.at[1:2, 0:slots],
            codes_ref,
        ),
        sems,
    )
    first.wait()
    inv_row = lax.rsqrt(degree_ref[...].astype(jnp.float32))
    second.wait()
    out_ref[...] = (inv_row * features_ref[...].astype(jnp.float32).T).astype(jnp.bfloat16)
    for copy in others:
        copy.wait()


def scale_rows(degree, features, tile_rows, tile_cols, codes):
    pieces, feat = features.shape
    return pl.pallas_call(
        scale_kernel,
        out_shape=[
            pltpu.VMEM((feat, pieces), jnp.bfloat16),
            pltpu.VMEM((8, codes.shape[0]), jnp.int32),
            pltpu.VMEM(codes.shape, codes.dtype),
        ],
        in_specs=[pl.BlockSpec(memory_space=pl.ANY)] * 5,
        out_specs=[pl.BlockSpec(memory_space=pltpu.VMEM)] * 3,
        scratch_shapes=[
            pltpu.VMEM((1, pieces), jnp.int32),
            pltpu.VMEM((pieces, feat), jnp.bfloat16),
            pltpu.SemaphoreType.DMA((5,)),
        ],
        compiler_params=pltpu.CompilerParams(vmem_limit_bytes=60 * 2**20),
        name="scale_rows",
    )(degree.reshape(1, pieces), features, tile_rows, tile_cols, codes)


def terms_kernel(skip, *refs):
    *parts, out_ref = refs
    total = parts[0][skip:, :].astype(jnp.float32)
    for part in parts[1:]:
        total += part[skip:, :].astype(jnp.float32)
    out_ref[...] = total.astype(jnp.bfloat16)


def terms_sum(parts, skip, name):
    rows, width = parts[0].shape
    vmem = pl.BlockSpec(memory_space=pltpu.VMEM)
    return pl.pallas_call(
        functools.partial(terms_kernel, skip),
        out_shape=jax.ShapeDtypeStruct((rows - skip, width), jnp.bfloat16),
        in_specs=[vmem] * len(parts),
        out_specs=vmem,
        compiler_params=pltpu.CompilerParams(vmem_limit_bytes=LIMIT),
        name=name,
    )(*parts)


def dense_local(
    features, degree, weight, bias, cotangent, tile_rows, tile_cols, tile_count, tile_codes
):
    pieces, feat = features.shape
    n_row = lax.axis_size("row")
    n_col = lax.axis_size("col")
    grad_scale = 1.0 / math.sqrt(pieces * n_row * n_col)
    scaled, lists, codes = scale_rows(
        degree, features, tile_rows, tile_cols, tile_codes[0, 0]
    )
    chips = [6, 4, 2]
    lines = list(range(n_col - 1, 0, -1))
    landed = [swap(scaled, "row", m) for m in chips]
    sibling = swap(scaled, "row", 1)
    slots = codes.shape[0]
    middle = slots * 3 // 4 // GROUP * GROUP
    size = (pieces * n_col, pieces * n_row)
    block = build_block(lists, tile_count, codes, *size, 0, middle)
    block, landed = lax.optimization_barrier((block, landed))
    parts = [scaled, sibling, *landed, swap(stack(landed), "row", 1)]
    bits = [0, 1, *chips, *(m + 1 for m in chips)]
    block = build_block(lists, tile_count, codes, *size, middle, slots, block)
    half = max(1, n_col // 2)
    far = forward_parts(block, parts, bits, lines[:half], "forward_far")
    near = forward_parts(block, parts, bits, lines[half:] + [0], "forward_near")
    parts = dict(zip(lines + [0], [*far, *near]))
    *dense, parts[0] = lax.optimization_barrier((weight, bias, cotangent, degree, parts[0]))
    *dense, root = turn(*dense)
    landed = [parts[0]] + [swap(parts[k], "col", k) for k in lines]
    grad_own, both, aggregate = gradient_step(degree, weight, dense, landed)
    grads = [grad_own, swap(both, "col", 1)] + [swap(grad_own, "col", k) for k in range(2, n_col)]
    grads[1], aggregate = lax.optimization_barrier((grads[1], aggregate))
    hidden = hidden_step(dense[0], dense[1], aggregate)
    terms = [terms_sum([both, grads[1]], pieces, "terms_col")]
    terms += [swap(terms[0], "col", k) for k in range(2, n_col, 2)]
    begun = backward_parts(block, grads, [0, 1], range(n_row), None, [], "backward_near")
    grads[2:], begun, terms = lax.optimization_barrier((grads[2:], begun, terms))
    far = range(2, n_col)
    sent = backward_parts(block, grads, far, [7, 5], begun, terms, "backward_other")
    got = swap(sent, "row", 1)
    rest = swap(backward_parts(block, grads, far, [3, 1], begun, [], "backward_rest"), "row", 1)
    mine = backward_parts(block, grads, far, [6, 4, 2, 0], begun, [], "backward_own")
    chunks = pair_sum(0, mine, got, sent, got)
    landed = [swap(chunk, "row", m) for chunk, m in zip(chunks, chips)]
    chunks = pair_sum(2, mine, rest, sent, got)
    landed = [chunks[1], *landed, swap(chunks[0], "row", chips[2])]
    grad_features, grad_weight, grad_bias = finish(root, landed, grad_scale)
    return (hidden, grad_features, grad_weight, grad_bias)


def solution(mesh):
    placed = (
        P(("row", "col"), None),
        P(("row", "col")),
        P(),
        P(),
        P(("row", "col"), None),
        P("row", "col", None),
        P("row", "col", None),
        P("row", "col", None),
        P("row", "col", None, None),
    )
    n_row, n_col = mesh.shape["row"], mesh.shape["col"]

    def local(features, *rest):
        block_bytes = 2 * features.shape[0] ** 2 * n_row * n_col
        paired = n_row == 8 and n_col == 4
        if paired and block_bytes <= DENSE_BYTES:
            return dense_local(features, *rest)
        return sparse_local(features, *rest)

    return jax.shard_map(
        local,
        mesh=mesh,
        in_specs=placed,
        out_specs=(P(("row", "col"), None), P(("row", "col"), None), P(), P()),
        check_vma=False,
    )
```

```python
import functools
import math

import jax
import jax.numpy as jnp
from jax import lax
from jax.experimental import pallas as pl
from jax.experimental.pallas import tpu as pltpu
from jax.sharding import PartitionSpec as P

BLOCK = 16
GROUP = 32
MOD = 4093
HIT = 64
DENSE_BYTES = 8 * 2**20
LIMIT = 16 * 2**20


def tile_mask(code_block, living):
    tile_side = code_block.shape[1] // 2
    row_code = code_block[:, :tile_side][:, :, None]
    col_code = code_block[:, tile_side:][:, None, :]
    hashed = (row_code * col_code + row_code + 3 * col_code) % MOD
    return ((hashed < HIT) & living[:, None, None]).astype(jnp.bfloat16)


def accumulate(codes_dev, rows_dev, cols_dev, count_dev, source, out_tiles, backward):
    tile_side = source.shape[1]
    width_feat = source.shape[2]

    def block_step(block_id, summed):
        slot_start = block_id * BLOCK
        code_block = lax.dynamic_slice_in_dim(codes_dev, slot_start, BLOCK, 0)
        row_block = lax.dynamic_slice_in_dim(rows_dev, slot_start, BLOCK, 0)
        col_block = lax.dynamic_slice_in_dim(cols_dev, slot_start, BLOCK, 0)
        slot_ids = slot_start + jnp.arange(BLOCK, dtype=jnp.int32)
        target = col_block if backward else row_block
        anchor = row_block if backward else col_block
        living = slot_ids < count_dev
        keep = tile_mask(code_block, living)
        picked = jnp.take(source, anchor, axis=0)
        if backward:
            product = jnp.einsum("tij,tif->tjf", keep, picked, preferred_element_type=jnp.float32)
        else:
            product = jnp.einsum("tij,tjf->tif", keep, picked, preferred_element_type=jnp.float32)
        return summed.at[target].add(product)

    start_sum = jnp.zeros((out_tiles, tile_side, width_feat), jnp.float32)
    loop_count = codes_dev.shape[0] // BLOCK
    summed = lax.fori_loop(0, loop_count, block_step, start_sum)
    return summed.reshape(out_tiles * tile_side, width_feat)


def dense_part(aggregate, weight, bias, cotangent, inv_root):
    preact = jnp.dot(aggregate, weight, preferred_element_type=jnp.float32) + bias
    hidden = jax.nn.elu(preact).astype(jnp.bfloat16)
    elu_slope = jnp.where(preact > 0, 1.0, jnp.exp(jnp.minimum(preact, 0.0)))
    grad_pre = cotangent.astype(jnp.float32) * elu_slope
    grad_pre_b = grad_pre.astype(jnp.bfloat16)
    grad_weight = lax.dot_general(
        aggregate, grad_pre_b, (((0,), (0,)), ((), ())), preferred_element_type=jnp.float32
    )
    grad_bias = jnp.sum(grad_pre, axis=0)
    grad_agg = jnp.dot(grad_pre_b, weight.T, preferred_element_type=jnp.float32)
    grad_scaled = (inv_root * grad_agg).astype(jnp.bfloat16)
    return (hidden, grad_weight, grad_bias, grad_scaled)


def sparse_local(
    features, degree, weight, bias, cotangent, tile_rows, tile_cols, tile_count, tile_codes
):
    codes_dev = tile_codes[0, 0]
    rows_dev = tile_rows[0, 0]
    cols_dev = tile_cols[0, 0]
    count_dev = tile_count[0, 0, 0]
    pieces = features.shape[0]
    width_feat = features.shape[1]
    tile_side = codes_dev.shape[1] // 2
    row_devs = lax.axis_size("row")
    col_devs = lax.axis_size("col")
    grad_scale = 1.0 / math.sqrt(pieces * row_devs * col_devs)
    row_tiles = pieces * col_devs // tile_side
    col_tiles = pieces * row_devs // tile_side
    inv_root = lax.rsqrt(degree.astype(jnp.float32))[:, None]
    scaled = (inv_root * features.astype(jnp.float32)).astype(jnp.bfloat16)
    column_feats = lax.all_gather(scaled, "row", axis=0, tiled=True).reshape(
        col_tiles, tile_side, width_feat
    )
    row_terms = accumulate(codes_dev, rows_dev, cols_dev, count_dev, column_feats, row_tiles, False)
    row_sum = lax.psum_scatter(
        row_terms.astype(jnp.bfloat16), "col", scatter_dimension=0, tiled=True
    ).astype(jnp.float32)
    aggregate = (inv_root * row_sum).astype(jnp.bfloat16)
    hidden, grad_weight, grad_bias, grads = dense_part(
        aggregate, weight, bias, cotangent, inv_root
    )
    grad_weight, grad_bias = (
        lax.psum((grad_weight * grad_scale).astype(jnp.bfloat16), ("row", "col")),
        lax.psum((grad_bias * grad_scale).astype(jnp.bfloat16), ("row", "col")),
    )
    row_sources = lax.all_gather(grads, "col", axis=0, tiled=True).reshape(
        row_tiles, tile_side, width_feat
    )
    col_terms = accumulate(codes_dev, rows_dev, cols_dev, count_dev, row_sources, col_tiles, True)
    grad_sum = lax.psum_scatter(
        col_terms.astype(jnp.bfloat16), "row", scatter_dimension=0, tiled=True
    ).astype(jnp.float32)
    grad_features = (inv_root * grad_sum).astype(jnp.bfloat16)
    return (
        hidden,
        grad_features,
        grad_weight.astype(jnp.float32),
        grad_bias.astype(jnp.float32),
    )


def swap(value, axis, bits):
    size = lax.axis_size(axis)
    return lax.ppermute(value, axis, [(i, i ^ bits) for i in range(size)])


def turned(lhs, rhs):
    return lax.dot_general(lhs, rhs, (((1,), (1,)), ((), ())), preferred_element_type=jnp.float32)


def fetch(sources, targets, sems):
    copies = [
        pltpu.make_async_copy(src, dst, sems.at[k])
        for k, (src, dst) in enumerate(zip(sources, targets))
    ]
    for copy in copies:
        copy.start()
    return copies


def build_kernel(first, last, lists_vmem, count_ref, codes_ref, *refs):
    block_ref, col_scr, row_scr, lists_ref, sems = refs[-5:]
    slots = codes_ref.shape[0]
    side = codes_ref.shape[1] // 2
    (copy,) = fetch((lists_vmem,), (lists_ref,), sems)
    if first == 0:
        block_ref[...] = jnp.zeros_like(block_ref)
    row_code = codes_ref[:, :side].astype(jnp.float32) + 3.0
    row_code = jnp.where(row_code > MOD // 2, row_code - MOD, row_code)
    col_code = codes_ref[:, side:].astype(jnp.float32) + 1.0
    col_code = jnp.where(col_code > MOD // 2, col_code - MOD, col_code)
    slot = lax.broadcasted_iota(jnp.int32, (slots, side), 0)
    col_code = jnp.where(slot < count_ref[0, 0, 0], col_code, 0.0)
    coarse = 2.0**-12
    row_scr[...] = row_code * coarse + row_code * (1.0 / MOD - coarse)
    by_side = col_code.T
    groups = range(first // GROUP, last // GROUP)
    for g in groups:
        col_scr[g] = by_side if g == 0 else pltpu.roll(by_side, slots - g * GROUP, axis=1)
    copy.wait()
    middle = (3.0 + (HIT - 1) / 2.0) / MOD
    reach = jnp.bfloat16(2.0**-7)
    one, zero = jnp.bfloat16(1.0), jnp.bfloat16(0.0)

    def step(g, carry):
        col_vals = col_scr[g]
        row_vals = row_scr[pl.ds(pl.multiple_of(g * GROUP, GROUP), GROUP), :]
        for t in range(GROUP):
            s = g * GROUP + t
            turns = jnp.broadcast_to(col_vals[:, t : t + 1], (side, side)) * jnp.broadcast_to(
                row_vals[t : t + 1, :], (side, side)
            )
            part = turns - jnp.round(turns)
            keep = jnp.abs((part - middle).astype(jnp.bfloat16)) < reach
            down = pl.ds(pl.multiple_of(lists_ref[1, s] * side, side), side)
            across = pl.ds(pl.multiple_of(lists_ref[0, s] * side, side), side)
            block_ref[down, across] += jnp.where(keep, one, zero)
        return carry

    lax.fori_loop(groups.start, groups.stop, step, 0)


def build_block(lists, tile_count, codes, row_nodes, col_nodes, first, last, block=None):
    slots, width = codes.shape
    side = width // 2
    vmem = pl.BlockSpec(memory_space=pltpu.VMEM)
    begun = [] if block is None else [block]
    return pl.pallas_call(
        functools.partial(build_kernel, first, last),
        out_shape=pltpu.VMEM((col_nodes, row_nodes), jnp.bfloat16),
        in_specs=[vmem, pl.BlockSpec(memory_space=pltpu.SMEM), vmem] + [vmem] * len(begun),
        out_specs=vmem,
        input_output_aliases={3: 0} if begun else {},
        scratch_shapes=[
            pltpu.VMEM((slots // GROUP, side, slots), jnp.float32),
            pltpu.VMEM((slots, side), jnp.float32),
            pltpu.SMEM(lists.shape, jnp.int32),
            pltpu.SemaphoreType.DMA((1,)),
        ],
        compiler_params=pltpu.CompilerParams(vmem_limit_bytes=LIMIT),
        cost_estimate=pl.CostEstimate(
            flops=20 * (last - first) * side * side, bytes_accessed=2**23, transcendentals=0
        ),
        name="build_rest" if begun else "build_block",
    )(lists, tile_count, codes, *begun)


def stack_kernel(*refs):
    *parts, out_ref = refs
    rows = parts[0].shape[0]
    for m, part in enumerate(parts):
        out_ref[m * rows : (m + 1) * rows, :] = part[...]


def stack(parts):
    rows, width = parts[0].shape
    vmem = pl.BlockSpec(memory_space=pltpu.VMEM)
    return pl.pallas_call(
        stack_kernel,
        out_shape=jax.ShapeDtypeStruct((len(parts) * rows, width), parts[0].dtype),
        in_specs=[vmem] * len(parts),
        out_specs=vmem,
        compiler_params=pltpu.CompilerParams(vmem_limit_bytes=LIMIT),
        name="stack",
    )(*parts)


def forward_kernel(bits, high, block_ref, *refs):
    *parts, even_ref, odd_ref, source = refs
    feat, pieces = even_ref.shape
    me_row = lax.axis_index("row")
    me_col = lax.axis_index("col")
    place = iter(bits)
    for part in parts:
        for m in range(part.shape[0] // feat):
            at = pl.multiple_of((me_row ^ next(place)) * pieces, pieces)
            source[:, pl.ds(at, pieces)] = part[m * feat : (m + 1) * feat, :]
    across = pl.multiple_of((me_col ^ high) // 2 * (2 * pieces), 2 * pieces)
    both = jnp.dot(
        source[...], block_ref[:, pl.ds(across, 2 * pieces)], preferred_element_type=jnp.float32
    ).astype(jnp.bfloat16)
    first = me_col % 2 == 0
    even_ref[...] = jnp.where(first, both[:, :pieces], both[:, pieces:])
    odd_ref[...] = jnp.where(first, both[:, pieces:], both[:, :pieces])


def forward_parts(block, parts, bits, high, name):
    feat, pieces = parts[0].shape
    vmem = pl.BlockSpec(memory_space=pltpu.VMEM)
    return pl.pallas_call(
        functools.partial(forward_kernel, bits, high),
        out_shape=[jax.ShapeDtypeStruct((feat, pieces), jnp.bfloat16)] * 2,
        in_specs=[vmem] * (1 + len(parts)),
        out_specs=[vmem] * 2,
        scratch_shapes=[pltpu.VMEM((feat, pieces * len(bits)), jnp.bfloat16)],
        compiler_params=pltpu.CompilerParams(vmem_limit_bytes=LIMIT),
        name=name,
    )(block, *parts)


def turn_kernel(
    weight_ref, bias_ref, cot_ref, degree_ref, weight_out, bias_out, cot_out, root_out
):
    feat, pieces = cot_out.shape
    weight_out[...] = weight_ref[...].T
    bias_out[...] = jnp.broadcast_to(bias_ref[...], (feat, feat)).T
    cot_out[...] = cot_ref[...].T
    inv_row = lax.rsqrt(degree_ref[...].astype(jnp.float32))
    root_out[...] = jnp.broadcast_to(inv_row, (feat, pieces)).T


def turn(weight, bias, cotangent, degree):
    pieces, feat = cotangent.shape
    vmem = pl.BlockSpec(memory_space=pltpu.VMEM)
    return pl.pallas_call(
        turn_kernel,
        out_shape=[
            jax.ShapeDtypeStruct((feat, feat), jnp.bfloat16),
            jax.ShapeDtypeStruct((feat, feat), jnp.float32),
            jax.ShapeDtypeStruct((feat, pieces), jnp.bfloat16),
            jax.ShapeDtypeStruct((pieces, feat), jnp.float32),
        ],
        in_specs=[vmem] * 4,
        out_specs=[vmem] * 4,
        compiler_params=pltpu.CompilerParams(vmem_limit_bytes=LIMIT),
        name="turn",
    )(weight, bias.reshape(1, feat), cotangent, degree.reshape(1, pieces))


def preact_of(aggregate, weight_turned, bias_turned):
    repeats = aggregate.shape[1] // bias_turned.shape[1]
    bias = jnp.concatenate([bias_turned] * repeats, axis=1)
    return jnp.dot(weight_turned, aggregate, preferred_element_type=jnp.float32) + bias


def gradient_kernel(n_col, degree_ref, weight_ref, turned_ref, bias_ref, cot_ref, *refs):
    grad_ref, both_ref, aggregate_ref = refs[n_col:]
    inv_row = lax.rsqrt(degree_ref[...].astype(jnp.float32))
    aggregate = (inv_row * sum_of(refs[:n_col])).astype(jnp.bfloat16)
    aggregate_ref[...] = aggregate
    feat = weight_ref.shape[0]
    preact = preact_of(aggregate, turned_ref[...], bias_ref[...])
    slope = jnp.where(preact > 0, 1.0, jnp.exp(jnp.minimum(preact, 0.0)))
    grad_pre = cot_ref[...].astype(jnp.float32) * slope
    grad = lax.dot_general(
        (inv_row * grad_pre).astype(jnp.bfloat16),
        weight_ref[...],
        (((0,), (1,)), ((), ())),
        preferred_element_type=jnp.float32,
    ).astype(jnp.bfloat16)
    pieces = grad.shape[0]
    grad_ref[...] = grad
    both_ref[:pieces, :] = grad
    grad_pre_b = grad_pre.astype(jnp.bfloat16)
    both_ref[pieces : pieces + feat, :] = turned(aggregate, grad_pre_b).astype(jnp.bfloat16)
    ones = jnp.ones((16, pieces), jnp.bfloat16)
    rest = (grad_pre - grad_pre_b.astype(jnp.float32)).astype(jnp.bfloat16)
    both_ref[pieces + feat :, :] = (turned(ones, grad_pre_b) + turned(ones, rest)).astype(
        jnp.bfloat16
    )


def gradient_step(degree, weight, turned_operands, parts):
    feat, pieces = parts[0].shape
    vmem = pl.BlockSpec(memory_space=pltpu.VMEM)
    return pl.pallas_call(
        functools.partial(gradient_kernel, len(parts)),
        out_shape=[
            jax.ShapeDtypeStruct((pieces, feat), jnp.bfloat16),
            jax.ShapeDtypeStruct((pieces + feat + 16, feat), jnp.bfloat16),
            jax.ShapeDtypeStruct((feat, pieces), jnp.bfloat16),
        ],
        in_specs=[vmem] * (5 + len(parts)),
        out_specs=[vmem] * 3,
        compiler_params=pltpu.CompilerParams(vmem_limit_bytes=LIMIT),
        name="gradient_step",
    )(degree.reshape(1, pieces), weight, *turned_operands, *parts)


def hidden_kernel(turned_ref, bias_ref, aggregate_ref, hidden_ref):
    preact = preact_of(aggregate_ref[...], turned_ref[...], bias_ref[...])
    hidden = jnp.where(preact > 0, preact, jnp.exp(jnp.minimum(preact, 0.0)) - 1.0)
    hidden_ref[...] = hidden.astype(jnp.bfloat16).T


def hidden_step(weight_turned, bias_turned, aggregate):
    feat, pieces = aggregate.shape
    vmem = pl.BlockSpec(memory_space=pltpu.VMEM)
    return pl.pallas_call(
        hidden_kernel,
        out_shape=jax.ShapeDtypeStruct((pieces, feat), jnp.bfloat16),
        in_specs=[vmem] * 3,
        out_specs=vmem,
        compiler_params=pltpu.CompilerParams(vmem_limit_bytes=LIMIT),
        name="hidden_step",
    )(weight_turned, bias_turned, aggregate)


def sum_of(refs):
    total = refs[0][...].astype(jnp.float32)
    for ref in refs[1:]:
        total += ref[...].astype(jnp.float32)
    return total


def backward_kernel(pieces, kinds, chunks, begun, block_ref, *refs):
    sources, out_ref = refs[: len(kinds)], refs[-1]
    terms = refs[len(kinds) + begun : -1]
    feat = out_ref.shape[1]
    me_row = lax.axis_index("row")
    me_col = lax.axis_index("col")
    for m, chunk in enumerate(chunks):
        down = pl.ds(pl.multiple_of((me_row ^ chunk) * pieces, pieces), pieces)
        if begun:
            total = refs[len(kinds)][chunk * pieces : (chunk + 1) * pieces, :]
        else:
            total = jnp.zeros((pieces, feat), jnp.float32)
        for k, source in zip(kinds, sources):
            across = pl.ds(pl.multiple_of((me_col ^ k) * pieces, pieces), pieces)
            total += jnp.dot(
                block_ref[down, across], source[:pieces, :], preferred_element_type=jnp.float32
            )
        out_ref[m * pieces : (m + 1) * pieces, :] = total.astype(out_ref.dtype)
    if terms:
        out_ref[len(chunks) * pieces :, :] = sum_of(terms).astype(out_ref.dtype)


def backward_parts(block, sources, kinds, chunks, begun, terms, name):
    pieces, feat = sources[0].shape
    begun = [] if begun is None else [begun]
    extra = terms[0].shape[0] if terms else 0
    vmem = pl.BlockSpec(memory_space=pltpu.VMEM)
    dtype = jnp.bfloat16 if begun else jnp.float32
    return pl.pallas_call(
        functools.partial(backward_kernel, pieces, kinds, chunks, len(begun)),
        out_shape=jax.ShapeDtypeStruct((len(chunks) * pieces + extra, feat), dtype),
        in_specs=[vmem] * (1 + len(kinds) + len(begun) + len(terms)),
        out_specs=vmem,
        compiler_params=pltpu.CompilerParams(vmem_limit_bytes=LIMIT),
        name=name,
    )(block, *(sources[k] for k in kinds), *begun, *terms)


def pair_kernel(first, mine_ref, theirs_ref, sent_ref, got_ref, *outs):
    feat = mine_ref.shape[0] // 4
    terms = sum_of((sent_ref.at[2 * feat :], got_ref.at[2 * feat :])).astype(jnp.bfloat16)
    for m, out in enumerate(outs):
        mine = mine_ref[(first + m) * feat : (first + m + 1) * feat, :].astype(jnp.float32)
        theirs = theirs_ref[m * feat : (m + 1) * feat, :].astype(jnp.float32)
        out[:feat, :] = (mine + theirs).astype(jnp.bfloat16)
        out[feat:, :] = terms


def pair_sum(first, mine, theirs, sent, got):
    vmem = pl.BlockSpec(memory_space=pltpu.VMEM)
    rows = sent.shape[0] - mine.shape[0] // 4
    return pl.pallas_call(
        functools.partial(pair_kernel, first),
        out_shape=[jax.ShapeDtypeStruct((rows, mine.shape[1]), jnp.bfloat16)] * 2,
        in_specs=[vmem] * 4,
        out_specs=[vmem] * 2,
        compiler_params=pltpu.CompilerParams(vmem_limit_bytes=LIMIT),
        name="pair_near" if first else "pair_far",
    )(mine, theirs, sent, got)


def finish_kernel(scale, root_ref, *refs):
    *parts, out_ref, weight_ref, bias_ref = refs
    total = sum_of(parts)
    pieces, feat = out_ref.shape
    out_ref[...] = (root_ref[...] * total[:pieces]).astype(jnp.bfloat16)
    weight_ref[...] = total[pieces : pieces + feat] * scale
    bias_ref[...] = total[pieces + feat : pieces + feat + 1] * scale


def finish(root, parts, scale):
    pieces, feat = root.shape
    vmem = pl.BlockSpec(memory_space=pltpu.VMEM)
    grad_features, grad_weight, grad_bias = pl.pallas_call(
        functools.partial(finish_kernel, scale),
        out_shape=[
            jax.ShapeDtypeStruct((pieces, feat), jnp.bfloat16),
            jax.ShapeDtypeStruct((feat, feat), jnp.float32),
            jax.ShapeDtypeStruct((1, feat), jnp.float32),
        ],
        in_specs=[vmem] * (1 + len(parts)),
        out_specs=[vmem] * 3,
        compiler_params=pltpu.CompilerParams(vmem_limit_bytes=LIMIT),
        name="finish",
    )(root, *parts)
    return grad_features, grad_weight, grad_bias.reshape(feat)


def scale_kernel(
    degree_hbm, features_hbm, rows_hbm, cols_hbm, codes_hbm, out_ref, lists_ref, codes_ref,
    degree_ref, features_ref, sems
):
    slots = codes_ref.shape[0]
    first, second, *others = fetch(
        (degree_hbm, features_hbm, rows_hbm.at[0], cols_hbm.at[0], codes_hbm),
        (
            degree_ref,
            features_ref,
            lists_ref.at[0:1, 0:slots],
            lists_ref.at[1:2, 0:slots],
            codes_ref,
        ),
        sems,
    )
    first.wait()
    inv_row = lax.rsqrt(degree_ref[...].astype(jnp.float32))
    second.wait()
    out_ref[...] = (inv_row * features_ref[...].astype(jnp.float32).T).astype(jnp.bfloat16)
    for copy in others:
        copy.wait()


def scale_rows(degree, features, tile_rows, tile_cols, codes):
    pieces, feat = features.shape
    return pl.pallas_call(
        scale_kernel,
        out_shape=[
            pltpu.VMEM((feat, pieces), jnp.bfloat16),
            pltpu.VMEM((8, codes.shape[0]), jnp.int32),
            pltpu.VMEM(codes.shape, codes.dtype),
        ],
        in_specs=[pl.BlockSpec(memory_space=pl.ANY)] * 5,
        out_specs=[pl.BlockSpec(memory_space=pltpu.VMEM)] * 3,
        scratch_shapes=[
            pltpu.VMEM((1, pieces), jnp.int32),
            pltpu.VMEM((pieces, feat), jnp.bfloat16),
            pltpu.SemaphoreType.DMA((5,)),
        ],
        compiler_params=pltpu.CompilerParams(vmem_limit_bytes=60 * 2**20),
        name="scale_rows",
    )(degree.reshape(1, pieces), features, tile_rows, tile_cols, codes)


def terms_kernel(skip, *refs):
    *parts, out_ref = refs
    total = parts[0][skip:, :].astype(jnp.float32)
    for part in parts[1:]:
        total += part[skip:, :].astype(jnp.float32)
    out_ref[...] = total.astype(jnp.bfloat16)


def terms_sum(parts, skip, name):
    rows, width = parts[0].shape
    vmem = pl.BlockSpec(memory_space=pltpu.VMEM)
    return pl.pallas_call(
        functools.partial(terms_kernel, skip),
        out_shape=jax.ShapeDtypeStruct((rows - skip, width), jnp.bfloat16),
        in_specs=[vmem] * len(parts),
        out_specs=vmem,
        compiler_params=pltpu.CompilerParams(vmem_limit_bytes=LIMIT),
        name=name,
    )(*parts)


def dense_local(
    features, degree, weight, bias, cotangent, tile_rows, tile_cols, tile_count, tile_codes
):
    pieces, feat = features.shape
    n_row = lax.axis_size("row")
    n_col = lax.axis_size("col")
    grad_scale = 1.0 / math.sqrt(pieces * n_row * n_col)
    scaled, lists, codes = scale_rows(
        degree, features, tile_rows, tile_cols, tile_codes[0, 0]
    )
    chips = [6, 4, 2]
    lines = list(range(n_col - 1, 0, -1))
    landed = [swap(scaled, "row", m) for m in chips]
    sibling = swap(scaled, "row", 1)
    slots = codes.shape[0]
    middle = slots * 3 // 4 // GROUP * GROUP
    size = (pieces * n_col, pieces * n_row)
    block = build_block(lists, tile_count, codes, *size, 0, middle)
    block, landed = lax.optimization_barrier((block, landed))
    parts = [scaled, sibling, *landed, swap(stack(landed), "row", 1)]
    bits = [0, 1, *chips, *(m + 1 for m in chips)]
    block = build_block(lists, tile_count, codes, *size, middle, slots, block)
    far = forward_parts(block, parts, bits, 2, "forward_far")
    near = forward_parts(block, parts, bits, 0, "forward_near")
    parts = [*near, *far]
    *dense, parts[0] = lax.optimization_barrier((weight, bias, cotangent, degree, parts[0]))
    *dense, root = turn(*dense)
    landed = [parts[0]] + [swap(parts[k], "col", k) for k in lines]
    grad_own, both, aggregate = gradient_step(degree, weight, dense, landed)
    grads = [grad_own, swap(both, "col", 1)] + [swap(grad_own, "col", k) for k in range(2, n_col)]
    grads[1], aggregate = lax.optimization_barrier((grads[1], aggregate))
    hidden = hidden_step(dense[0], dense[1], aggregate)
    terms = [terms_sum([both, grads[1]], pieces, "terms_col")]
    terms += [swap(terms[0], "col", k) for k in range(2, n_col, 2)]
    begun = backward_parts(block, grads, [0, 1], range(n_row), None, [], "backward_near")
    grads[2:], begun, terms = lax.optimization_barrier((grads[2:], begun, terms))
    far = range(2, n_col)
    sent = backward_parts(block, grads, far, [7, 5], begun, terms, "backward_other")
    got = swap(sent, "row", 1)
    rest = swap(backward_parts(block, grads, far, [3, 1], begun, [], "backward_rest"), "row", 1)
    mine = backward_parts(block, grads, far, [6, 4, 2, 0], begun, [], "backward_own")
    chunks = pair_sum(0, mine, got, sent, got)
    landed = [swap(chunk, "row", m) for chunk, m in zip(chunks, chips)]
    chunks = pair_sum(2, mine, rest, sent, got)
    landed = [chunks[1], *landed, swap(chunks[0], "row", chips[2])]
    grad_features, grad_weight, grad_bias = finish(root, landed, grad_scale)
    return (hidden, grad_features, grad_weight, grad_bias)


def solution(mesh):
    placed = (
        P(("row", "col"), None),
        P(("row", "col")),
        P(),
        P(),
        P(("row", "col"), None),
        P("row", "col", None),
        P("row", "col", None),
        P("row", "col", None),
        P("row", "col", None, None),
    )
    n_row, n_col = mesh.shape["row"], mesh.shape["col"]

    def local(features, *rest):
        block_bytes = 2 * features.shape[0] ** 2 * n_row * n_col
        paired = n_row == 8 and n_col == 4
        if paired and block_bytes <= DENSE_BYTES:
            return dense_local(features, *rest)
        return sparse_local(features, *rest)

    return jax.shard_map(
        local,
        mesh=mesh,
        in_specs=placed,
        out_specs=(P(("row", "col"), None), P(("row", "col"), None), P(), P()),
        check_vma=False,
    )
```

```python
import functools
import math

import jax
import jax.numpy as jnp
from jax import lax
from jax.experimental import pallas as pl
from jax.experimental.pallas import tpu as pltpu
from jax.sharding import PartitionSpec as P

BLOCK = 16
GROUP = 32
MOD = 4093
HIT = 64
DENSE_BYTES = 8 * 2**20
LIMIT = 16 * 2**20


def tile_mask(code_block, living):
    tile_side = code_block.shape[1] // 2
    row_code = code_block[:, :tile_side][:, :, None]
    col_code = code_block[:, tile_side:][:, None, :]
    hashed = (row_code * col_code + row_code + 3 * col_code) % MOD
    return ((hashed < HIT) & living[:, None, None]).astype(jnp.bfloat16)


def accumulate(codes_dev, rows_dev, cols_dev, count_dev, source, out_tiles, backward):
    tile_side = source.shape[1]
    width_feat = source.shape[2]

    def block_step(block_id, summed):
        slot_start = block_id * BLOCK
        code_block = lax.dynamic_slice_in_dim(codes_dev, slot_start, BLOCK, 0)
        row_block = lax.dynamic_slice_in_dim(rows_dev, slot_start, BLOCK, 0)
        col_block = lax.dynamic_slice_in_dim(cols_dev, slot_start, BLOCK, 0)
        slot_ids = slot_start + jnp.arange(BLOCK, dtype=jnp.int32)
        target = col_block if backward else row_block
        anchor = row_block if backward else col_block
        living = slot_ids < count_dev
        keep = tile_mask(code_block, living)
        picked = jnp.take(source, anchor, axis=0)
        if backward:
            product = jnp.einsum("tij,tif->tjf", keep, picked, preferred_element_type=jnp.float32)
        else:
            product = jnp.einsum("tij,tjf->tif", keep, picked, preferred_element_type=jnp.float32)
        return summed.at[target].add(product)

    start_sum = jnp.zeros((out_tiles, tile_side, width_feat), jnp.float32)
    loop_count = codes_dev.shape[0] // BLOCK
    summed = lax.fori_loop(0, loop_count, block_step, start_sum)
    return summed.reshape(out_tiles * tile_side, width_feat)


def dense_part(aggregate, weight, bias, cotangent, inv_root):
    preact = jnp.dot(aggregate, weight, preferred_element_type=jnp.float32) + bias
    hidden = jax.nn.elu(preact).astype(jnp.bfloat16)
    elu_slope = jnp.where(preact > 0, 1.0, jnp.exp(jnp.minimum(preact, 0.0)))
    grad_pre = cotangent.astype(jnp.float32) * elu_slope
    grad_pre_b = grad_pre.astype(jnp.bfloat16)
    grad_weight = lax.dot_general(
        aggregate, grad_pre_b, (((0,), (0,)), ((), ())), preferred_element_type=jnp.float32
    )
    grad_bias = jnp.sum(grad_pre, axis=0)
    grad_agg = jnp.dot(grad_pre_b, weight.T, preferred_element_type=jnp.float32)
    grad_scaled = (inv_root * grad_agg).astype(jnp.bfloat16)
    return (hidden, grad_weight, grad_bias, grad_scaled)


def sparse_local(
    features, degree, weight, bias, cotangent, tile_rows, tile_cols, tile_count, tile_codes
):
    codes_dev = tile_codes[0, 0]
    rows_dev = tile_rows[0, 0]
    cols_dev = tile_cols[0, 0]
    count_dev = tile_count[0, 0, 0]
    pieces = features.shape[0]
    width_feat = features.shape[1]
    tile_side = codes_dev.shape[1] // 2
    row_devs = lax.axis_size("row")
    col_devs = lax.axis_size("col")
    grad_scale = 1.0 / math.sqrt(pieces * row_devs * col_devs)
    row_tiles = pieces * col_devs // tile_side
    col_tiles = pieces * row_devs // tile_side
    inv_root = lax.rsqrt(degree.astype(jnp.float32))[:, None]
    scaled = (inv_root * features.astype(jnp.float32)).astype(jnp.bfloat16)
    column_feats = lax.all_gather(scaled, "row", axis=0, tiled=True).reshape(
        col_tiles, tile_side, width_feat
    )
    row_terms = accumulate(codes_dev, rows_dev, cols_dev, count_dev, column_feats, row_tiles, False)
    row_sum = lax.psum_scatter(
        row_terms.astype(jnp.bfloat16), "col", scatter_dimension=0, tiled=True
    ).astype(jnp.float32)
    aggregate = (inv_root * row_sum).astype(jnp.bfloat16)
    hidden, grad_weight, grad_bias, grads = dense_part(
        aggregate, weight, bias, cotangent, inv_root
    )
    grad_weight, grad_bias = (
        lax.psum((grad_weight * grad_scale).astype(jnp.bfloat16), ("row", "col")),
        lax.psum((grad_bias * grad_scale).astype(jnp.bfloat16), ("row", "col")),
    )
    row_sources = lax.all_gather(grads, "col", axis=0, tiled=True).reshape(
        row_tiles, tile_side, width_feat
    )
    col_terms = accumulate(codes_dev, rows_dev, cols_dev, count_dev, row_sources, col_tiles, True)
    grad_sum = lax.psum_scatter(
        col_terms.astype(jnp.bfloat16), "row", scatter_dimension=0, tiled=True
    ).astype(jnp.float32)
    grad_features = (inv_root * grad_sum).astype(jnp.bfloat16)
    return (
        hidden,
        grad_features,
        grad_weight.astype(jnp.float32),
        grad_bias.astype(jnp.float32),
    )


def swap(value, axis, bits):
    size = lax.axis_size(axis)
    return lax.ppermute(value, axis, [(i, i ^ bits) for i in range(size)])


def turned(lhs, rhs):
    return lax.dot_general(lhs, rhs, (((1,), (1,)), ((), ())), preferred_element_type=jnp.float32)


def fetch(sources, targets, sems):
    copies = [
        pltpu.make_async_copy(src, dst, sems.at[k])
        for k, (src, dst) in enumerate(zip(sources, targets))
    ]
    for copy in copies:
        copy.start()
    return copies


def build_kernel(first, last, lists_vmem, count_ref, codes_ref, *refs):
    block_ref, col_scr, row_scr, lists_ref, sems = refs[-5:]
    slots = codes_ref.shape[0]
    side = codes_ref.shape[1] // 2
    (copy,) = fetch((lists_vmem,), (lists_ref,), sems)
    if first == 0:
        block_ref[...] = jnp.zeros_like(block_ref)
    row_code = codes_ref[:, :side].astype(jnp.float32) + 3.0
    row_code = jnp.where(row_code > MOD // 2, row_code - MOD, row_code)
    col_code = codes_ref[:, side:].astype(jnp.float32) + 1.0
    col_code = jnp.where(col_code > MOD // 2, col_code - MOD, col_code)
    slot = lax.broadcasted_iota(jnp.int32, (slots, side), 0)
    col_code = jnp.where(slot < count_ref[0, 0, 0], col_code, 0.0)
    coarse = 2.0**-12
    row_scr[...] = row_code * coarse + row_code * (1.0 / MOD - coarse)
    by_side = col_code.T
    groups = range(first // GROUP, last // GROUP)
    for g in groups:
        col_scr[g] = by_side if g == 0 else pltpu.roll(by_side, slots - g * GROUP, axis=1)
    copy.wait()
    middle = (3.0 + (HIT - 1) / 2.0) / MOD
    reach = jnp.bfloat16(2.0**-7)
    one, zero = jnp.bfloat16(1.0), jnp.bfloat16(0.0)

    def step(g, carry):
        col_vals = col_scr[g]
        row_vals = row_scr[pl.ds(pl.multiple_of(g * GROUP, GROUP), GROUP), :]
        for t in range(GROUP):
            s = g * GROUP + t
            turns = jnp.broadcast_to(col_vals[:, t : t + 1], (side, side)) * jnp.broadcast_to(
                row_vals[t : t + 1, :], (side, side)
            )
            part = turns - jnp.round(turns)
            keep = jnp.abs((part - middle).astype(jnp.bfloat16)) < reach
            down = pl.ds(pl.multiple_of(lists_ref[1, s] * side, side), side)
            across = pl.ds(pl.multiple_of(lists_ref[0, s] * side, side), side)
            block_ref[down, across] += jnp.where(keep, one, zero)
        return carry

    lax.fori_loop(groups.start, groups.stop, step, 0)


def build_block(lists, tile_count, codes, row_nodes, col_nodes, first, last, block=None):
    slots, width = codes.shape
    side = width // 2
    vmem = pl.BlockSpec(memory_space=pltpu.VMEM)
    begun = [] if block is None else [block]
    return pl.pallas_call(
        functools.partial(build_kernel, first, last),
        out_shape=pltpu.VMEM((col_nodes, row_nodes), jnp.bfloat16),
        in_specs=[vmem, pl.BlockSpec(memory_space=pltpu.SMEM), vmem] + [vmem] * len(begun),
        out_specs=vmem,
        input_output_aliases={3: 0} if begun else {},
        scratch_shapes=[
            pltpu.VMEM((slots // GROUP, side, slots), jnp.float32),
            pltpu.VMEM((slots, side), jnp.float32),
            pltpu.SMEM(lists.shape, jnp.int32),
            pltpu.SemaphoreType.DMA((1,)),
        ],
        compiler_params=pltpu.CompilerParams(vmem_limit_bytes=LIMIT),
        cost_estimate=pl.CostEstimate(
            flops=20 * (last - first) * side * side, bytes_accessed=2**23, transcendentals=0
        ),
        name="build_rest" if begun else "build_block",
    )(lists, tile_count, codes, *begun)


def stack_kernel(*refs):
    *parts, out_ref = refs
    rows = parts[0].shape[0]
    for m, part in enumerate(parts):
        out_ref[m * rows : (m + 1) * rows, :] = part[...]


def stack(parts):
    rows, width = parts[0].shape
    vmem = pl.BlockSpec(memory_space=pltpu.VMEM)
    return pl.pallas_call(
        stack_kernel,
        out_shape=jax.ShapeDtypeStruct((len(parts) * rows, width), parts[0].dtype),
        in_specs=[vmem] * len(parts),
        out_specs=vmem,
        compiler_params=pltpu.CompilerParams(vmem_limit_bytes=LIMIT),
        name="stack",
    )(*parts)


def forward_kernel(bits, far, block_ref, *refs):
    outs = refs[len(refs) - len(far) :]
    parts = refs[: len(refs) - len(far)]
    feat, pieces = parts[0].shape
    me_row = lax.axis_index("row")
    me_col = lax.axis_index("col")
    for out, k in zip(outs, far):
        across = pl.ds(pl.multiple_of((me_col ^ k) * pieces, pieces), pieces)
        total = jnp.zeros((feat, pieces), jnp.float32)
        place = iter(bits)
        for part in parts:
            for m in range(part.shape[0] // feat):
                down = pl.ds(pl.multiple_of((me_row ^ next(place)) * pieces, pieces), pieces)
                total += jnp.dot(
                    part[m * feat : (m + 1) * feat, :],
                    block_ref[down, across],
                    preferred_element_type=jnp.float32,
                )
        out[...] = total.astype(jnp.bfloat16)


def forward_parts(block, parts, bits, far, name):
    feat, pieces = parts[0].shape
    vmem = pl.BlockSpec(memory_space=pltpu.VMEM)
    return pl.pallas_call(
        functools.partial(forward_kernel, bits, far),
        out_shape=[jax.ShapeDtypeStruct((feat, pieces), jnp.bfloat16)] * len(far),
        in_specs=[vmem] * (1 + len(parts)),
        out_specs=[vmem] * len(far),
        compiler_params=pltpu.CompilerParams(vmem_limit_bytes=LIMIT),
        name=name,
    )(block, *parts)


def turn_kernel(
    weight_ref, bias_ref, cot_ref, degree_ref, weight_out, bias_out, cot_out, root_out
):
    feat, pieces = cot_out.shape
    weight_out[...] = weight_ref[...].T
    bias_out[...] = jnp.broadcast_to(bias_ref[...], (feat, feat)).T
    cot_out[...] = cot_ref[...].T
    inv_row = lax.rsqrt(degree_ref[...].astype(jnp.float32))
    root_out[...] = jnp.broadcast_to(inv_row, (feat, pieces)).T


def turn(weight, bias, cotangent, degree):
    pieces, feat = cotangent.shape
    vmem = pl.BlockSpec(memory_space=pltpu.VMEM)
    return pl.pallas_call(
        turn_kernel,
        out_shape=[
            jax.ShapeDtypeStruct((feat, feat), jnp.bfloat16),
            jax.ShapeDtypeStruct((feat, feat), jnp.float32),
            jax.ShapeDtypeStruct((feat, pieces), jnp.bfloat16),
            jax.ShapeDtypeStruct((pieces, feat), jnp.float32),
        ],
        in_specs=[vmem] * 4,
        out_specs=[vmem] * 4,
        compiler_params=pltpu.CompilerParams(vmem_limit_bytes=LIMIT),
        name="turn",
    )(weight, bias.reshape(1, feat), cotangent, degree.reshape(1, pieces))


def preact_of(aggregate, weight_turned, bias_turned):
    repeats = aggregate.shape[1] // bias_turned.shape[1]
    bias = jnp.concatenate([bias_turned] * repeats, axis=1)
    return jnp.dot(weight_turned, aggregate, preferred_element_type=jnp.float32) + bias


def gradient_kernel(n_col, degree_ref, weight_ref, turned_ref, bias_ref, cot_ref, *refs):
    grad_ref, both_ref, aggregate_ref = refs[n_col:]
    inv_row = lax.rsqrt(degree_ref[...].astype(jnp.float32))
    aggregate = (inv_row * sum_of(refs[:n_col])).astype(jnp.bfloat16)
    aggregate_ref[...] = aggregate
    feat = weight_ref.shape[0]
    preact = preact_of(aggregate, turned_ref[...], bias_ref[...])
    slope = jnp.where(preact > 0, 1.0, jnp.exp(jnp.minimum(preact, 0.0)))
    grad_pre = cot_ref[...].astype(jnp.float32) * slope
    grad = lax.dot_general(
        (inv_row * grad_pre).astype(jnp.bfloat16),
        weight_ref[...],
        (((0,), (1,)), ((), ())),
        preferred_element_type=jnp.float32,
    ).astype(jnp.bfloat16)
    pieces = grad.shape[0]
    grad_ref[...] = grad
    both_ref[:pieces, :] = grad
    grad_pre_b = grad_pre.astype(jnp.bfloat16)
    both_ref[pieces : pieces + feat, :] = turned(aggregate, grad_pre_b).astype(jnp.bfloat16)
    ones = jnp.ones((16, pieces), jnp.bfloat16)
    rest = (grad_pre - grad_pre_b.astype(jnp.float32)).astype(jnp.bfloat16)
    both_ref[pieces + feat :, :] = (turned(ones, grad_pre_b) + turned(ones, rest)).astype(
        jnp.bfloat16
    )


def gradient_step(degree, weight, turned_operands, parts):
    feat, pieces = parts[0].shape
    vmem = pl.BlockSpec(memory_space=pltpu.VMEM)
    return pl.pallas_call(
        functools.partial(gradient_kernel, len(parts)),
        out_shape=[
            jax.ShapeDtypeStruct((pieces, feat), jnp.bfloat16),
            jax.ShapeDtypeStruct((pieces + feat + 16, feat), jnp.bfloat16),
            jax.ShapeDtypeStruct((feat, pieces), jnp.bfloat16),
        ],
        in_specs=[vmem] * (5 + len(parts)),
        out_specs=[vmem] * 3,
        compiler_params=pltpu.CompilerParams(vmem_limit_bytes=LIMIT),
        name="gradient_step",
    )(degree.reshape(1, pieces), weight, *turned_operands, *parts)


def hidden_kernel(turned_ref, bias_ref, aggregate_ref, hidden_ref):
    preact = preact_of(aggregate_ref[...], turned_ref[...], bias_ref[...])
    hidden = jnp.where(preact > 0, preact, jnp.exp(jnp.minimum(preact, 0.0)) - 1.0)
    hidden_ref[...] = hidden.astype(jnp.bfloat16).T


def hidden_step(weight_turned, bias_turned, aggregate):
    feat, pieces = aggregate.shape
    vmem = pl.BlockSpec(memory_space=pltpu.VMEM)
    return pl.pallas_call(
        hidden_kernel,
        out_shape=jax.ShapeDtypeStruct((pieces, feat), jnp.bfloat16),
        in_specs=[vmem] * 3,
        out_specs=vmem,
        compiler_params=pltpu.CompilerParams(vmem_limit_bytes=LIMIT),
        name="hidden_step",
    )(weight_turned, bias_turned, aggregate)


def sum_of(refs):
    total = refs[0][...].astype(jnp.float32)
    for ref in refs[1:]:
        total += ref[...].astype(jnp.float32)
    return total


def backward_kernel(pieces, kinds, chunks, begun, block_ref, *refs):
    sources, out_ref = refs[: len(kinds)], refs[-1]
    terms = refs[len(kinds) + begun : -1]
    feat = out_ref.shape[1]
    me_row = lax.axis_index("row")
    me_col = lax.axis_index("col")
    for m, chunk in enumerate(chunks):
        down = pl.ds(pl.multiple_of((me_row ^ chunk) * pieces, pieces), pieces)
        if begun:
            total = refs[len(kinds)][chunk * pieces : (chunk + 1) * pieces, :]
        else:
            total = jnp.zeros((pieces, feat), jnp.float32)
        for k, source in zip(kinds, sources):
            across = pl.ds(pl.multiple_of((me_col ^ k) * pieces, pieces), pieces)
            total += jnp.dot(
                block_ref[down, across], source[:pieces, :], preferred_element_type=jnp.float32
            )
        out_ref[m * pieces : (m + 1) * pieces, :] = total.astype(out_ref.dtype)
    if terms:
        out_ref[len(chunks) * pieces :, :] = sum_of(terms).astype(out_ref.dtype)


def backward_parts(block, sources, kinds, chunks, begun, terms, name):
    pieces, feat = sources[0].shape
    begun = [] if begun is None else [begun]
    extra = terms[0].shape[0] if terms else 0
    vmem = pl.BlockSpec(memory_space=pltpu.VMEM)
    dtype = jnp.bfloat16 if begun else jnp.float32
    return pl.pallas_call(
        functools.partial(backward_kernel, pieces, kinds, chunks, len(begun)),
        out_shape=jax.ShapeDtypeStruct((len(chunks) * pieces + extra, feat), dtype),
        in_specs=[vmem] * (1 + len(kinds) + len(begun) + len(terms)),
        out_specs=vmem,
        compiler_params=pltpu.CompilerParams(vmem_limit_bytes=LIMIT),
        name=name,
    )(block, *(sources[k] for k in kinds), *begun, *terms)


def pair_kernel(first, mine_ref, theirs_ref, sent_ref, got_ref, *outs):
    feat = mine_ref.shape[0] // 2
    terms = sum_of((sent_ref.at[2 * feat :], got_ref.at[2 * feat :])).astype(jnp.bfloat16)
    for m, out in enumerate(outs):
        mine = mine_ref[(first + m) * feat : (first + m + 1) * feat, :].astype(jnp.float32)
        theirs = theirs_ref[m * feat : (m + 1) * feat, :].astype(jnp.float32)
        out[:feat, :] = (mine + theirs).astype(jnp.bfloat16)
        out[feat:, :] = terms


def pair_sum(first, mine, theirs, sent, got):
    vmem = pl.BlockSpec(memory_space=pltpu.VMEM)
    rows = sent.shape[0] - mine.shape[0] // 2
    return pl.pallas_call(
        functools.partial(pair_kernel, first),
        out_shape=[jax.ShapeDtypeStruct((rows, mine.shape[1]), jnp.bfloat16)] * 2,
        in_specs=[vmem] * 4,
        out_specs=[vmem] * 2,
        compiler_params=pltpu.CompilerParams(vmem_limit_bytes=LIMIT),
        name="pair_near" if first else "pair_far",
    )(mine, theirs, sent, got)


def finish_kernel(scale, root_ref, *refs):
    *parts, out_ref, weight_ref, bias_ref = refs
    total = sum_of(parts)
    pieces, feat = out_ref.shape
    out_ref[...] = (root_ref[...] * total[:pieces]).astype(jnp.bfloat16)
    weight_ref[...] = total[pieces : pieces + feat] * scale
    bias_ref[...] = total[pieces + feat : pieces + feat + 1] * scale


def finish(root, parts, scale):
    pieces, feat = root.shape
    vmem = pl.BlockSpec(memory_space=pltpu.VMEM)
    grad_features, grad_weight, grad_bias = pl.pallas_call(
        functools.partial(finish_kernel, scale),
        out_shape=[
            jax.ShapeDtypeStruct((pieces, feat), jnp.bfloat16),
            jax.ShapeDtypeStruct((feat, feat), jnp.float32),
            jax.ShapeDtypeStruct((1, feat), jnp.float32),
        ],
        in_specs=[vmem] * (1 + len(parts)),
        out_specs=[vmem] * 3,
        compiler_params=pltpu.CompilerParams(vmem_limit_bytes=LIMIT),
        name="finish",
    )(root, *parts)
    return grad_features, grad_weight, grad_bias.reshape(feat)


def scale_kernel(
    degree_hbm, features_hbm, rows_hbm, cols_hbm, codes_hbm, out_ref, lists_ref, codes_ref,
    degree_ref, features_ref, sems
):
    slots = codes_ref.shape[0]
    first, second, *others = fetch(
        (degree_hbm, features_hbm, rows_hbm.at[0], cols_hbm.at[0], codes_hbm),
        (
            degree_ref,
            features_ref,
            lists_ref.at[0:1, 0:slots],
            lists_ref.at[1:2, 0:slots],
            codes_ref,
        ),
        sems,
    )
    first.wait()
    inv_row = lax.rsqrt(degree_ref[...].astype(jnp.float32))
    second.wait()
    out_ref[...] = (inv_row * features_ref[...].astype(jnp.float32).T).astype(jnp.bfloat16)
    for copy in others:
        copy.wait()


def scale_rows(degree, features, tile_rows, tile_cols, codes):
    pieces, feat = features.shape
    return pl.pallas_call(
        scale_kernel,
        out_shape=[
            pltpu.VMEM((feat, pieces), jnp.bfloat16),
            pltpu.VMEM((8, codes.shape[0]), jnp.int32),
            pltpu.VMEM(codes.shape, codes.dtype),
        ],
        in_specs=[pl.BlockSpec(memory_space=pl.ANY)] * 5,
        out_specs=[pl.BlockSpec(memory_space=pltpu.VMEM)] * 3,
        scratch_shapes=[
            pltpu.VMEM((1, pieces), jnp.int32),
            pltpu.VMEM((pieces, feat), jnp.bfloat16),
            pltpu.SemaphoreType.DMA((5,)),
        ],
        compiler_params=pltpu.CompilerParams(vmem_limit_bytes=60 * 2**20),
        name="scale_rows",
    )(degree.reshape(1, pieces), features, tile_rows, tile_cols, codes)


def terms_kernel(skip, *refs):
    *parts, out_ref = refs
    total = parts[0][skip:, :].astype(jnp.float32)
    for part in parts[1:]:
        total += part[skip:, :].astype(jnp.float32)
    out_ref[...] = total.astype(jnp.bfloat16)


def terms_sum(parts, skip, name):
    rows, width = parts[0].shape
    vmem = pl.BlockSpec(memory_space=pltpu.VMEM)
    return pl.pallas_call(
        functools.partial(terms_kernel, skip),
        out_shape=jax.ShapeDtypeStruct((rows - skip, width), jnp.bfloat16),
        in_specs=[vmem] * len(parts),
        out_specs=vmem,
        compiler_params=pltpu.CompilerParams(vmem_limit_bytes=LIMIT),
        name=name,
    )(*parts)


def dense_local(
    features, degree, weight, bias, cotangent, tile_rows, tile_cols, tile_count, tile_codes
):
    pieces, feat = features.shape
    n_row = lax.axis_size("row")
    n_col = lax.axis_size("col")
    grad_scale = 1.0 / math.sqrt(pieces * n_row * n_col)
    scaled, lists, codes = scale_rows(
        degree, features, tile_rows, tile_cols, tile_codes[0, 0]
    )
    chips = [6, 4, 2]
    lines = list(range(n_col - 1, 0, -1))
    landed = [swap(scaled, "row", m) for m in chips]
    sibling = swap(scaled, "row", 1)
    slots = codes.shape[0]
    middle = slots * 3 // 4 // GROUP * GROUP
    size = (pieces * n_col, pieces * n_row)
    block = build_block(lists, tile_count, codes, *size, 0, middle)
    block, landed = lax.optimization_barrier((block, landed))
    parts = [scaled, sibling, *landed, swap(stack(landed), "row", 1)]
    bits = [0, 1, *chips, *(m + 1 for m in chips)]
    block = build_block(lists, tile_count, codes, *size, middle, slots, block)
    half = max(1, n_col // 2)
    far = forward_parts(block, parts, bits, lines[:half], "forward_far")
    near = forward_parts(block, parts, bits, lines[half:] + [0], "forward_near")
    parts = dict(zip(lines + [0], [*far, *near]))
    *dense, parts[0] = lax.optimization_barrier((weight, bias, cotangent, degree, parts[0]))
    *dense, root = turn(*dense)
    landed = [parts[0]] + [swap(parts[k], "col", k) for k in lines]
    grad_own, both, aggregate = gradient_step(degree, weight, dense, landed)
    grads = [grad_own, swap(both, "col", 1)] + [swap(grad_own, "col", k) for k in range(2, n_col)]
    grads[1], aggregate = lax.optimization_barrier((grads[1], aggregate))
    hidden = hidden_step(dense[0], dense[1], aggregate)
    terms = [terms_sum([both, grads[1]], pieces, "terms_col")]
    terms += [swap(terms[0], "col", k) for k in range(2, n_col, 2)]
    begun = backward_parts(block, grads, [0, 1], range(n_row), None, [], "backward_near")
    grads[2:], begun, terms = lax.optimization_barrier((grads[2:], begun, terms))
    far = range(2, n_col)
    sent = backward_parts(block, grads, far, [7, 5], begun, terms, "backward_other")
    got = swap(sent, "row", 1)
    rest = swap(backward_parts(block, grads, far, [3, 1], begun, [], "backward_rest"), "row", 1)
    mine = backward_parts(block, grads, far, [6, 4], begun, [], "backward_own")
    chunks = pair_sum(0, mine, got, sent, got)
    landed = [swap(chunk, "row", m) for chunk, m in zip(chunks, chips)]
    mine = backward_parts(block, grads, far, [2, 0], begun, [], "backward_last")
    chunks = pair_sum(0, mine, rest, sent, got)
    landed = [chunks[1], *landed, swap(chunks[0], "row", chips[2])]
    grad_features, grad_weight, grad_bias = finish(root, landed, grad_scale)
    return (hidden, grad_features, grad_weight, grad_bias)


def solution(mesh):
    placed = (
        P(("row", "col"), None),
        P(("row", "col")),
        P(),
        P(),
        P(("row", "col"), None),
        P("row", "col", None),
        P("row", "col", None),
        P("row", "col", None),
        P("row", "col", None, None),
    )
    n_row, n_col = mesh.shape["row"], mesh.shape["col"]

    def local(features, *rest):
        block_bytes = 2 * features.shape[0] ** 2 * n_row * n_col
        paired = n_row == 8 and n_col == 4
        if paired and block_bytes <= DENSE_BYTES:
            return dense_local(features, *rest)
        return sparse_local(features, *rest)

    return jax.shard_map(
        local,
        mesh=mesh,
        in_specs=placed,
        out_specs=(P(("row", "col"), None), P(("row", "col"), None), P(), P()),
        check_vma=False,
    )
```

```python
import functools
import math

import jax
import jax.numpy as jnp
from jax import lax
from jax.experimental import pallas as pl
from jax.experimental.pallas import tpu as pltpu
from jax.sharding import PartitionSpec as P

BLOCK = 16
GROUP = 32
MOD = 4093
HIT = 64
DENSE_BYTES = 8 * 2**20
LIMIT = 16 * 2**20


def tile_mask(code_block, living):
    tile_side = code_block.shape[1] // 2
    row_code = code_block[:, :tile_side][:, :, None]
    col_code = code_block[:, tile_side:][:, None, :]
    hashed = (row_code * col_code + row_code + 3 * col_code) % MOD
    return ((hashed < HIT) & living[:, None, None]).astype(jnp.bfloat16)


def accumulate(codes_dev, rows_dev, cols_dev, count_dev, source, out_tiles, backward):
    tile_side = source.shape[1]
    width_feat = source.shape[2]

    def block_step(block_id, summed):
        slot_start = block_id * BLOCK
        code_block = lax.dynamic_slice_in_dim(codes_dev, slot_start, BLOCK, 0)
        row_block = lax.dynamic_slice_in_dim(rows_dev, slot_start, BLOCK, 0)
        col_block = lax.dynamic_slice_in_dim(cols_dev, slot_start, BLOCK, 0)
        slot_ids = slot_start + jnp.arange(BLOCK, dtype=jnp.int32)
        target = col_block if backward else row_block
        anchor = row_block if backward else col_block
        living = slot_ids < count_dev
        keep = tile_mask(code_block, living)
        picked = jnp.take(source, anchor, axis=0)
        if backward:
            product = jnp.einsum("tij,tif->tjf", keep, picked, preferred_element_type=jnp.float32)
        else:
            product = jnp.einsum("tij,tjf->tif", keep, picked, preferred_element_type=jnp.float32)
        return summed.at[target].add(product)

    start_sum = jnp.zeros((out_tiles, tile_side, width_feat), jnp.float32)
    loop_count = codes_dev.shape[0] // BLOCK
    summed = lax.fori_loop(0, loop_count, block_step, start_sum)
    return summed.reshape(out_tiles * tile_side, width_feat)


def dense_part(aggregate, weight, bias, cotangent, inv_root):
    preact = jnp.dot(aggregate, weight, preferred_element_type=jnp.float32) + bias
    hidden = jax.nn.elu(preact).astype(jnp.bfloat16)
    elu_slope = jnp.where(preact > 0, 1.0, jnp.exp(jnp.minimum(preact, 0.0)))
    grad_pre = cotangent.astype(jnp.float32) * elu_slope
    grad_pre_b = grad_pre.astype(jnp.bfloat16)
    grad_weight = lax.dot_general(
        aggregate, grad_pre_b, (((0,), (0,)), ((), ())), preferred_element_type=jnp.float32
    )
    grad_bias = jnp.sum(grad_pre, axis=0)
    grad_agg = jnp.dot(grad_pre_b, weight.T, preferred_element_type=jnp.float32)
    grad_scaled = (inv_root * grad_agg).astype(jnp.bfloat16)
    return (hidden, grad_weight, grad_bias, grad_scaled)


def sparse_local(
    features, degree, weight, bias, cotangent, tile_rows, tile_cols, tile_count, tile_codes
):
    codes_dev = tile_codes[0, 0]
    rows_dev = tile_rows[0, 0]
    cols_dev = tile_cols[0, 0]
    count_dev = tile_count[0, 0, 0]
    pieces = features.shape[0]
    width_feat = features.shape[1]
    tile_side = codes_dev.shape[1] // 2
    row_devs = lax.axis_size("row")
    col_devs = lax.axis_size("col")
    grad_scale = 1.0 / math.sqrt(pieces * row_devs * col_devs)
    row_tiles = pieces * col_devs // tile_side
    col_tiles = pieces * row_devs // tile_side
    inv_root = lax.rsqrt(degree.astype(jnp.float32))[:, None]
    scaled = (inv_root * features.astype(jnp.float32)).astype(jnp.bfloat16)
    column_feats = lax.all_gather(scaled, "row", axis=0, tiled=True).reshape(
        col_tiles, tile_side, width_feat
    )
    row_terms = accumulate(codes_dev, rows_dev, cols_dev, count_dev, column_feats, row_tiles, False)
    row_sum = lax.psum_scatter(
        row_terms.astype(jnp.bfloat16), "col", scatter_dimension=0, tiled=True
    ).astype(jnp.float32)
    aggregate = (inv_root * row_sum).astype(jnp.bfloat16)
    hidden, grad_weight, grad_bias, grads = dense_part(
        aggregate, weight, bias, cotangent, inv_root
    )
    grad_weight, grad_bias = (
        lax.psum((grad_weight * grad_scale).astype(jnp.bfloat16), ("row", "col")),
        lax.psum((grad_bias * grad_scale).astype(jnp.bfloat16), ("row", "col")),
    )
    row_sources = lax.all_gather(grads, "col", axis=0, tiled=True).reshape(
        row_tiles, tile_side, width_feat
    )
    col_terms = accumulate(codes_dev, rows_dev, cols_dev, count_dev, row_sources, col_tiles, True)
    grad_sum = lax.psum_scatter(
        col_terms.astype(jnp.bfloat16), "row", scatter_dimension=0, tiled=True
    ).astype(jnp.float32)
    grad_features = (inv_root * grad_sum).astype(jnp.bfloat16)
    return (
        hidden,
        grad_features,
        grad_weight.astype(jnp.float32),
        grad_bias.astype(jnp.float32),
    )


def swap(value, axis, bits):
    size = lax.axis_size(axis)
    return lax.ppermute(value, axis, [(i, i ^ bits) for i in range(size)])


def turned(lhs, rhs):
    return lax.dot_general(lhs, rhs, (((1,), (1,)), ((), ())), preferred_element_type=jnp.float32)


def fetch(sources, targets, sems):
    copies = [
        pltpu.make_async_copy(src, dst, sems.at[k])
        for k, (src, dst) in enumerate(zip(sources, targets))
    ]
    for copy in copies:
        copy.start()
    return copies


def build_kernel(first, last, lists_vmem, count_ref, codes_ref, *refs):
    block_ref, col_scr, row_scr, lists_ref, sems = refs[-5:]
    slots = codes_ref.shape[0]
    side = codes_ref.shape[1] // 2
    (copy,) = fetch((lists_vmem,), (lists_ref,), sems)
    if first == 0:
        block_ref[...] = jnp.zeros_like(block_ref)
    row_code = codes_ref[:, :side].astype(jnp.float32) + 3.0
    row_code = jnp.where(row_code > MOD // 2, row_code - MOD, row_code)
    col_code = codes_ref[:, side:].astype(jnp.float32) + 1.0
    col_code = jnp.where(col_code > MOD // 2, col_code - MOD, col_code)
    slot = lax.broadcasted_iota(jnp.int32, (slots, side), 0)
    col_code = jnp.where(slot < count_ref[0, 0, 0], col_code, 0.0)
    coarse = 2.0**-12
    row_scr[...] = row_code * coarse + row_code * (1.0 / MOD - coarse)
    by_side = col_code.T
    groups = range(first // GROUP, last // GROUP)
    for g in groups:
        col_scr[g] = by_side if g == 0 else pltpu.roll(by_side, slots - g * GROUP, axis=1)
    copy.wait()
    middle = (3.0 + (HIT - 1) / 2.0) / MOD
    reach = jnp.bfloat16(2.0**-7)
    one, zero = jnp.bfloat16(1.0), jnp.bfloat16(0.0)

    def step(g, carry):
        col_vals = col_scr[g]
        row_vals = row_scr[pl.ds(pl.multiple_of(g * GROUP, GROUP), GROUP), :]
        for t in range(GROUP):
            s = g * GROUP + t
            turns = jnp.broadcast_to(col_vals[:, t : t + 1], (side, side)) * jnp.broadcast_to(
                row_vals[t : t + 1, :], (side, side)
            )
            part = turns - jnp.round(turns)
            keep = jnp.abs((part - middle).astype(jnp.bfloat16)) < reach
            down = pl.ds(pl.multiple_of(lists_ref[1, s] * side, side), side)
            across = pl.ds(pl.multiple_of(lists_ref[0, s] * side, side), side)
            block_ref[down, across] += jnp.where(keep, one, zero)
        return carry

    lax.fori_loop(groups.start, groups.stop, step, 0)


def build_block(lists, tile_count, codes, row_nodes, col_nodes, first, last, block=None):
    slots, width = codes.shape
    side = width // 2
    vmem = pl.BlockSpec(memory_space=pltpu.VMEM)
    begun = [] if block is None else [block]
    return pl.pallas_call(
        functools.partial(build_kernel, first, last),
        out_shape=pltpu.VMEM((col_nodes, row_nodes), jnp.bfloat16),
        in_specs=[vmem, pl.BlockSpec(memory_space=pltpu.SMEM), vmem] + [vmem] * len(begun),
        out_specs=vmem,
        input_output_aliases={3: 0} if begun else {},
        scratch_shapes=[
            pltpu.VMEM((slots // GROUP, side, slots), jnp.float32),
            pltpu.VMEM((slots, side), jnp.float32),
            pltpu.SMEM(lists.shape, jnp.int32),
            pltpu.SemaphoreType.DMA((1,)),
        ],
        compiler_params=pltpu.CompilerParams(vmem_limit_bytes=LIMIT),
        cost_estimate=pl.CostEstimate(
            flops=20 * (last - first) * side * side, bytes_accessed=2**23, transcendentals=0
        ),
        name="build_rest" if begun else "build_block",
    )(lists, tile_count, codes, *begun)


def stack_kernel(*refs):
    *parts, out_ref = refs
    rows = parts[0].shape[0]
    for m, part in enumerate(parts):
        out_ref[m * rows : (m + 1) * rows, :] = part[...]


def stack(parts):
    rows, width = parts[0].shape
    vmem = pl.BlockSpec(memory_space=pltpu.VMEM)
    return pl.pallas_call(
        stack_kernel,
        out_shape=jax.ShapeDtypeStruct((len(parts) * rows, width), parts[0].dtype),
        in_specs=[vmem] * len(parts),
        out_specs=vmem,
        compiler_params=pltpu.CompilerParams(vmem_limit_bytes=LIMIT),
        name="stack",
    )(*parts)


def forward_kernel(bits, high, block_ref, *refs):
    *parts, even_ref, odd_ref, source = refs
    feat, pieces = even_ref.shape
    me_row = lax.axis_index("row")
    me_col = lax.axis_index("col")
    place = iter(bits)
    for part in parts:
        for m in range(part.shape[0] // feat):
            at = pl.multiple_of((me_row ^ next(place)) * pieces, pieces)
            source[:, pl.ds(at, pieces)] = part[m * feat : (m + 1) * feat, :]
    across = pl.multiple_of((me_col ^ high) // 2 * (2 * pieces), 2 * pieces)
    both = jnp.dot(
        source[...], block_ref[:, pl.ds(across, 2 * pieces)], preferred_element_type=jnp.float32
    ).astype(jnp.bfloat16)
    first = me_col % 2 == 0
    even_ref[...] = jnp.where(first, both[:, :pieces], both[:, pieces:])
    odd_ref[...] = jnp.where(first, both[:, pieces:], both[:, :pieces])


def forward_parts(block, parts, bits, high, name):
    feat, pieces = parts[0].shape
    vmem = pl.BlockSpec(memory_space=pltpu.VMEM)
    return pl.pallas_call(
        functools.partial(forward_kernel, bits, high),
        out_shape=[jax.ShapeDtypeStruct((feat, pieces), jnp.bfloat16)] * 2,
        in_specs=[vmem] * (1 + len(parts)),
        out_specs=[vmem] * 2,
        scratch_shapes=[pltpu.VMEM((feat, pieces * len(bits)), jnp.bfloat16)],
        compiler_params=pltpu.CompilerParams(vmem_limit_bytes=LIMIT),
        name=name,
    )(block, *parts)


def turn_kernel(
    weight_ref, bias_ref, cot_ref, degree_ref, weight_out, bias_out, cot_out, root_out
):
    feat, pieces = cot_out.shape
    weight_out[...] = weight_ref[...].T
    bias_out[...] = jnp.broadcast_to(bias_ref[...], (feat, feat)).T
    cot_out[...] = cot_ref[...].T
    inv_row = lax.rsqrt(degree_ref[...].astype(jnp.float32))
    root_out[...] = jnp.broadcast_to(inv_row, (feat, pieces)).T


def turn(weight, bias, cotangent, degree):
    pieces, feat = cotangent.shape
    vmem = pl.BlockSpec(memory_space=pltpu.VMEM)
    return pl.pallas_call(
        turn_kernel,
        out_shape=[
            jax.ShapeDtypeStruct((feat, feat), jnp.bfloat16),
            jax.ShapeDtypeStruct((feat, feat), jnp.float32),
            jax.ShapeDtypeStruct((feat, pieces), jnp.bfloat16),
            jax.ShapeDtypeStruct((pieces, feat), jnp.float32),
        ],
        in_specs=[vmem] * 4,
        out_specs=[vmem] * 4,
        compiler_params=pltpu.CompilerParams(vmem_limit_bytes=LIMIT),
        name="turn",
    )(weight, bias.reshape(1, feat), cotangent, degree.reshape(1, pieces))


def preact_of(aggregate, weight_turned, bias_turned):
    repeats = aggregate.shape[1] // bias_turned.shape[1]
    bias = jnp.concatenate([bias_turned] * repeats, axis=1)
    return jnp.dot(weight_turned, aggregate, preferred_element_type=jnp.float32) + bias


def gradient_kernel(n_col, degree_ref, weight_ref, turned_ref, bias_ref, cot_ref, *refs):
    grad_ref, both_ref, aggregate_ref = refs[n_col:]
    inv_row = lax.rsqrt(degree_ref[...].astype(jnp.float32))
    aggregate = (inv_row * sum_of(refs[:n_col])).astype(jnp.bfloat16)
    aggregate_ref[...] = aggregate
    feat = weight_ref.shape[0]
    preact = preact_of(aggregate, turned_ref[...], bias_ref[...])
    slope = jnp.where(preact > 0, 1.0, jnp.exp(jnp.minimum(preact, 0.0)))
    grad_pre = cot_ref[...].astype(jnp.float32) * slope
    grad = lax.dot_general(
        (inv_row * grad_pre).astype(jnp.bfloat16),
        weight_ref[...],
        (((0,), (1,)), ((), ())),
        preferred_element_type=jnp.float32,
    ).astype(jnp.bfloat16)
    pieces = grad.shape[0]
    grad_ref[...] = grad
    both_ref[:pieces, :] = grad
    grad_pre_b = grad_pre.astype(jnp.bfloat16)
    both_ref[pieces : pieces + feat, :] = turned(aggregate, grad_pre_b).astype(jnp.bfloat16)
    ones = jnp.ones((16, pieces), jnp.bfloat16)
    rest = (grad_pre - grad_pre_b.astype(jnp.float32)).astype(jnp.bfloat16)
    both_ref[pieces + feat :, :] = (turned(ones, grad_pre_b) + turned(ones, rest)).astype(
        jnp.bfloat16
    )


def gradient_step(degree, weight, turned_operands, parts):
    feat, pieces = parts[0].shape
    vmem = pl.BlockSpec(memory_space=pltpu.VMEM)
    return pl.pallas_call(
        functools.partial(gradient_kernel, len(parts)),
        out_shape=[
            jax.ShapeDtypeStruct((pieces, feat), jnp.bfloat16),
            jax.ShapeDtypeStruct((pieces + feat + 16, feat), jnp.bfloat16),
            jax.ShapeDtypeStruct((feat, pieces), jnp.bfloat16),
        ],
        in_specs=[vmem] * (5 + len(parts)),
        out_specs=[vmem] * 3,
        compiler_params=pltpu.CompilerParams(vmem_limit_bytes=LIMIT),
        name="gradient_step",
    )(degree.reshape(1, pieces), weight, *turned_operands, *parts)


def hidden_kernel(turned_ref, bias_ref, aggregate_ref, hidden_ref):
    preact = preact_of(aggregate_ref[...], turned_ref[...], bias_ref[...])
    hidden = jnp.where(preact > 0, preact, jnp.exp(jnp.minimum(preact, 0.0)) - 1.0)
    hidden_ref[...] = hidden.astype(jnp.bfloat16).T


def hidden_step(weight_turned, bias_turned, aggregate):
    feat, pieces = aggregate.shape
    vmem = pl.BlockSpec(memory_space=pltpu.VMEM)
    return pl.pallas_call(
        hidden_kernel,
        out_shape=jax.ShapeDtypeStruct((pieces, feat), jnp.bfloat16),
        in_specs=[vmem] * 3,
        out_specs=vmem,
        compiler_params=pltpu.CompilerParams(vmem_limit_bytes=LIMIT),
        name="hidden_step",
    )(weight_turned, bias_turned, aggregate)


def sum_of(refs):
    total = refs[0][...].astype(jnp.float32)
    for ref in refs[1:]:
        total += ref[...].astype(jnp.float32)
    return total


def backward_kernel(pieces, kinds, chunks, begun, block_ref, *refs):
    sources, out_ref = refs[: len(kinds)], refs[-1]
    terms = refs[len(kinds) + begun : -1]
    feat = out_ref.shape[1]
    me_row = lax.axis_index("row")
    me_col = lax.axis_index("col")
    for m, chunk in enumerate(chunks):
        down = pl.ds(pl.multiple_of((me_row ^ chunk) * pieces, pieces), pieces)
        if begun:
            total = refs[len(kinds)][chunk * pieces : (chunk + 1) * pieces, :]
        else:
            total = jnp.zeros((pieces, feat), jnp.float32)
        for k, source in zip(kinds, sources):
            across = pl.ds(pl.multiple_of((me_col ^ k) * pieces, pieces), pieces)
            total += jnp.dot(
                block_ref[down, across], source[:pieces, :], preferred_element_type=jnp.float32
            )
        out_ref[m * pieces : (m + 1) * pieces, :] = total.astype(out_ref.dtype)
    if terms:
        out_ref[len(chunks) * pieces :, :] = sum_of(terms).astype(out_ref.dtype)


def backward_parts(block, sources, kinds, chunks, begun, terms, name):
    pieces, feat = sources[0].shape
    begun = [] if begun is None else [begun]
    extra = terms[0].shape[0] if terms else 0
    vmem = pl.BlockSpec(memory_space=pltpu.VMEM)
    dtype = jnp.bfloat16 if begun else jnp.float32
    return pl.pallas_call(
        functools.partial(backward_kernel, pieces, kinds, chunks, len(begun)),
        out_shape=jax.ShapeDtypeStruct((len(chunks) * pieces + extra, feat), dtype),
        in_specs=[vmem] * (1 + len(kinds) + len(begun) + len(terms)),
        out_specs=vmem,
        compiler_params=pltpu.CompilerParams(vmem_limit_bytes=LIMIT),
        name=name,
    )(block, *(sources[k] for k in kinds), *begun, *terms)


def pair_kernel(first, mine_ref, theirs_ref, sent_ref, got_ref, *outs):
    feat = mine_ref.shape[0] // 2
    terms = sum_of((sent_ref.at[2 * feat :], got_ref.at[2 * feat :])).astype(jnp.bfloat16)
    for m, out in enumerate(outs):
        mine = mine_ref[(first + m) * feat : (first + m + 1) * feat, :].astype(jnp.float32)
        theirs = theirs_ref[m * feat : (m + 1) * feat, :].astype(jnp.float32)
        out[:feat, :] = (mine + theirs).astype(jnp.bfloat16)
        out[feat:, :] = terms


def pair_sum(first, mine, theirs, sent, got):
    vmem = pl.BlockSpec(memory_space=pltpu.VMEM)
    rows = sent.shape[0] - mine.shape[0] // 2
    return pl.pallas_call(
        functools.partial(pair_kernel, first),
        out_shape=[jax.ShapeDtypeStruct((rows, mine.shape[1]), jnp.bfloat16)] * 2,
        in_specs=[vmem] * 4,
        out_specs=[vmem] * 2,
        compiler_params=pltpu.CompilerParams(vmem_limit_bytes=LIMIT),
        name="pair_near" if first else "pair_far",
    )(mine, theirs, sent, got)


def finish_kernel(scale, root_ref, *refs):
    *parts, out_ref, weight_ref, bias_ref = refs
    total = sum_of(parts)
    pieces, feat = out_ref.shape
    out_ref[...] = (root_ref[...] * total[:pieces]).astype(jnp.bfloat16)
    weight_ref[...] = total[pieces : pieces + feat] * scale
    bias_ref[...] = total[pieces + feat : pieces + feat + 1] * scale


def finish(root, parts, scale):
    pieces, feat = root.shape
    vmem = pl.BlockSpec(memory_space=pltpu.VMEM)
    grad_features, grad_weight, grad_bias = pl.pallas_call(
        functools.partial(finish_kernel, scale),
        out_shape=[
            jax.ShapeDtypeStruct((pieces, feat), jnp.bfloat16),
            jax.ShapeDtypeStruct((feat, feat), jnp.float32),
            jax.ShapeDtypeStruct((1, feat), jnp.float32),
        ],
        in_specs=[vmem] * (1 + len(parts)),
        out_specs=[vmem] * 3,
        compiler_params=pltpu.CompilerParams(vmem_limit_bytes=LIMIT),
        name="finish",
    )(root, *parts)
    return grad_features, grad_weight, grad_bias.reshape(feat)


def scale_kernel(
    degree_hbm, features_hbm, rows_hbm, cols_hbm, codes_hbm, out_ref, lists_ref, codes_ref,
    degree_ref, features_ref, sems
):
    slots = codes_ref.shape[0]
    first, second, *others = fetch(
        (degree_hbm, features_hbm, rows_hbm.at[0], cols_hbm.at[0], codes_hbm),
        (
            degree_ref,
            features_ref,
            lists_ref.at[0:1, 0:slots],
            lists_ref.at[1:2, 0:slots],
            codes_ref,
        ),
        sems,
    )
    first.wait()
    inv_row = lax.rsqrt(degree_ref[...].astype(jnp.float32))
    second.wait()
    out_ref[...] = (inv_row * features_ref[...].astype(jnp.float32).T).astype(jnp.bfloat16)
    for copy in others:
        copy.wait()


def scale_rows(degree, features, tile_rows, tile_cols, codes):
    pieces, feat = features.shape
    return pl.pallas_call(
        scale_kernel,
        out_shape=[
            pltpu.VMEM((feat, pieces), jnp.bfloat16),
            pltpu.VMEM((8, codes.shape[0]), jnp.int32),
            pltpu.VMEM(codes.shape, codes.dtype),
        ],
        in_specs=[pl.BlockSpec(memory_space=pl.ANY)] * 5,
        out_specs=[pl.BlockSpec(memory_space=pltpu.VMEM)] * 3,
        scratch_shapes=[
            pltpu.VMEM((1, pieces), jnp.int32),
            pltpu.VMEM((pieces, feat), jnp.bfloat16),
            pltpu.SemaphoreType.DMA((5,)),
        ],
        compiler_params=pltpu.CompilerParams(vmem_limit_bytes=60 * 2**20),
        name="scale_rows",
    )(degree.reshape(1, pieces), features, tile_rows, tile_cols, codes)


def terms_kernel(skip, *refs):
    *parts, out_ref = refs
    total = parts[0][skip:, :].astype(jnp.float32)
    for part in parts[1:]:
        total += part[skip:, :].astype(jnp.float32)
    out_ref[...] = total.astype(jnp.bfloat16)


def terms_sum(parts, skip, name):
    rows, width = parts[0].shape
    vmem = pl.BlockSpec(memory_space=pltpu.VMEM)
    return pl.pallas_call(
        functools.partial(terms_kernel, skip),
        out_shape=jax.ShapeDtypeStruct((rows - skip, width), jnp.bfloat16),
        in_specs=[vmem] * len(parts),
        out_specs=vmem,
        compiler_params=pltpu.CompilerParams(vmem_limit_bytes=LIMIT),
        name=name,
    )(*parts)


def dense_local(
    features, degree, weight, bias, cotangent, tile_rows, tile_cols, tile_count, tile_codes
):
    pieces, feat = features.shape
    n_row = lax.axis_size("row")
    n_col = lax.axis_size("col")
    grad_scale = 1.0 / math.sqrt(pieces * n_row * n_col)
    scaled, lists, codes = scale_rows(
        degree, features, tile_rows, tile_cols, tile_codes[0, 0]
    )
    chips = [6, 4, 2]
    lines = list(range(n_col - 1, 0, -1))
    landed = [swap(scaled, "row", m) for m in chips]
    sibling = swap(scaled, "row", 1)
    slots = codes.shape[0]
    middle = slots * 3 // 4 // GROUP * GROUP
    size = (pieces * n_col, pieces * n_row)
    block = build_block(lists, tile_count, codes, *size, 0, middle)
    block, landed = lax.optimization_barrier((block, landed))
    parts = [scaled, sibling, *landed, swap(stack(landed), "row", 1)]
    bits = [0, 1, *chips, *(m + 1 for m in chips)]
    block = build_block(lists, tile_count, codes, *size, middle, slots, block)
    far = forward_parts(block, parts, bits, 2, "forward_far")
    near = forward_parts(block, parts, bits, 0, "forward_near")
    parts = [*near, *far]
    *dense, parts[0] = lax.optimization_barrier((weight, bias, cotangent, degree, parts[0]))
    *dense, root = turn(*dense)
    landed = [parts[0]] + [swap(parts[k], "col", k) for k in lines]
    grad_own, both, aggregate = gradient_step(degree, weight, dense, landed)
    grads = [grad_own, swap(both, "col", 1)] + [swap(grad_own, "col", k) for k in range(2, n_col)]
    grads[1], aggregate = lax.optimization_barrier((grads[1], aggregate))
    hidden = hidden_step(dense[0], dense[1], aggregate)
    terms = [terms_sum([both, grads[1]], pieces, "terms_col")]
    terms += [swap(terms[0], "col", k) for k in range(2, n_col, 2)]
    begun = backward_parts(block, grads, [0, 1], range(n_row), None, [], "backward_near")
    grads[2:], begun, terms = lax.optimization_barrier((grads[2:], begun, terms))
    far = range(2, n_col)
    sent = backward_parts(block, grads, far, [7, 5], begun, terms, "backward_other")
    got = swap(sent, "row", 1)
    rest = swap(backward_parts(block, grads, far, [3, 1], begun, [], "backward_rest"), "row", 1)
    mine = backward_parts(block, grads, far, [6, 4], begun, [], "backward_own")
    chunks = pair_sum(0, mine, got, sent, got)
    landed = [swap(chunk, "row", m) for chunk, m in zip(chunks, chips)]
    mine = backward_parts(block, grads, far, [2, 0], begun, [], "backward_last")
    chunks = pair_sum(0, mine, rest, sent, got)
    landed = [chunks[1], *landed, swap(chunks[0], "row", chips[2])]
    grad_features, grad_weight, grad_bias = finish(root, landed, grad_scale)
    return (hidden, grad_features, grad_weight, grad_bias)


def solution(mesh):
    placed = (
        P(("row", "col"), None),
        P(("row", "col")),
        P(),
        P(),
        P(("row", "col"), None),
        P("row", "col", None),
        P("row", "col", None),
        P("row", "col", None),
        P("row", "col", None, None),
    )
    n_row, n_col = mesh.shape["row"], mesh.shape["col"]

    def local(features, *rest):
        block_bytes = 2 * features.shape[0] ** 2 * n_row * n_col
        paired = n_row == 8 and n_col == 4
        if paired and block_bytes <= DENSE_BYTES:
            return dense_local(features, *rest)
        return sparse_local(features, *rest)

    return jax.shard_map(
        local,
        mesh=mesh,
        in_specs=placed,
        out_specs=(P(("row", "col"), None), P(("row", "col"), None), P(), P()),
        check_vma=False,
    )
```

```python
import functools
import math

import jax
import jax.numpy as jnp
from jax import lax
from jax.experimental import pallas as pl
from jax.experimental.pallas import tpu as pltpu
from jax.sharding import PartitionSpec as P

BLOCK = 16
GROUP = 16
MOD = 4093
HIT = 64
DENSE_BYTES = 8 * 2**20
LIMIT = 16 * 2**20


def tile_mask(code_block, living):
    tile_side = code_block.shape[1] // 2
    row_code = code_block[:, :tile_side][:, :, None]
    col_code = code_block[:, tile_side:][:, None, :]
    hashed = (row_code * col_code + row_code + 3 * col_code) % MOD
    return ((hashed < HIT) & living[:, None, None]).astype(jnp.bfloat16)


def accumulate(codes_dev, rows_dev, cols_dev, count_dev, source, out_tiles, backward):
    tile_side = source.shape[1]
    width_feat = source.shape[2]

    def block_step(block_id, summed):
        slot_start = block_id * BLOCK
        code_block = lax.dynamic_slice_in_dim(codes_dev, slot_start, BLOCK, 0)
        row_block = lax.dynamic_slice_in_dim(rows_dev, slot_start, BLOCK, 0)
        col_block = lax.dynamic_slice_in_dim(cols_dev, slot_start, BLOCK, 0)
        slot_ids = slot_start + jnp.arange(BLOCK, dtype=jnp.int32)
        target = col_block if backward else row_block
        anchor = row_block if backward else col_block
        living = slot_ids < count_dev
        keep = tile_mask(code_block, living)
        picked = jnp.take(source, anchor, axis=0)
        if backward:
            product = jnp.einsum("tij,tif->tjf", keep, picked, preferred_element_type=jnp.float32)
        else:
            product = jnp.einsum("tij,tjf->tif", keep, picked, preferred_element_type=jnp.float32)
        return summed.at[target].add(product)

    start_sum = jnp.zeros((out_tiles, tile_side, width_feat), jnp.float32)
    loop_count = codes_dev.shape[0] // BLOCK
    summed = lax.fori_loop(0, loop_count, block_step, start_sum)
    return summed.reshape(out_tiles * tile_side, width_feat)


def dense_part(aggregate, weight, bias, cotangent, inv_root):
    preact = jnp.dot(aggregate, weight, preferred_element_type=jnp.float32) + bias
    hidden = jax.nn.elu(preact).astype(jnp.bfloat16)
    elu_slope = jnp.where(preact > 0, 1.0, jnp.exp(jnp.minimum(preact, 0.0)))
    grad_pre = cotangent.astype(jnp.float32) * elu_slope
    grad_pre_b = grad_pre.astype(jnp.bfloat16)
    grad_weight = lax.dot_general(
        aggregate, grad_pre_b, (((0,), (0,)), ((), ())), preferred_element_type=jnp.float32
    )
    grad_bias = jnp.sum(grad_pre, axis=0)
    grad_agg = jnp.dot(grad_pre_b, weight.T, preferred_element_type=jnp.float32)
    grad_scaled = (inv_root * grad_agg).astype(jnp.bfloat16)
    return (hidden, grad_weight, grad_bias, grad_scaled)


def sparse_local(
    features, degree, weight, bias, cotangent, tile_rows, tile_cols, tile_count, tile_codes
):
    codes_dev = tile_codes[0, 0]
    rows_dev = tile_rows[0, 0]
    cols_dev = tile_cols[0, 0]
    count_dev = tile_count[0, 0, 0]
    pieces = features.shape[0]
    width_feat = features.shape[1]
    tile_side = codes_dev.shape[1] // 2
    row_devs = lax.axis_size("row")
    col_devs = lax.axis_size("col")
    grad_scale = 1.0 / math.sqrt(pieces * row_devs * col_devs)
    row_tiles = pieces * col_devs // tile_side
    col_tiles = pieces * row_devs // tile_side
    inv_root = lax.rsqrt(degree.astype(jnp.float32))[:, None]
    scaled = (inv_root * features.astype(jnp.float32)).astype(jnp.bfloat16)
    column_feats = lax.all_gather(scaled, "row", axis=0, tiled=True).reshape(
        col_tiles, tile_side, width_feat
    )
    row_terms = accumulate(codes_dev, rows_dev, cols_dev, count_dev, column_feats, row_tiles, False)
    row_sum = lax.psum_scatter(
        row_terms.astype(jnp.bfloat16), "col", scatter_dimension=0, tiled=True
    ).astype(jnp.float32)
    aggregate = (inv_root * row_sum).astype(jnp.bfloat16)
    hidden, grad_weight, grad_bias, grads = dense_part(
        aggregate, weight, bias, cotangent, inv_root
    )
    grad_weight, grad_bias = (
        lax.psum((grad_weight * grad_scale).astype(jnp.bfloat16), ("row", "col")),
        lax.psum((grad_bias * grad_scale).astype(jnp.bfloat16), ("row", "col")),
    )
    row_sources = lax.all_gather(grads, "col", axis=0, tiled=True).reshape(
        row_tiles, tile_side, width_feat
    )
    col_terms = accumulate(codes_dev, rows_dev, cols_dev, count_dev, row_sources, col_tiles, True)
    grad_sum = lax.psum_scatter(
        col_terms.astype(jnp.bfloat16), "row", scatter_dimension=0, tiled=True
    ).astype(jnp.float32)
    grad_features = (inv_root * grad_sum).astype(jnp.bfloat16)
    return (
        hidden,
        grad_features,
        grad_weight.astype(jnp.float32),
        grad_bias.astype(jnp.float32),
    )


def swap(value, axis, bits):
    size = lax.axis_size(axis)
    return lax.ppermute(value, axis, [(i, i ^ bits) for i in range(size)])


def turned(lhs, rhs):
    return lax.dot_general(lhs, rhs, (((1,), (1,)), ((), ())), preferred_element_type=jnp.float32)


def fetch(sources, targets, sems):
    copies = [
        pltpu.make_async_copy(src, dst, sems.at[k])
        for k, (src, dst) in enumerate(zip(sources, targets))
    ]
    for copy in copies:
        copy.start()
    return copies


def build_kernel(first, last, lists_vmem, count_ref, codes_ref, *refs):
    block_ref, col_scr, row_scr, lists_ref, sems = refs[-5:]
    slots = codes_ref.shape[0]
    side = codes_ref.shape[1] // 2
    (copy,) = fetch((lists_vmem,), (lists_ref,), sems)
    if first == 0:
        block_ref[...] = jnp.zeros_like(block_ref)
    row_code = codes_ref[:, :side].astype(jnp.float32) + 3.0
    row_code = jnp.where(row_code > MOD // 2, row_code - MOD, row_code)
    col_code = codes_ref[:, side:].astype(jnp.float32) + 1.0
    col_code = jnp.where(col_code > MOD // 2, col_code - MOD, col_code)
    slot = lax.broadcasted_iota(jnp.int32, (slots, side), 0)
    col_code = jnp.where(slot < count_ref[0, 0, 0], col_code, 0.0)
    coarse = 2.0**-12
    row_scr[...] = row_code * coarse + row_code * (1.0 / MOD - coarse)
    by_side = col_code.T
    groups = range(first // GROUP, last // GROUP)
    for g in groups:
        col_scr[g] = by_side if g == 0 else pltpu.roll(by_side, slots - g * GROUP, axis=1)
    copy.wait()
    middle = (3.0 + (HIT - 1) / 2.0) / MOD
    reach = jnp.bfloat16(2.0**-7)
    one, zero = jnp.bfloat16(1.0), jnp.bfloat16(0.0)

    def step(g, carry):
        col_vals = col_scr[g]
        row_vals = row_scr[pl.ds(pl.multiple_of(g * GROUP, GROUP), GROUP), :]
        for t in range(GROUP):
            s = g * GROUP + t
            turns = jnp.broadcast_to(col_vals[:, t : t + 1], (side, side)) * jnp.broadcast_to(
                row_vals[t : t + 1, :], (side, side)
            )
            part = turns - jnp.round(turns)
            keep = jnp.abs((part - middle).astype(jnp.bfloat16)) < reach
            down = pl.ds(pl.multiple_of(lists_ref[1, s] * side, side), side)
            across = pl.ds(pl.multiple_of(lists_ref[0, s] * side, side), side)
            block_ref[down, across] += jnp.where(keep, one, zero)
        return carry

    lax.fori_loop(groups.start, groups.stop, step, 0)


def build_block(lists, tile_count, codes, row_nodes, col_nodes, first, last, block=None):
    slots, width = codes.shape
    side = width // 2
    vmem = pl.BlockSpec(memory_space=pltpu.VMEM)
    begun = [] if block is None else [block]
    return pl.pallas_call(
        functools.partial(build_kernel, first, last),
        out_shape=pltpu.VMEM((col_nodes, row_nodes), jnp.bfloat16),
        in_specs=[vmem, pl.BlockSpec(memory_space=pltpu.SMEM), vmem] + [vmem] * len(begun),
        out_specs=vmem,
        input_output_aliases={3: 0} if begun else {},
        scratch_shapes=[
            pltpu.VMEM((slots // GROUP, side, slots), jnp.float32),
            pltpu.VMEM((slots, side), jnp.float32),
            pltpu.SMEM(lists.shape, jnp.int32),
            pltpu.SemaphoreType.DMA((1,)),
        ],
        compiler_params=pltpu.CompilerParams(vmem_limit_bytes=LIMIT),
        cost_estimate=pl.CostEstimate(
            flops=20 * (last - first) * side * side, bytes_accessed=2**23, transcendentals=0
        ),
        name="build_rest" if begun else "build_block",
    )(lists, tile_count, codes, *begun)


def stack_kernel(*refs):
    *parts, out_ref = refs
    rows = parts[0].shape[0]
    for m, part in enumerate(parts):
        out_ref[m * rows : (m + 1) * rows, :] = part[...]


def stack(parts):
    rows, width = parts[0].shape
    vmem = pl.BlockSpec(memory_space=pltpu.VMEM)
    return pl.pallas_call(
        stack_kernel,
        out_shape=jax.ShapeDtypeStruct((len(parts) * rows, width), parts[0].dtype),
        in_specs=[vmem] * len(parts),
        out_specs=vmem,
        compiler_params=pltpu.CompilerParams(vmem_limit_bytes=LIMIT),
        name="stack",
    )(*parts)


def forward_kernel(bits, far, block_ref, *refs):
    outs = refs[len(refs) - len(far) :]
    parts = refs[: len(refs) - len(far)]
    feat, pieces = parts[0].shape
    me_row = lax.axis_index("row")
    me_col = lax.axis_index("col")
    for out, k in zip(outs, far):
        across = pl.ds(pl.multiple_of((me_col ^ k) * pieces, pieces), pieces)
        total = jnp.zeros((feat, pieces), jnp.float32)
        place = iter(bits)
        for part in parts:
            for m in range(part.shape[0] // feat):
                down = pl.ds(pl.multiple_of((me_row ^ next(place)) * pieces, pieces), pieces)
                total += jnp.dot(
                    part[m * feat : (m + 1) * feat, :],
                    block_ref[down, across],
                    preferred_element_type=jnp.float32,
                )
        out[...] = total.astype(jnp.bfloat16)


def forward_parts(block, parts, bits, far, name):
    feat, pieces = parts[0].shape
    vmem = pl.BlockSpec(memory_space=pltpu.VMEM)
    return pl.pallas_call(
        functools.partial(forward_kernel, bits, far),
        out_shape=[jax.ShapeDtypeStruct((feat, pieces), jnp.bfloat16)] * len(far),
        in_specs=[vmem] * (1 + len(parts)),
        out_specs=[vmem] * len(far),
        compiler_params=pltpu.CompilerParams(vmem_limit_bytes=LIMIT),
        name=name,
    )(block, *parts)


def turn_kernel(
    weight_ref, bias_ref, cot_ref, degree_ref, weight_out, bias_out, cot_out, root_out
):
    feat, pieces = cot_out.shape
    weight_out[...] = weight_ref[...].T
    bias_out[...] = jnp.broadcast_to(bias_ref[...], (feat, feat)).T
    cot_out[...] = cot_ref[...].T
    inv_row = lax.rsqrt(degree_ref[...].astype(jnp.float32))
    root_out[...] = jnp.broadcast_to(inv_row, (feat, pieces)).T


def turn(weight, bias, cotangent, degree):
    pieces, feat = cotangent.shape
    vmem = pl.BlockSpec(memory_space=pltpu.VMEM)
    return pl.pallas_call(
        turn_kernel,
        out_shape=[
            jax.ShapeDtypeStruct((feat, feat), jnp.bfloat16),
            jax.ShapeDtypeStruct((feat, feat), jnp.float32),
            jax.ShapeDtypeStruct((feat, pieces), jnp.bfloat16),
            jax.ShapeDtypeStruct((pieces, feat), jnp.float32),
        ],
        in_specs=[vmem] * 4,
        out_specs=[vmem] * 4,
        compiler_params=pltpu.CompilerParams(vmem_limit_bytes=LIMIT),
        name="turn",
    )(weight, bias.reshape(1, feat), cotangent, degree.reshape(1, pieces))


def preact_of(aggregate, weight_turned, bias_turned):
    repeats = aggregate.shape[1] // bias_turned.shape[1]
    bias = jnp.concatenate([bias_turned] * repeats, axis=1)
    return jnp.dot(weight_turned, aggregate, preferred_element_type=jnp.float32) + bias


def gradient_kernel(n_col, degree_ref, weight_ref, turned_ref, bias_ref, cot_ref, *refs):
    grad_ref, both_ref, aggregate_ref = refs[n_col:]
    inv_row = lax.rsqrt(degree_ref[...].astype(jnp.float32))
    aggregate = (inv_row * sum_of(refs[:n_col])).astype(jnp.bfloat16)
    aggregate_ref[...] = aggregate
    feat = weight_ref.shape[0]
    preact = preact_of(aggregate, turned_ref[...], bias_ref[...])
    slope = jnp.where(preact > 0, 1.0, jnp.exp(jnp.minimum(preact, 0.0)))
    grad_pre = cot_ref[...].astype(jnp.float32) * slope
    grad = lax.dot_general(
        (inv_row * grad_pre).astype(jnp.bfloat16),
        weight_ref[...],
        (((0,), (1,)), ((), ())),
        preferred_element_type=jnp.float32,
    ).astype(jnp.bfloat16)
    pieces = grad.shape[0]
    grad_ref[...] = grad
    both_ref[:pieces, :] = grad
    grad_pre_b = grad_pre.astype(jnp.bfloat16)
    both_ref[pieces : pieces + feat, :] = turned(aggregate, grad_pre_b).astype(jnp.bfloat16)
    ones = jnp.ones((16, pieces), jnp.bfloat16)
    rest = (grad_pre - grad_pre_b.astype(jnp.float32)).astype(jnp.bfloat16)
    both_ref[pieces + feat :, :] = (turned(ones, grad_pre_b) + turned(ones, rest)).astype(
        jnp.bfloat16
    )


def gradient_step(degree, weight, turned_operands, parts):
    feat, pieces = parts[0].shape
    vmem = pl.BlockSpec(memory_space=pltpu.VMEM)
    return pl.pallas_call(
        functools.partial(gradient_kernel, len(parts)),
        out_shape=[
            jax.ShapeDtypeStruct((pieces, feat), jnp.bfloat16),
            jax.ShapeDtypeStruct((pieces + feat + 16, feat), jnp.bfloat16),
            jax.ShapeDtypeStruct((feat, pieces), jnp.bfloat16),
        ],
        in_specs=[vmem] * (5 + len(parts)),
        out_specs=[vmem] * 3,
        compiler_params=pltpu.CompilerParams(vmem_limit_bytes=LIMIT),
        name="gradient_step",
    )(degree.reshape(1, pieces), weight, *turned_operands, *parts)


def hidden_kernel(turned_ref, bias_ref, aggregate_ref, hidden_ref):
    preact = preact_of(aggregate_ref[...], turned_ref[...], bias_ref[...])
    hidden = jnp.where(preact > 0, preact, jnp.exp(jnp.minimum(preact, 0.0)) - 1.0)
    hidden_ref[...] = hidden.astype(jnp.bfloat16).T


def hidden_step(weight_turned, bias_turned, aggregate):
    feat, pieces = aggregate.shape
    vmem = pl.BlockSpec(memory_space=pltpu.VMEM)
    return pl.pallas_call(
        hidden_kernel,
        out_shape=jax.ShapeDtypeStruct((pieces, feat), jnp.bfloat16),
        in_specs=[vmem] * 3,
        out_specs=vmem,
        compiler_params=pltpu.CompilerParams(vmem_limit_bytes=LIMIT),
        name="hidden_step",
    )(weight_turned, bias_turned, aggregate)


def sum_of(refs):
    total = refs[0][...].astype(jnp.float32)
    for ref in refs[1:]:
        total += ref[...].astype(jnp.float32)
    return total


def backward_kernel(pieces, kinds, chunks, begun, block_ref, *refs):
    sources, out_ref = refs[: len(kinds)], refs[-1]
    terms = refs[len(kinds) + begun : -1]
    feat = out_ref.shape[1]
    me_row = lax.axis_index("row")
    me_col = lax.axis_index("col")
    for m, chunk in enumerate(chunks):
        down = pl.ds(pl.multiple_of((me_row ^ chunk) * pieces, pieces), pieces)
        if begun:
            total = refs[len(kinds)][chunk * pieces : (chunk + 1) * pieces, :]
        else:
            total = jnp.zeros((pieces, feat), jnp.float32)
        for k, source in zip(kinds, sources):
            across = pl.ds(pl.multiple_of((me_col ^ k) * pieces, pieces), pieces)
            total += jnp.dot(
                block_ref[down, across], source[:pieces, :], preferred_element_type=jnp.float32
            )
        out_ref[m * pieces : (m + 1) * pieces, :] = total.astype(out_ref.dtype)
    if terms:
        out_ref[len(chunks) * pieces :, :] = sum_of(terms).astype(out_ref.dtype)


def backward_parts(block, sources, kinds, chunks, begun, terms, name):
    pieces, feat = sources[0].shape
    begun = [] if begun is None else [begun]
    extra = terms[0].shape[0] if terms else 0
    vmem = pl.BlockSpec(memory_space=pltpu.VMEM)
    dtype = jnp.bfloat16 if begun else jnp.float32
    return pl.pallas_call(
        functools.partial(backward_kernel, pieces, kinds, chunks, len(begun)),
        out_shape=jax.ShapeDtypeStruct((len(chunks) * pieces + extra, feat), dtype),
        in_specs=[vmem] * (1 + len(kinds) + len(begun) + len(terms)),
        out_specs=vmem,
        compiler_params=pltpu.CompilerParams(vmem_limit_bytes=LIMIT),
        name=name,
    )(block, *(sources[k] for k in kinds), *begun, *terms)


def pair_kernel(first, mine_ref, theirs_ref, sent_ref, got_ref, *outs):
    feat = mine_ref.shape[0] // 2
    terms = sum_of((sent_ref.at[2 * feat :], got_ref.at[2 * feat :])).astype(jnp.bfloat16)
    for m, out in enumerate(outs):
        mine = mine_ref[(first + m) * feat : (first + m + 1) * feat, :].astype(jnp.float32)
        theirs = theirs_ref[m * feat : (m + 1) * feat, :].astype(jnp.float32)
        out[:feat, :] = (mine + theirs).astype(jnp.bfloat16)
        out[feat:, :] = terms


def pair_sum(first, mine, theirs, sent, got):
    vmem = pl.BlockSpec(memory_space=pltpu.VMEM)
    rows = sent.shape[0] - mine.shape[0] // 2
    return pl.pallas_call(
        functools.partial(pair_kernel, first),
        out_shape=[jax.ShapeDtypeStruct((rows, mine.shape[1]), jnp.bfloat16)] * 2,
        in_specs=[vmem] * 4,
        out_specs=[vmem] * 2,
        compiler_params=pltpu.CompilerParams(vmem_limit_bytes=LIMIT),
        name="pair_near" if first else "pair_far",
    )(mine, theirs, sent, got)


def finish_kernel(scale, root_ref, *refs):
    *parts, out_ref, weight_ref, bias_ref = refs
    total = sum_of(parts)
    pieces, feat = out_ref.shape
    out_ref[...] = (root_ref[...] * total[:pieces]).astype(jnp.bfloat16)
    weight_ref[...] = total[pieces : pieces + feat] * scale
    bias_ref[...] = total[pieces + feat : pieces + feat + 1] * scale


def finish(root, parts, scale):
    pieces, feat = root.shape
    vmem = pl.BlockSpec(memory_space=pltpu.VMEM)
    grad_features, grad_weight, grad_bias = pl.pallas_call(
        functools.partial(finish_kernel, scale),
        out_shape=[
            jax.ShapeDtypeStruct((pieces, feat), jnp.bfloat16),
            jax.ShapeDtypeStruct((feat, feat), jnp.float32),
            jax.ShapeDtypeStruct((1, feat), jnp.float32),
        ],
        in_specs=[vmem] * (1 + len(parts)),
        out_specs=[vmem] * 3,
        compiler_params=pltpu.CompilerParams(vmem_limit_bytes=LIMIT),
        name="finish",
    )(root, *parts)
    return grad_features, grad_weight, grad_bias.reshape(feat)


def scale_kernel(
    degree_hbm, features_hbm, rows_hbm, cols_hbm, codes_hbm, out_ref, lists_ref, codes_ref,
    degree_ref, features_ref, sems
):
    slots = codes_ref.shape[0]
    first, second, *others = fetch(
        (degree_hbm, features_hbm, rows_hbm.at[0], cols_hbm.at[0], codes_hbm),
        (
            degree_ref,
            features_ref,
            lists_ref.at[0:1, 0:slots],
            lists_ref.at[1:2, 0:slots],
            codes_ref,
        ),
        sems,
    )
    first.wait()
    inv_row = lax.rsqrt(degree_ref[...].astype(jnp.float32))
    second.wait()
    out_ref[...] = (inv_row * features_ref[...].astype(jnp.float32).T).astype(jnp.bfloat16)
    for copy in others:
        copy.wait()


def scale_rows(degree, features, tile_rows, tile_cols, codes):
    pieces, feat = features.shape
    return pl.pallas_call(
        scale_kernel,
        out_shape=[
            pltpu.VMEM((feat, pieces), jnp.bfloat16),
            pltpu.VMEM((8, codes.shape[0]), jnp.int32),
            pltpu.VMEM(codes.shape, codes.dtype),
        ],
        in_specs=[pl.BlockSpec(memory_space=pl.ANY)] * 5,
        out_specs=[pl.BlockSpec(memory_space=pltpu.VMEM)] * 3,
        scratch_shapes=[
            pltpu.VMEM((1, pieces), jnp.int32),
            pltpu.VMEM((pieces, feat), jnp.bfloat16),
            pltpu.SemaphoreType.DMA((5,)),
        ],
        compiler_params=pltpu.CompilerParams(vmem_limit_bytes=60 * 2**20),
        name="scale_rows",
    )(degree.reshape(1, pieces), features, tile_rows, tile_cols, codes)


def terms_kernel(skip, *refs):
    *parts, out_ref = refs
    total = parts[0][skip:, :].astype(jnp.float32)
    for part in parts[1:]:
        total += part[skip:, :].astype(jnp.float32)
    out_ref[...] = total.astype(jnp.bfloat16)


def terms_sum(parts, skip, name):
    rows, width = parts[0].shape
    vmem = pl.BlockSpec(memory_space=pltpu.VMEM)
    return pl.pallas_call(
        functools.partial(terms_kernel, skip),
        out_shape=jax.ShapeDtypeStruct((rows - skip, width), jnp.bfloat16),
        in_specs=[vmem] * len(parts),
        out_specs=vmem,
        compiler_params=pltpu.CompilerParams(vmem_limit_bytes=LIMIT),
        name=name,
    )(*parts)


def dense_local(
    features, degree, weight, bias, cotangent, tile_rows, tile_cols, tile_count, tile_codes
):
    pieces, feat = features.shape
    n_row = lax.axis_size("row")
    n_col = lax.axis_size("col")
    grad_scale = 1.0 / math.sqrt(pieces * n_row * n_col)
    scaled, lists, codes = scale_rows(
        degree, features, tile_rows, tile_cols, tile_codes[0, 0]
    )
    chips = [6, 4, 2]
    lines = list(range(n_col - 1, 0, -1))
    landed = [swap(scaled, "row", m) for m in chips]
    sibling = swap(scaled, "row", 1)
    slots = codes.shape[0]
    middle = slots * 7 // 8 // GROUP * GROUP
    size = (pieces * n_col, pieces * n_row)
    block = build_block(lists, tile_count, codes, *size, 0, middle)
    block, landed = lax.optimization_barrier((block, landed))
    parts = [scaled, sibling, *landed, swap(stack(landed), "row", 1)]
    bits = [0, 1, *chips, *(m + 1 for m in chips)]
    block = build_block(lists, tile_count, codes, *size, middle, slots, block)
    half = max(1, n_col // 2)
    far = forward_parts(block, parts, bits, lines[:half], "forward_far")
    near = forward_parts(block, parts, bits, lines[half:] + [0], "forward_near")
    parts = dict(zip(lines + [0], [*far, *near]))
    *dense, parts[0] = lax.optimization_barrier((weight, bias, cotangent, degree, parts[0]))
    *dense, root = turn(*dense)
    landed = [parts[0]] + [swap(parts[k], "col", k) for k in lines]
    grad_own, both, aggregate = gradient_step(degree, weight, dense, landed)
    grads = [grad_own, swap(both, "col", 1)] + [swap(grad_own, "col", k) for k in range(2, n_col)]
    grads[1], aggregate = lax.optimization_barrier((grads[1], aggregate))
    hidden = hidden_step(dense[0], dense[1], aggregate)
    terms = [terms_sum([both, grads[1]], pieces, "terms_col")]
    terms += [swap(terms[0], "col", k) for k in range(2, n_col, 2)]
    begun = backward_parts(block, grads, [0, 1], range(n_row), None, [], "backward_near")
    grads[2:], begun, terms = lax.optimization_barrier((grads[2:], begun, terms))
    far = range(2, n_col)
    sent = backward_parts(block, grads, far, [7, 5], begun, terms, "backward_other")
    got = swap(sent, "row", 1)
    rest = swap(backward_parts(block, grads, far, [3, 1], begun, [], "backward_rest"), "row", 1)
    mine = backward_parts(block, grads, far, [6, 4], begun, [], "backward_own")
    chunks = pair_sum(0, mine, got, sent, got)
    landed = [swap(chunk, "row", m) for chunk, m in zip(chunks, chips)]
    mine = backward_parts(block, grads, far, [2, 0], begun, [], "backward_last")
    chunks = pair_sum(0, mine, rest, sent, got)
    landed = [chunks[1], *landed, swap(chunks[0], "row", chips[2])]
    grad_features, grad_weight, grad_bias = finish(root, landed, grad_scale)
    return (hidden, grad_features, grad_weight, grad_bias)


def solution(mesh):
    placed = (
        P(("row", "col"), None),
        P(("row", "col")),
        P(),
        P(),
        P(("row", "col"), None),
        P("row", "col", None),
        P("row", "col", None),
        P("row", "col", None),
        P("row", "col", None, None),
    )
    n_row, n_col = mesh.shape["row"], mesh.shape["col"]

    def local(features, *rest):
        block_bytes = 2 * features.shape[0] ** 2 * n_row * n_col
        paired = n_row == 8 and n_col == 4
        if paired and block_bytes <= DENSE_BYTES:
            return dense_local(features, *rest)
        return sparse_local(features, *rest)

    return jax.shard_map(
        local,
        mesh=mesh,
        in_specs=placed,
        out_specs=(P(("row", "col"), None), P(("row", "col"), None), P(), P()),
        check_vma=False,
    )
```
